32 devices in a mesh: seq: 8 (over z, y), mat: 4 (over x, core).
Axes of the slice: x: 2, y: 2, z: 4, core: 2. Of those that a mesh axis runs over, the one named last changes fastest.
Arguments:
- token_ids: int32 [2, 4, 1024], P(None, 'mat'), may hold values from 0 to 50256
- expert_route: int32 [2, 4, 1024, 1], P(None, 'mat', 'seq'), may hold values from 0 to 7; in each aligned block of 128 rows (0 to 127, 128 to 255, ..., all dimensions but the last counted through in order) at most 32 rows name the same one
- doc_lengths: int32 [2, 4, 3], P(None, 'mat'), may hold values from 1 to 960, 1024 in all within a row
- loss_slots: int32 [2, 4, 256], P(None, 'mat', 'seq'), may hold values from 0 to 1023, as said below
- loss_weight: int32 [2, 4, 256], P(None, 'mat'), may hold values from 0 to 1
- target_ids: int32 [2, 4, 256], P(None, 'mat'), may hold values from 0 to 50256
- embedding: float32 [50304, 768], P('seq', 'mat')
- embedding_mom: float32 [50304, 768], P('seq', 'mat'), may hold values from -2.9802322e-07 to 2.9802322e-07
- embedding_sq: float32 [50304, 768], P('seq', 'mat'), may hold values from 5.1895214e-15 to 4.1915364e-14
- in_project: float32 [768, 3072], P(None, 'mat'), may hold values from -0.21875 to 0.21875
- in_project_mom: float32 [768, 3072], P(None, 'mat'), may hold values from -2.861023e-06 to 2.861023e-06
- out_project: float32 [1536, 768], P('mat'), may hold values from -0.15625 to 0.15625
- out_project_mom: float32 [1536, 768], P('mat'), may hold values from -2.861023e-06 to 2.861023e-06
- expert_up: float32 [8, 768, 3072], P('seq', None, 'mat'), may hold values from -0.21875 to 0.21875
- expert_up_mom: float32 [8, 768, 3072], P('seq', None, 'mat'), may hold values from -2.861023e-06 to 2.861023e-06
- expert_down: float32 [8, 3072, 768], P('seq', 'mat'), may hold values from -0.109375 to 0.109375
- expert_down_mom: float32 [8, 3072, 768], P('seq', 'mat'), may hold values from -2.861023e-06 to 2.861023e-06
- x_project: float32 [1536, 80], P('mat'), may hold values from -0.15625 to 0.15625
- x_project_mom: float32 [1536, 80], P('mat'), may hold values from -2.9802322e-07 to 2.9802322e-07
- x_project_sq: float32 [1536, 80], P('mat'), may hold values from 5.1895214e-15 to 4.1915364e-14
- step_project: float32 [48, 1536], P(None, 'mat'), may hold values from -0.875 to 0.875
- step_project_mom: float32 [48, 1536], P(None, 'mat'), may hold values from -2.9802322e-07 to 2.9802322e-07
- step_project_sq: float32 [48, 1536], P(None, 'mat'), may hold values from 5.1895214e-15 to 4.1915364e-14
- router_weight: float32 [768, 8], P('mat'), may hold values from -0.15625 to 0.15625
- router_mom: float32 [768, 8], P('mat'), may hold values from -2.9802322e-07 to 2.9802322e-07
- router_sq: float32 [768, 8], P('mat'), may hold values from 5.1895214e-15 to 4.1915364e-14
- channel_param: float32 [23, 1536], P(None, 'mat')
- channel_mom: float32 [23, 1536], P(None, 'mat'), may hold values from -1.1920929e-06 to 1.1920929e-06
- channel_sq: float32 [23, 1536], P(None, 'mat'), may hold values from 7.983879e-14 to 6.7862973e-13
- norm_gains: float32 [3, 768], P(None, 'mat')
- gains_mom: float32 [3, 768], P(None, 'mat'), may hold values from -1.1920929e-06 to 1.1920929e-06
- gains_sq: float32 [3, 768], P(None, 'mat'), may hold values from 7.983879e-14 to 6.7862973e-13
Outputs:
- loss_total: float32 [], replicated
- loss_count: float32 [], replicated
- grad_norm: float32 [], replicated
- row_loss: float32 [2, 4, 256], P(None, 'mat', 'seq')
- new_embedding: float32 [50304, 768], P('seq', 'mat')
- new_embedding_mom: float32 [50304, 768], P('seq', 'mat')
- new_embedding_sq: float32 [50304, 768], P('seq', 'mat')
- new_in_project: float32 [768, 3072], P(None, 'mat')
- new_in_project_mom: float32 [768, 3072], P(None, 'mat')
- new_out_project: float32 [1536, 768], P('mat')
- new_out_project_mom: float32 [1536, 768], P('mat')
- new_expert_up: float32 [8, 768, 3072], P('seq', None, 'mat')
- new_expert_up_mom: float32 [8, 768, 3072], P('seq', None, 'mat')
- new_expert_down: float32 [8, 3072, 768], P('seq', 'mat')
- new_expert_down_mom: float32 [8, 3072, 768], P('seq', 'mat')
- new_x_project: float32 [1536, 80], P('mat')
- new_x_project_mom: float32 [1536, 80], P('mat')
- new_x_project_sq: float32 [1536, 80], P('mat')
- new_step_project: float32 [48, 1536], P(None, 'mat')
- new_step_project_mom: float32 [48, 1536], P(None, 'mat')
- new_step_project_sq: float32 [48, 1536], P(None, 'mat')
- new_router: float32 [768, 8], P('mat')
- new_router_mom: float32 [768, 8], P('mat')
- new_router_sq: float32 [768, 8], P('mat')
- new_channel: float32 [23, 1536], P(None, 'mat')
- new_channel_mom: float32 [23, 1536], P(None, 'mat')
- new_channel_sq: float32 [23, 1536], P(None, 'mat')
- new_gains: float32 [3, 768], P(None, 'mat')
- new_gains_mom: float32 [3, 768], P(None, 'mat')
- new_gains_sq: float32 [3, 768], P(None, 'mat')
The draws below stay inside these ranges and needn't reach their ends.
Inputs may be any that keep to these rules, and one draw needn't show every extreme that they name: `loss_slots`: each aligned block of 32 slots names different positions inside the matching block of 128 positions. `expert_route`: in each aligned block of 128 positions of a row (the positions of one device) no expert is named more than 32 times. `doc_lengths`: each row's lengths sum to 1024.
All inputs are finite; a program needn't handle non-finite values.
Results may differ from the reference program's by a relative error of at most 0.025.
The reference program's roundings to bfloat16 on the way count: a program that leaves them out, or rounds other values in their place, can miss the bound.
Values may be sent and summed in bfloat16 or wider, within the bound.
A program may use at most 512 MiB of HBM per device.

```python
import math
import jax
import jax.numpy as jnp
import numpy as np
from jax import lax

D = 768
DI = 1536
NST = 16
RANK = 48
FF = 3072
VOCAB = 50304
VOCAB_REAL = 50257
CONV = 4
TOK_DEV = 128
MICRO = 2
DOCS = 3
ORTHO_STEPS = 5
STEP_COUNT = 10
EXPERTS = 8
SEQLEN = 1024
BATCH = 4
LOSS_DEV = 32
SLOTS = 256
CAP = 32
XW = 80
CHAN = 23
LOSS_ALL = 2048
PARAMS = 80161536
N_SEQ = 8
N_MAT = 4


def draw_loss_slots(key, part):
    key = jax.random.fold_in(key, 11)
    groups = SLOTS // LOSS_DEV
    blocks = MICRO * BATCH * groups
    keys = jax.random.split(key, blocks)

    def single(block_key):
        middle = jax.random.permutation(block_key, TOK_DEV - 2).astype(jnp.int32) + 1
        chosen = jnp.concatenate([jnp.array([0, TOK_DEV - 1], jnp.int32), middle[:LOSS_DEV - 2]])
        return jax.random.permutation(jax.random.fold_in(block_key, 1), chosen)
    offsets = jax.vmap(single)(keys).reshape(MICRO, BATCH, groups, LOSS_DEV)
    starts = (jnp.arange(groups, dtype=jnp.int32) * TOK_DEV)[None, None, :, None]
    return (offsets + starts).reshape(MICRO, BATCH, SLOTS)


def draw_loss_weight(key, part):
    key = jax.random.fold_in(key, 12)
    position = jnp.arange(SLOTS, dtype=jnp.int32)
    limit = 250 + 500 * position // SLOTS
    tickets = jax.random.randint(key, (MICRO, BATCH, SLOTS), 0, 1000)
    return (tickets < limit[None, None, :]).astype(jnp.int32)


def draw_embedding(key, part):
    key = jax.random.fold_in(key, 13)
    height = jnp.arange(VOCAB, dtype=jnp.float32)[:, None] / VOCAB
    values = jax.random.normal(key, (VOCAB, D), jnp.float32)
    rising = 1.0 + 2.0 * height
    return values * rising / math.sqrt(D)


def draw_channel_param(key, part):
    key = jax.random.fold_in(key, 14)
    pieces = jax.random.split(key, 5)
    taps = 0.5 * jax.random.normal(pieces[0], (CONV, DI), jnp.float32)
    conv_bias = 0.3 * jax.random.normal(pieces[1], (1, DI), jnp.float32)
    step_value = jnp.exp(jax.random.uniform(pieces[2], (1, DI), jnp.float32, math.log(0.001), math.log(0.1)))
    step_bias = jnp.log(jnp.expm1(step_value))
    skipping = 1.0 + 0.3 * jax.random.normal(pieces[3], (1, DI), jnp.float32)
    log_rates = jax.random.uniform(pieces[4], (NST, DI), jnp.float32, math.log(0.01), math.log(16.0))
    return jnp.concatenate([taps, conv_bias, step_bias, skipping, log_rates], axis=0)


def draw_norm_gains(key, part):
    key = jax.random.fold_in(key, 15)
    column = jnp.arange(D, dtype=jnp.float32)[None, :] / D
    noise = 1.0 + 0.1 * jax.random.normal(key, (3, D), jnp.float32)
    return (0.5 + column) * noise


def set_ends(values, own_key, smallest, high):
    dims = values.shape
    place = [jax.random.randint(jax.random.fold_in(own_key, axis), (), 0, dims[axis]) for axis in range(len(dims))]
    values = values.at[tuple(place)].set(smallest)
    longest = dims.index(max(dims))
    place[longest] = (place[longest] + 1) % dims[longest]
    return values.at[tuple(place)].set(high)


def block_scale(own_key, shape, cuts, smallest, top_value):
    factor_of, own = 1.0, jax.random.fold_in(own_key, 6)
    for dim, blocks in cuts:
        steps = jnp.exp(jax.random.uniform(jax.random.fold_in(own, dim), (blocks,), jnp.float32, smallest / len(cuts), top_value / len(cuts)))
        factor_of = factor_of * jnp.repeat(steps, shape[dim] // blocks).reshape([-1 if axis == dim else 1 for axis in range(len(shape))])
    return factor_of


def rank_bounds(number_of, slope):
    portions = [(1 << 20) // math.isqrt(rank ** slope) + 1 for rank in range(1, number_of + 1)]
    width = 1 + sum(portions) // (1 << 30)
    return np.cumsum(np.array([max(1, weight // width) for weight in portions]))


def ranked_ids(rng, dims, amount, skew):
    table = rank_bounds(amount, skew)
    ticket = jax.random.randint(jax.random.fold_in(rng, 1), dims, 0, int(table[amount - 1]))
    standing = jnp.searchsorted(jnp.asarray(table, jnp.int32), ticket, side="right")
    return jax.random.permutation(jax.random.fold_in(rng, 2), amount)[standing].astype(jnp.int32)


def profile(amount, total, reach, skew):
    portions = [(1 << 20) // math.isqrt(grade ** skew) + 1 for grade in range(2, amount + 1)]
    spare, holding = total - reach - (amount - 1), [1] * (amount - 1)
    while spare > 0:
        free = [i for i in range(amount - 1) if holding[i] < reach]
        mass, left = sum([portions[i] for i in free]), spare
        for i in free:
            addition = min(reach - holding[i], max(1, left * portions[i] // mass), spare)
            holding[i] = holding[i] + addition
            spare = spare - addition
    return np.array([reach] + holding)


def ragged(key, count, total, most, lean):
    if count == 2:
        one = jax.random.randint(key, (), max(1, total - most), min(most, total - 1) + 1)
        return jnp.stack([one, total - one])
    tallies = jnp.asarray(profile(count, total, most, lean), jnp.int32)
    couples = (count - 1) // 2
    donor, taker = tallies[1:1 + 2 * couples:2], tallies[2:2 + 2 * couples:2]
    slack = jnp.minimum(donor - 1, most - taker)
    moved = jax.random.randint(jax.random.fold_in(key, 1), (couples,), 0, 1 << 20) % (slack + 1)
    tallies = tallies.at[1:1 + 2 * couples:2].set(donor - moved).at[2:2 + 2 * couples:2].set(taker + moved)
    return tallies[jax.random.permutation(jax.random.fold_in(key, 2), count)]


def assign_block(key, own, number, rows, number_of, top, most, slope):
    order = jax.random.permutation(key, number_of)
    heavy_load, ordinary = shares(number_of, rows * top, most, slope, True), shares(number_of, rows * top, most, slope, False)
    places = jnp.arange(number_of)

    def named(sizes, offset_by):
        used = int((sizes > 0).sum())
        fixed = max(1, used // 4)
        shifted = fixed + (places - fixed + offset_by * (used - fixed)) % max(1, number_of - fixed)
        return jnp.zeros((number_of,), jnp.int32).at[order[jnp.where(places < fixed, places, shifted)]].set(jnp.asarray(sizes, jnp.int32))

    sizes = jnp.where(number % 4 == 0, named(heavy_load, number // 4), named(ordinary, number - number // 4 - 1))
    mixed = jax.random.permutation(jax.random.fold_in(own, 3), number_of)
    source_of, sink = mixed[0:number_of // 2 * 2:2], mixed[1:number_of // 2 * 2:2]
    margin = jnp.minimum(sizes[source_of] - 1, most - sizes[sink]) // 2
    margin = jnp.where((source_of == order[0]) | (sink == order[0]) | (sizes[sink] == 0), 0, jnp.maximum(margin, 0))
    shifted = jax.random.randint(jax.random.fold_in(own, 4), (number_of // 2,), 0, 1 << 20) % (margin + 1)
    sizes = sizes.at[source_of].add(-shifted).at[sink].add(shifted)
    items = jnp.searchsorted(jnp.cumsum(sizes), jnp.arange(rows * top), side="right").astype(jnp.int32)
    table = items.reshape(top, rows).T
    table = table[jax.random.permutation(jax.random.fold_in(own, 1), rows)]
    offset_by = jax.random.randint(jax.random.fold_in(own, 2), (rows, 1), 0, top)
    return jnp.take_along_axis(table, (jnp.arange(top)[None, :] + offset_by) % top, axis=1)


def shares(count, total, reach, slope, full):
    loads = [(1 << 20) // math.isqrt(grade ** slope) + 1 for grade in range(1, count + 1)]
    largest = reach if full else min(reach, max(-(-total // count), total * loads[0] // sum(loads)))
    least = 1 if total - largest >= count - 1 else 0
    holding, surplus = [largest] + [least] * (count - 1), total - largest - least * (count - 1)
    while surplus > 0:
        free = [i for i in range(1, count) if holding[i] < largest] or [i for i in range(1, count) if holding[i] < reach]
        mass, budget = sum([loads[i] for i in free]), surplus
        for i in free:
            addition = min(reach - holding[i], max(1, budget * loads[i] // mass), surplus)
            holding[i] = holding[i] + addition
            surplus = surplus - addition
    return np.array(holding)


def gaussian(rng, extent, deviation, most, shards=(), kind=jnp.bfloat16):
    values = deviation * jax.random.normal(rng, extent, jnp.float32)
    if shards:
        values = values * block_scale(rng, extent, shards, -0.22, 0.18)
    return jnp.clip(values, -most, most).astype(kind)


def setup_inputs(seed: int = 0) -> dict:
    arg_keys = jax.random.split(jax.random.key(seed), 33)
    token_ids = set_ends(ranked_ids(arg_keys[0], (MICRO, BATCH, SEQLEN), VOCAB_REAL, 2), jax.random.fold_in(arg_keys[0], 3), 0, VOCAB_REAL - 1).astype(jnp.int32)
    expert_route_keys = jax.random.split(jax.random.fold_in(arg_keys[1], 1), MICRO * BATCH * SEQLEN // TOK_DEV)
    expert_route_turns = jax.random.permutation(jax.random.fold_in(arg_keys[1], 3), MICRO * BATCH * SEQLEN // TOK_DEV)
    expert_route = jax.vmap(lambda own, number: assign_block(jax.random.fold_in(arg_keys[1], 2), own, number, TOK_DEV, EXPERTS, 1, CAP, 2))(expert_route_keys, expert_route_turns).reshape((MICRO, BATCH, SEQLEN, 1))
    doc_lengths = jax.vmap(lambda own: ragged(own, DOCS, SEQLEN, SEQLEN - TOK_DEV // 2, 0))(jax.random.split(arg_keys[2], MICRO * BATCH)).reshape((MICRO, BATCH, DOCS)).astype(jnp.int32)
    loss_slots = draw_loss_slots(jax.random.fold_in(arg_keys[32], 71), 0)
    loss_weight = draw_loss_weight(jax.random.fold_in(arg_keys[32], 71), 0)
    target_ids = set_ends(jax.random.randint(arg_keys[5], (MICRO, BATCH, SLOTS), 0, VOCAB_REAL), jax.random.fold_in(arg_keys[5], 1), 0, VOCAB_REAL - 1).astype(jnp.int32)
    embedding = draw_embedding(jax.random.fold_in(arg_keys[32], 71), 0)
    embedding_mom = gaussian(arg_keys[7], (VOCAB, D), (0.11 * 0.004 / PARAMS ** 0.5), 2.980232238769531e-07, ((0, 8), (1, 4)), jnp.float32)
    embedding_sq = jnp.clip(jnp.exp(math.log(4.191536440850685e-14) - 2.089011 * jax.random.uniform(arg_keys[8], (VOCAB, D), jnp.float32) ** block_scale(arg_keys[8], (VOCAB, D), ((0, 8), (1, 4)), -0.2, 0.2)), 5.189521416624132e-15, 4.191536440850685e-14)
    in_project = gaussian(arg_keys[9], (D, 2 * DI), D ** -0.5, 0.21875, ((1, 4),), jnp.float32)
    in_project_mom = gaussian(arg_keys[10], (D, 2 * DI), (0.004 / PARAMS ** 0.5), 2.86102294921875e-06, ((1, 4),), jnp.float32)
    out_project = gaussian(arg_keys[11], (DI, D), DI ** -0.5, 0.15625, ((0, 4),), jnp.float32)
    out_project_mom = gaussian(arg_keys[12], (DI, D), (0.004 / PARAMS ** 0.5), 2.86102294921875e-06, ((0, 4),), jnp.float32)
    expert_up = gaussian(arg_keys[13], (EXPERTS, D, FF), D ** -0.5, 0.21875, ((0, 8), (2, 4)), jnp.float32)
    expert_up_mom = gaussian(arg_keys[14], (EXPERTS, D, FF), (0.004 / PARAMS ** 0.5), 2.86102294921875e-06, ((0, 8), (2, 4)), jnp.float32)
    expert_down = gaussian(arg_keys[15], (EXPERTS, FF, D), FF ** -0.5, 0.109375, ((0, 8), (1, 4)), jnp.float32)
    expert_down_mom = gaussian(arg_keys[16], (EXPERTS, FF, D), (0.004 / PARAMS ** 0.5), 2.86102294921875e-06, ((0, 8), (1, 4)), jnp.float32)
    x_project = gaussian(arg_keys[17], (DI, XW), DI ** -0.5, 0.15625, ((0, 4),), jnp.float32)
    x_project_mom = gaussian(arg_keys[18], (DI, XW), (0.11 * 0.004 / PARAMS ** 0.5), 2.980232238769531e-07, ((0, 4),), jnp.float32)
    x_project_sq = jnp.clip(jnp.exp(math.log(4.191536440850685e-14) - 2.089011 * jax.random.uniform(arg_keys[19], (DI, XW), jnp.float32) ** block_scale(arg_keys[19], (DI, XW), ((0, 4),), -0.2, 0.2)), 5.189521416624132e-15, 4.191536440850685e-14)
    step_project = gaussian(arg_keys[20], (RANK, DI), RANK ** -0.5, 0.875, ((1, 4),), jnp.float32)
    step_project_mom = gaussian(arg_keys[21], (RANK, DI), (0.11 * 0.004 / PARAMS ** 0.5), 2.980232238769531e-07, ((1, 4),), jnp.float32)
    step_project_sq = jnp.clip(jnp.exp(math.log(4.191536440850685e-14) - 2.089011 * jax.random.uniform(arg_keys[22], (RANK, DI), jnp.float32) ** block_scale(arg_keys[22], (RANK, DI), ((1, 4),), -0.2, 0.2)), 5.189521416624132e-15, 4.191536440850685e-14)
    router_weight = gaussian(arg_keys[23], (D, EXPERTS), (2 * D) ** -0.5, 0.15625, ((0, 4),), jnp.float32)
    router_mom = gaussian(arg_keys[24], (D, EXPERTS), (0.11 * 0.004 / PARAMS ** 0.5), 2.980232238769531e-07, ((0, 4),), jnp.float32)
    router_sq = jnp.clip(jnp.exp(math.log(4.191536440850685e-14) - 2.089011 * jax.random.uniform(arg_keys[25], (D, EXPERTS), jnp.float32) ** block_scale(arg_keys[25], (D, EXPERTS), ((0, 4),), -0.2, 0.2)), 5.189521416624132e-15, 4.191536440850685e-14)
    channel_param = draw_channel_param(jax.random.fold_in(arg_keys[32], 71), 0)
    channel_mom = gaussian(arg_keys[27], (CHAN, DI), (0.44 * 0.004 / PARAMS ** 0.5), 1.1920928955078125e-06, ((1, 4),), jnp.float32)
    channel_sq = jnp.clip(jnp.exp(math.log(6.78629732703967e-13) - 2.1400662 * jax.random.uniform(arg_keys[28], (CHAN, DI), jnp.float32) ** block_scale(arg_keys[28], (CHAN, DI), ((1, 4),), -0.2, 0.2)), 7.983879128561217e-14, 6.78629732703967e-13)
    norm_gains = draw_norm_gains(jax.random.fold_in(arg_keys[32], 71), 0)
    gains_mom = gaussian(arg_keys[30], (3, D), (0.44 * 0.004 / PARAMS ** 0.5), 1.1920928955078125e-06, ((1, 4),), jnp.float32)
    gains_sq = jnp.clip(jnp.exp(math.log(6.78629732703967e-13) - 2.1400662 * jax.random.uniform(arg_keys[31], (3, D), jnp.float32) ** block_scale(arg_keys[31], (3, D), ((1, 4),), -0.2, 0.2)), 7.983879128561217e-14, 6.78629732703967e-13)
    return dict(token_ids=token_ids, expert_route=expert_route, doc_lengths=doc_lengths, loss_slots=loss_slots, loss_weight=loss_weight, target_ids=target_ids, embedding=embedding, embedding_mom=embedding_mom, embedding_sq=embedding_sq, in_project=in_project, in_project_mom=in_project_mom, out_project=out_project, out_project_mom=out_project_mom, expert_up=expert_up, expert_up_mom=expert_up_mom, expert_down=expert_down, expert_down_mom=expert_down_mom, x_project=x_project, x_project_mom=x_project_mom, x_project_sq=x_project_sq, step_project=step_project, step_project_mom=step_project_mom, step_project_sq=step_project_sq, router_weight=router_weight, router_mom=router_mom, router_sq=router_sq, channel_param=channel_param, channel_mom=channel_mom, channel_sq=channel_sq, norm_gains=norm_gains, gains_mom=gains_mom, gains_sq=gains_sq)


HIGH = lax.Precision.HIGHEST
CLIP_NORM = 0.004
COEF_A = 3.4445
COEF_B = -4.775
COEF_C = 2.0315
MOMENTUM = 0.95
LR_MUON = 0.2
DECAY_MUON = 0.01
BETA_ONE = 0.9
BETA_TWO = 0.95
ADAM_EPS = 1e-08

@jax.custom_vjp
def low(v):
    return lax.optimization_barrier(v.astype(jnp.bfloat16)).astype(jnp.float32)

@jax.custom_vjp
def low_back(v):
    return v

def low_keep(v):
    return (low(v), None)

def low_pass(kept, grad):
    return (grad,)

def back_keep(v):
    return (v, None)

def back_low(kept, grad):
    return (low(grad),)
low.defvjp(low_keep, low_pass)
low_back.defvjp(back_keep, back_low)

def normalize(values, gain):
    return values * lax.rsqrt(lax.optimization_barrier(jnp.mean(values * values, axis=-1, keepdims=True)) + 1e-05) * gain

def matmul(left, weight):
    return low_back(jnp.dot(low(left), weight, precision=HIGH))

def expert_matmul(left, weight):
    return low_back(jnp.einsum('erk,ekn->ern', low(left), weight, precision=HIGH))

def doc_layout(lengths):
    bounds = jnp.cumsum(lengths).astype(jnp.int32)
    position = jnp.arange(SEQLEN, dtype=jnp.int32)
    document = lax.optimization_barrier(jnp.sum((position[:, None] >= bounds[None, :-1]).astype(jnp.int32), axis=1))
    starts = jnp.concatenate([jnp.zeros((1,), jnp.int32), bounds[:-1]])
    opening = jnp.any(position[:, None] == starts[None, :], axis=1)
    return (document, opening)

def mixer(resid, gain, channel, w_in, w_x, w_step, w_out, document, opening):
    halves = matmul(normalize(resid, gain), w_in)
    raw_half, gate_half = (halves[:, :DI], halves[:, DI:])
    padded = jnp.concatenate([jnp.zeros((CONV - 1, DI), jnp.float32), raw_half])
    doc_padded = jnp.concatenate([jnp.full((CONV - 1,), -1, jnp.int32), document])
    convolved = channel[CONV] + jnp.zeros_like(raw_half)
    for tap_index in range(CONV):
        sameness = (doc_padded[tap_index:tap_index + SEQLEN] == document).astype(jnp.float32)
        convolved = convolved + channel[tap_index] * padded[tap_index:tap_index + SEQLEN] * sameness[:, None]
    activated = jax.nn.silu(convolved)
    projected = matmul(activated, w_x)
    step_low = projected[:, :RANK]
    inject = projected[:, RANK:RANK + NST]
    readout = projected[:, RANK + NST:]
    step_size = jax.nn.softplus(matmul(step_low, w_step) + channel[CONV + 1])
    rate = -jnp.exp(channel[CONV + 3:])
    keeping = 1.0 - opening.astype(jnp.float32)

    def advance(state, item):
        x_item, step_item, inject_item, read_item, keep_item = item
        state = jnp.exp(rate * step_item[None, :]) * keep_item * state + inject_item[:, None] * (step_item * x_item)[None, :]
        return (state, jnp.dot(read_item, state, precision=HIGH))
    _, scanned = lax.scan(advance, jnp.zeros((NST, DI), jnp.float32), (activated, step_size, inject, readout, keeping))
    mixed = (scanned + channel[CONV + 2] * activated) * jax.nn.silu(gate_half)
    return resid + matmul(mixed, w_out)

def experts(resid, gain, route, w_route, w_up, w_down):
    sent = low(normalize(resid, gain))
    scores = matmul(sent, w_route)
    chosen = route[:, None] == jnp.arange(EXPERTS, dtype=jnp.int32)[None, :]
    gate = jax.nn.sigmoid(lax.optimization_barrier(jnp.sum(jnp.where(chosen, scores, 0.0), axis=1)))
    blocks = route.reshape(N_SEQ, TOK_DEV)
    onehot = (blocks[..., None] == jnp.arange(EXPERTS, dtype=jnp.int32)).astype(jnp.int32)
    ranking = lax.optimization_barrier(jnp.sum(jnp.cumsum(onehot, axis=1) * onehot, axis=2)) - 1
    placed = blocks * CAP + ranking
    sender = (placed[:, None, :] == jnp.arange(EXPERTS * CAP, dtype=jnp.int32)[None, :, None]).astype(jnp.float32)
    tokens = low_back(sent).reshape(N_SEQ, TOK_DEV, D)
    outgoing = jnp.einsum('bst,btd->bsd', sender, tokens, precision=HIGH)
    arrived = outgoing.reshape(N_SEQ, EXPERTS, CAP, D).transpose(1, 0, 2, 3).reshape(EXPERTS, N_SEQ * CAP, D)
    hidden = jax.nn.gelu(expert_matmul(arrived, w_up), approximate=False)
    result = low(expert_matmul(hidden, w_down))
    returned = result.reshape(EXPERTS, N_SEQ, CAP, D).transpose(1, 0, 2, 3).reshape(N_SEQ, EXPERTS * CAP, D)
    combined = jnp.einsum('bst,bsd->btd', sender, returned, precision=HIGH).reshape(SEQLEN, D)
    return resid + gate[:, None] * combined

def head(resid, gain, table, slots, targets, weight_mask):
    final = normalize(resid, gain)
    rows = low(final[slots])
    logits = low_back(jnp.dot(rows, table.T, precision=HIGH))
    valid = jnp.arange(VOCAB) < VOCAB_REAL
    logits = jnp.where(valid[None, :], logits, -1e+30)
    lse = jax.nn.logsumexp(logits, axis=1)
    target = jnp.take_along_axis(logits, targets[:, None], axis=1)[:, 0]
    counted = weight_mask.astype(jnp.float32)
    terms = lse - target
    return (jnp.sum(terms * counted), jnp.sum(counted), terms)

def sequence(weights, item):
    table, w_in, w_out, w_up, w_down, w_x, w_step, w_route, channel, gains = weights
    ids, route, lengths, slots, weight_mask, targets = item
    document, opening = doc_layout(lengths)
    resid = low_back(table[ids])
    resid = mixer(resid, gains[0], channel, w_in, w_x, w_step, w_out, document, opening)
    resid = experts(resid, gains[1], route, w_route, w_up, w_down)
    return head(resid, gains[2], table, slots, targets, weight_mask)

def objective(params, data):
    weights = tuple((low(param) for param in params))
    checked = jax.checkpoint(sequence)

    def run(carry, item):
        loss_row, count_row, terms = checked(weights, item)
        return ((carry[0] + loss_row, carry[1] + count_row), terms)
    (loss_sum, count_sum), row_terms = lax.scan(run, (jnp.zeros((), jnp.float32), jnp.zeros((), jnp.float32)), data)
    return (loss_sum / LOSS_ALL, (loss_sum, count_sum, row_terms))

def orthogonalize(view):
    current = view
    for sweep in range(ORTHO_STEPS):
        rounded = low(current)
        blocks = rounded.reshape(rounded.shape[:-1] + (N_MAT, rounded.shape[-1] // N_MAT))
        partial_grams = low(jnp.einsum('...mbk,...jbk->...bmj', blocks, blocks, precision=HIGH))
        gram = lax.optimization_barrier(jnp.sum(partial_grams, axis=-3))
        if sweep == 0:
            factor = (1.0 / (jnp.sqrt(jnp.trace(gram, axis1=-2, axis2=-1)) + 1e-07))[..., None, None]
            current = rounded * factor
            gram = gram * factor * factor
        poly = COEF_B * gram + COEF_C * jnp.matmul(gram, gram, precision=HIGH)
        current = COEF_A * current + jnp.matmul(poly, current, precision=HIGH)
    return current

def muon_update(weight, momentum, grad, flipped, size_factor):
    momentum = MOMENTUM * momentum + grad
    view = jnp.swapaxes(momentum, -1, -2) if flipped else momentum
    ortho = orthogonalize(view)
    ortho = jnp.swapaxes(ortho, -1, -2) if flipped else ortho
    return (weight * (1.0 - LR_MUON * DECAY_MUON) - LR_MUON * 0.2 * size_factor * ortho, momentum)

def adamw_update(weight, mean, square, grad, rate, decay):
    mean = BETA_ONE * mean + (1.0 - BETA_ONE) * grad
    square = BETA_TWO * square + (1.0 - BETA_TWO) * grad * grad
    ratio = mean / (1.0 - BETA_ONE ** STEP_COUNT) / (jnp.sqrt(square / (1.0 - BETA_TWO ** STEP_COUNT)) + ADAM_EPS)
    return (weight * (1.0 - rate * decay) - rate * ratio, mean, square)

def reference(token_ids, expert_route, doc_lengths, loss_slots, loss_weight, target_ids, embedding, embedding_mom, embedding_sq, in_project, in_project_mom, out_project, out_project_mom, expert_up, expert_up_mom, expert_down, expert_down_mom, x_project, x_project_mom, x_project_sq, step_project, step_project_mom, step_project_sq, router_weight, router_mom, router_sq, channel_param, channel_mom, channel_sq, norm_gains, gains_mom, gains_sq):
    rows_all = MICRO * BATCH
    data = (token_ids.reshape(rows_all, SEQLEN), expert_route[..., 0].reshape(rows_all, SEQLEN), doc_lengths.reshape(rows_all, DOCS), loss_slots.reshape(rows_all, SLOTS), loss_weight.reshape(rows_all, SLOTS), target_ids.reshape(rows_all, SLOTS))
    params = (embedding, in_project, out_project, expert_up, expert_down, x_project, step_project, router_weight, channel_param, norm_gains)
    _, back_fn, (loss_total, loss_count, row_terms) = jax.vjp(lambda values: objective(values, data), params, has_aux=True)
    row_loss = row_terms.reshape(MICRO, BATCH, SLOTS)
    grads = back_fn(jnp.ones((), jnp.float32))[0]
    squares = jnp.zeros((), jnp.float32)
    for grad in grads:
        squares = squares + jnp.sum(grad * grad)
    grad_norm = jnp.sqrt(squares)
    scale = jnp.minimum(1.0, CLIP_NORM / (grad_norm + 1e-06))
    grads = tuple((grad * scale for grad in grads))
    table_new = adamw_update(embedding, embedding_mom, embedding_sq, grads[0], 0.05, 0.1)
    in_new = muon_update(in_project, in_project_mom, grads[1], False, math.sqrt(max(D, 2 * DI)))
    out_new = muon_update(out_project, out_project_mom, grads[2], True, math.sqrt(max(D, DI)))
    up_new = muon_update(expert_up, expert_up_mom, grads[3], False, math.sqrt(max(D, FF)))
    down_new = muon_update(expert_down, expert_down_mom, grads[4], True, math.sqrt(max(D, FF)))
    x_new = adamw_update(x_project, x_project_mom, x_project_sq, grads[5], 0.06, 0.1)
    step_new = adamw_update(step_project, step_project_mom, step_project_sq, grads[6], 0.06, 0.1)
    route_new = adamw_update(router_weight, router_mom, router_sq, grads[7], 0.06, 0.1)
    chan_new = adamw_update(channel_param, channel_mom, channel_sq, grads[8], 1.0, 0.0)
    gains_new = adamw_update(norm_gains, gains_mom, gains_sq, grads[9], 0.4, 0.0)
    return (loss_total, loss_count, grad_norm, row_loss, table_new[0], table_new[1], table_new[2], in_new[0], in_new[1], out_new[0], out_new[1], up_new[0], up_new[1], down_new[0], down_new[1], x_new[0], x_new[1], x_new[2], step_new[0], step_new[1], step_new[2], route_new[0], route_new[1], route_new[2], chan_new[0], chan_new[1], chan_new[2], gains_new[0], gains_new[1], gains_new[2])
```

```python
import functools
import math

import jax
import jax.numpy as jnp
from jax import lax
from jax.experimental import pallas as pl
from jax.experimental.pallas import tpu as pltpu
from jax.sharding import PartitionSpec as P

D = 768
DI = 1536
FF = 3072
VOCAB_REAL = 50257
CONV = 4
ORTHO_STEPS = 5
STEP_COUNT = 10
STATES = 16
RANK = 48

CLIP_NORM = 0.004
COEF_A = 3.4445
COEF_B = -4.775
COEF_C = 2.0315
MOMENTUM = 0.95
LR_MUON = 0.2
DECAY_MUON = 0.01
BETA_ONE = 0.9
BETA_TWO = 0.95
ADAM_EPS = 1e-08
F32 = jnp.float32
BF16 = jnp.bfloat16
LANES = 512
UNROLL = 8
TILE = 256
CUT = 256
VOCAB_TILE = 640
UP_PLACE, IN_PLACE, DOWN_PLACE, OUT_PLACE = 0, 1, 2, 3
TOTAL_ROWS = 8
MESH = pl.DeviceIdType.MESH


def dot(left, right, left_dim, right_dim, **kw):
    return lax.dot_general(
        left, right, (((left_dim,), (right_dim,)), ((), ())), preferred_element_type=F32, **kw
    )


def spread(values, width):
    return jnp.concatenate([values] * (width // 128), axis=1)


def end_kernel(keep, dt, act, inject, rate, out):
    micro = pl.program_id(0)
    tokens, width = dt.shape[1], dt.shape[2]
    rates = rate[...]

    def block(step, state):
        for inner in range(UNROLL):
            t = step * UNROLL + inner
            d = dt[0, pl.ds(t, 1), :]
            w = d * act[0, pl.ds(t, 1), :]
            state = jnp.exp(rates * d) * keep[micro, t] * state + spread(inject[0, t], width) * w
        return state

    state = lax.fori_loop(0, tokens // UNROLL, block, jnp.zeros((STATES, width), F32))
    out[...] = state.astype(BF16)


def forward_kernel(
    place, keep, dt, act, inject, readout, rate, ends, totals, y_out, h_out, start_out
):
    micro = pl.program_id(0)
    micros = pl.num_programs(0)
    tokens, width = dt.shape[1], dt.shape[2]
    rates = rate[...]
    me = place[0]

    def fold(source, state):
        total = totals[source, pl.ds(micro, 1), :]
        alive = totals[source, pl.ds(micros + micro, 1), :]
        return jnp.exp(rates * total) * alive * state + ends[source].astype(F32)

    state = lax.fori_loop(0, me, fold, jnp.zeros((STATES, width), F32))
    start_out[0] = state

    def block(step, state):
        for inner in range(UNROLL):
            t = step * UNROLL + inner
            d = dt[0, pl.ds(t, 1), :]
            w = d * act[0, pl.ds(t, 1), :]
            state = jnp.exp(rates * d) * keep[micro, t] * state + spread(inject[0, t], width) * w
            h_out[0, t] = state
            y_out[0, pl.ds(t, 1), :] = jnp.sum(
                spread(readout[0, t], width) * state, axis=0, keepdims=True
            )
        return state

    lax.fori_loop(0, tokens // UNROLL, block, state)


def start_kernel(keep, dt, dy, readout, rate, out):
    micro = pl.program_id(0)
    tokens, width = dt.shape[1], dt.shape[2]
    rates = rate[...]

    def block(step, state):
        for inner in range(UNROLL):
            t = tokens - 1 - (step * UNROLL + inner)
            d = dt[0, pl.ds(t, 1), :]
            state = state + spread(readout[0, t], width) * dy[0, pl.ds(t, 1), :]
            state = jnp.exp(rates * d) * keep[micro, t] * state
        return state

    state = lax.fori_loop(0, tokens // UNROLL, block, jnp.zeros((STATES, width), F32))
    out[...] = state.astype(BF16)


def backward_kernel(
    place,
    keep,
    dt,
    act,
    dy,
    inject,
    readout,
    rate,
    totals,
    starts,
    start,
    hs,
    ddt_out,
    da_out,
    db_out,
    dc_out,
    drate_out,
):
    micro = pl.program_id(0)
    micros = pl.num_programs(0)
    group = pl.program_id(1)
    tokens, width = dt.shape[1], dt.shape[2]
    rates = rate[...]
    me = place[0]
    count = totals.shape[0]

    def fold(lap, state):
        source = count - 1 - lap
        total = totals[source, pl.ds(micro, 1), :]
        alive = totals[source, pl.ds(micros + micro, 1), :]
        return jnp.exp(rates * total) * alive * state + starts[source].astype(F32)

    grad = lax.fori_loop(0, count - 1 - me, fold, jnp.zeros((STATES, width), F32))

    @pl.when(group == 0)
    def _():
        db_out[...] = jnp.zeros_like(db_out)
        dc_out[...] = jnp.zeros_like(dc_out)

    def gather_lanes(values):
        total = values[:, 0:128]
        for tile in range(1, width // 128):
            total = total + values[:, tile * 128 : (tile + 1) * 128]
        return total

    def one(t, before, carry):
        grad, drate, state = carry
        d = dt[0, pl.ds(t, 1), :]
        x = act[0, pl.ds(t, 1), :]
        g_y = dy[0, pl.ds(t, 1), :]
        w = d * x
        grad = grad + spread(readout[0, t], width) * g_y
        db_out[0, t] += gather_lanes(grad * w)
        dc_out[0, t] += gather_lanes(state * g_y)
        dw = jnp.sum(grad * spread(inject[0, t], width), axis=0, keepdims=True)
        grad = jnp.exp(rates * d) * keep[micro, t] * grad
        effect = grad * before
        drate = drate + effect * d
        ddt_out[0, pl.ds(t, 1), :] = (
            jnp.sum(effect * rates, axis=0, keepdims=True) + dw * x
        )
        da_out[0, pl.ds(t, 1), :] = dw * d
        return grad, drate, before

    def block(step, carry):
        for inner in range(UNROLL):
            t = tokens - 1 - (step * UNROLL + inner)
            carry = one(t, hs[0, t - 1], carry)
        return carry

    carry = (grad, jnp.zeros((STATES, width), F32), hs[0, tokens - 1])
    carry = lax.fori_loop(0, tokens // UNROLL - 1, block, carry)
    for t in range(UNROLL - 1, -1, -1):
        carry = one(t, hs[0, t - 1] if t else start[0], carry)
    drate_out[0] = carry[1]


def specs(tokens, seq_count):
    rows = pl.BlockSpec((1, tokens, LANES), lambda m, g: (m, 0, g))
    wide = pl.BlockSpec((1, tokens, STATES, 128), lambda m, g: (m, 0, 0, 0))
    rate = pl.BlockSpec((STATES, LANES), lambda m, g: (0, g))
    state = pl.BlockSpec((1, STATES, LANES), lambda m, g: (m, 0, g))
    edge = pl.BlockSpec((STATES, LANES), lambda m, g: (m, g))
    edges = pl.BlockSpec((seq_count, STATES, LANES), lambda m, g: (0, m, g))
    totals = pl.BlockSpec((seq_count, TOTAL_ROWS, LANES), lambda m, g: (0, 0, g))
    every = pl.BlockSpec((1, tokens, STATES, LANES), lambda m, g: (m, 0, 0, g))
    scalars = pl.BlockSpec(memory_space=pltpu.SMEM)
    return rows, wide, rate, state, edge, edges, totals, every, scalars


def kernel_params():
    return pltpu.CompilerParams(vmem_limit_bytes=48 * 1024 * 1024)


def scan_end(keep, dt, act, inject, rate):
    micros, tokens, inner = dt.shape
    rows, wide, rated, _, edge, _, _, _, scalars = specs(tokens, 1)
    return pl.pallas_call(
        end_kernel,
        grid=(micros, inner // LANES),
        in_specs=[scalars, rows, rows, wide, rated],
        out_specs=edge,
        out_shape=jax.ShapeDtypeStruct((micros * STATES, inner), BF16),
        compiler_params=kernel_params(),
        name="scan_end",
    )(keep, dt, act, inject, rate)


def scan_forward(place, keep, dt, act, inject, readout, rate, ends_all, totals_all):
    micros, tokens, inner = dt.shape
    rows, wide, rated, state, _, edges, totals, every, scalars = specs(tokens, ends_all.shape[0])
    return pl.pallas_call(
        forward_kernel,
        grid=(micros, inner // LANES),
        in_specs=[scalars, scalars, rows, rows, wide, wide, rated, edges, totals],
        out_specs=[rows, every, state],
        out_shape=[
            jax.ShapeDtypeStruct((micros, tokens, inner), F32),
            jax.ShapeDtypeStruct((micros, tokens, STATES, inner), F32),
            jax.ShapeDtypeStruct((micros, STATES, inner), F32),
        ],
        compiler_params=kernel_params(),
        name="scan_forward",
    )(place, keep, dt, act, inject, readout, rate, ends_all, totals_all)


def scan_start(keep, dt, dy, readout, rate, ahead):
    micros, tokens, inner = dt.shape
    rows, wide, rated, _, edge, _, _, _, scalars = specs(tokens, 1)
    unread = pl.BlockSpec(memory_space=pl.ANY)

    def body(keep, dt, dy, readout, rate, *rest):
        start_kernel(keep, dt, dy, readout, rate, rest[-1])

    return pl.pallas_call(
        body,
        grid=(micros, inner // LANES),
        in_specs=[scalars, rows, rows, wide, rated] + [unread] * len(ahead),
        out_specs=edge,
        out_shape=jax.ShapeDtypeStruct((micros * STATES, inner), BF16),
        compiler_params=kernel_params(),
        name="scan_start",
    )(keep, dt, dy, readout, rate, *ahead)


def scan_backward(
    place, keep, dt, act, dy, inject, readout, rate, totals_all, starts_all, start, hs, ahead
):
    micros, tokens, inner = dt.shape
    rows, wide, rated, state, _, edges, totals, every, scalars = specs(tokens, totals_all.shape[0])
    unread = pl.BlockSpec(memory_space=pl.ANY)

    def body(*refs):
        backward_kernel(*refs[:12], *refs[12 + len(ahead) :])

    return pl.pallas_call(
        body,
        grid=(micros, inner // LANES),
        in_specs=[
            scalars, scalars, rows, rows, rows, wide, wide, rated, totals, edges, state, every,
        ]
        + [unread] * len(ahead),
        out_specs=[rows, rows, wide, wide, state],
        out_shape=[
            jax.ShapeDtypeStruct((micros, tokens, inner), F32),
            jax.ShapeDtypeStruct((micros, tokens, inner), F32),
            jax.ShapeDtypeStruct((micros, tokens, STATES, 128), F32),
            jax.ShapeDtypeStruct((micros, tokens, STATES, 128), F32),
            jax.ShapeDtypeStruct((micros, STATES, inner), F32),
        ],
        compiler_params=kernel_params(),
        name="scan_backward",
    )(place, keep, dt, act, dy, inject, readout, rate, totals_all, starts_all, start, hs, *ahead)


def exchange_kernel(groups, gathers, ahead, through, *refs):
    arrays = len(groups)
    inputs, outputs = refs[:arrays], refs[arrays + ahead : 2 * arrays + ahead]
    sends, receives, own_sem = refs[2 * arrays + ahead + through :]

    def place_of(axes):
        if len(axes) == 1:
            return lax.axis_size(axes[0]), lax.axis_index(axes[0]), lambda peer: {axes[0]: peer}
        width = lax.axis_size(axes[1])
        return (
            lax.axis_size(axes[0]) * width,
            lax.axis_index(axes[0]) * width + lax.axis_index(axes[1]),
            lambda peer: {axes[0]: peer // width, axes[1]: peer % width},
        )

    def source(index, peer):
        return inputs[index] if gathers[index] else inputs[index].at[peer]

    def copy(index, device, peer, block):
        return pltpu.make_async_remote_copy(
            src_ref=source(index, peer),
            dst_ref=outputs[index].at[block],
            send_sem=sends.at[index, peer],
            recv_sem=receives.at[index, block],
            device_id=device(peer),
            device_id_type=MESH,
        )

    barrier = pltpu.get_barrier_semaphore()
    total = 0
    for axes in sorted(set(groups)):
        peers, me, device = place_of(axes)

        def greet(lap, _):
            pl.semaphore_signal(
                barrier, inc=1, device_id=device((me + lap) % peers), device_id_type=MESH
            )
            return _

        lax.fori_loop(1, peers, greet, 0)
        total += peers - 1
    own = []
    for index, axes in enumerate(groups):
        me = place_of(axes)[1]
        own.append(
            pltpu.make_async_copy(source(index, me), outputs[index].at[me], own_sem.at[index])
        )
        own[-1].start()
    pl.semaphore_wait(barrier, total)
    for index, axes in enumerate(groups):
        peers, me, device = place_of(axes)

        def begin(lap, _):
            copy(index, device, (me + lap) % peers, me).start()
            return _

        lax.fori_loop(1, peers, begin, 0)
    for index, axes in enumerate(groups):
        peers, me, device = place_of(axes)
        own[index].wait()

        def end(lap, _):
            before = (me + peers - lap) % peers
            copy(index, device, before, before).wait_recv()
            copy(index, device, (me + lap) % peers, me).wait_send()
            return _

        lax.fori_loop(1, peers, end, 0)


def exchange(
    values, gathers, identity, axes=("seq",), space=pltpu.VMEM, ahead=(), riders=(), through=()
):
    groups = [axes] * len(values) + [("mat",)] * len(riders)
    gathers = list(gathers) + [False] * len(riders)
    peers = [math.prod(lax.axis_size(axis) for axis in group) for group in groups]
    place = pl.BlockSpec(memory_space=space)
    unread = pl.BlockSpec(memory_space=pl.ANY)
    places = [place] * len(values) + [unread] * len(riders)
    values = list(values) + list(riders)
    shapes = [
        jax.ShapeDtypeStruct(((count,) if gather else ()) + value.shape, value.dtype)
        for value, gather, count in zip(values, gathers, peers)
    ]
    arrays = len(values)
    ahead = list(ahead) + list(through)
    first = arrays + len(ahead) - len(through)
    shapes += [jax.ShapeDtypeStruct(value.shape, value.dtype) for value in through]
    return pl.pallas_call(
        functools.partial(exchange_kernel, tuple(groups), tuple(gathers), len(ahead), len(through)),
        out_shape=shapes,
        in_specs=places + [unread] * len(ahead),
        out_specs=places + [unread] * len(through),
        input_output_aliases={first + index: arrays + index for index in range(len(through))},
        scratch_shapes=[
            pltpu.SemaphoreType.DMA((arrays, max(peers))),
            pltpu.SemaphoreType.DMA((arrays, max(peers))),
            pltpu.SemaphoreType.DMA((arrays,)),
        ],
        compiler_params=pltpu.CompilerParams(collective_id=identity, has_side_effects=True),
        name="exchange",
    )(*values, *ahead)


def hold(values, ahead):
    unread = pl.BlockSpec(memory_space=pl.ANY)
    return pl.pallas_call(
        lambda *refs: None,
        out_shape=[jax.ShapeDtypeStruct(value.shape, value.dtype) for value in values],
        in_specs=[unread] * (len(values) + 1),
        out_specs=[unread] * len(values),
        input_output_aliases={index: index for index in range(len(values))},
        name="hold",
    )(*values, ahead)


class Line:
    SEMAPHORES = 6

    def __init__(self, inputs, outputs, semaphores):
        self.inputs, self.outputs = inputs, outputs
        self.sends, self.receives = semaphores[0::2], semaphores[1::2]
        self.outers = lax.axis_size("seq") // 2
        me = lax.axis_index("seq")
        self.outer, self.inner = me // 2, me % 2
        self.later = self.outer + 1 < self.outers
        self.earlier = self.outer > 0

    def block(self, outer):
        return outer * 2 + self.inner

    def across(self, outer):
        return outer * 2 + 1 - self.inner

    def target(self, way):
        step = (2, -2, 1 - 2 * self.inner)[way]
        return {"seq": self.outer * 2 + self.inner + step}

    def pieces(self):
        for index, source in enumerate(self.inputs):
            for piece in range(source.shape[0]):
                yield index, piece

    def copy(self, way, index, outer, piece, place, first=False):
        source = self.outputs[index].at[place, piece]
        return pltpu.make_async_remote_copy(
            src_ref=self.inputs[index].at[piece] if first else source,
            dst_ref=self.outputs[index].at[place, piece],
            send_sem=self.sends[way].at[index, outer, piece],
            recv_sem=self.receives[way].at[index, outer, piece],
            device_id=self.target(way),
            device_id_type=MESH,
        )

    def ways(self):
        return ((0, self.later), (1, self.earlier))

    def greet(self, barrier):
        for way, exists in self.ways():

            @pl.when(exists)
            def _():
                pl.semaphore_signal(
                    barrier, inc=1, device_id=self.target(way), device_id_type=MESH
                )

        pl.semaphore_signal(barrier, inc=1, device_id=self.target(2), device_id_type=MESH)
        return 1 + self.later.astype(jnp.int32) + self.earlier.astype(jnp.int32)

    def begin(self):
        mine = self.block(self.outer)
        for index, piece in self.pieces():
            for way, exists in self.ways():

                @pl.when(exists)
                def _():
                    self.copy(way, index, self.outer, piece, mine, True).start()

            self.copy(2, index, self.outer, piece, mine, True).start()

    def forward(self, lap):
        for index, piece in self.pieces():
            for way, exists in self.ways():
                outer = self.outer + (-lap, lap)[way]
                place = self.block(outer)

                @pl.when(jnp.logical_and(outer >= 0, outer < self.outers))
                def _():
                    self.copy(way, index, outer, piece, place).wait_recv()

                    @pl.when(exists)
                    def _():
                        self.copy(way, index, outer, piece, place).start()

                    self.copy(2, index, outer, piece, place).start()

    def take(self, outer):
        for index, piece in self.pieces():
            self.copy(2, index, outer, piece, self.across(outer)).wait_recv()

    def each(self, lap, use):
        for way in range(2):
            outer = self.outer + (-lap, lap)[way]

            @pl.when(jnp.logical_and(outer >= 0, outer < self.outers))
            def _():
                use(self.block(outer))
                self.take(outer)
                use(self.across(outer))

    def end(self):
        def one(outer, _):
            for index, piece in self.pieces():
                place = self.block(outer)

                @pl.when(jnp.logical_and(self.later, outer <= self.outer))
                def _():
                    self.copy(0, index, outer, piece, place).wait_send()

                @pl.when(jnp.logical_and(self.earlier, outer >= self.outer))
                def _():
                    self.copy(1, index, outer, piece, place).wait_send()

                self.copy(2, index, outer, piece, place).wait_send()
            return 0

        lax.fori_loop(0, self.outers, one, 0)


def line_semaphores(values):
    shape = (len(values), lax.axis_size("seq") // 2, max(value.shape[0] for value in values))
    return [pltpu.SemaphoreType.DMA(shape)] * Line.SEMAPHORES


def gather_kernel(arrays, ahead, relays, *refs):
    inputs = refs[:arrays]
    outputs = refs[arrays + ahead : 2 * arrays + ahead]
    wholes = refs[2 * arrays + ahead : 2 * arrays + ahead + len(relays)]
    rest = refs[2 * arrays + ahead + len(relays) :]
    line = Line(inputs, outputs, rest[: Line.SEMAPHORES])
    own_sem, relay_sends, relay_receives, relay_own = rest[Line.SEMAPHORES :]
    mats, here = lax.axis_size("mat"), lax.axis_index("mat")
    me = lax.axis_index("seq")

    def relayed(relay, block, origin):
        index, place = relays[relay]
        return pltpu.make_async_remote_copy(
            src_ref=outputs[index].at[block],
            dst_ref=wholes[relay].at[origin, block],
            send_sem=relay_sends.at[relay, block],
            recv_sem=relay_receives.at[relay, origin, block],
            device_id={"mat": place},
            device_id_type=MESH,
        )

    def kept(relay, block):
        index, place = relays[relay]
        return pltpu.make_async_copy(
            outputs[index].at[block], wholes[relay].at[place, block], relay_own.at[relay, block]
        )

    def relay_all(block):
        for relay, (_, place) in enumerate(relays):

            @pl.when(here != place)
            def _():
                relayed(relay, block, here).start()

            @pl.when(here == place)
            def _():
                kept(relay, block).start()

    def relay_end(block, _):
        for relay, (_, place) in enumerate(relays):

            @pl.when(here != place)
            def _():
                relayed(relay, block, here).wait_send()

            @pl.when(here == place)
            def _():
                kept(relay, block).wait()
                for origin in range(mats):
                    if origin != place:
                        relayed(relay, block, origin).wait_recv()

        return 0

    barrier = pltpu.get_barrier_semaphore()
    greeted = line.greet(barrier)
    if relays:

        def greet_mat(lap, _):
            pl.semaphore_signal(
                barrier, inc=1, device_id={"mat": (here + lap) % mats}, device_id_type=MESH
            )
            return 0

        lax.fori_loop(1, mats, greet_mat, 0)
        greeted = greeted + mats - 1
    own = [
        pltpu.make_async_copy(inputs[index], outputs[index].at[me], own_sem.at[index])
        for index in range(arrays)
    ]
    for copy in own:
        copy.start()
    pl.semaphore_wait(barrier, greeted)
    line.begin()
    for copy in own:
        copy.wait()
    relay_all(me)

    def step(lap, _):
        line.forward(lap)

        @pl.when(lap > 1)
        def _():
            line.each(lap - 1, relay_all)

        return 0

    lax.fori_loop(1, line.outers, step, 0)
    line.take(line.outer)
    relay_all(line.across(line.outer))
    line.each(line.outers - 1, relay_all)
    line.end()
    if relays:
        lax.fori_loop(0, lax.axis_size("seq"), relay_end, 0)


def gather_seq(values, identity, space=pltpu.VMEM, ahead=(), relays=()):
    peers = lax.axis_size("seq")
    mats = lax.axis_size("mat")
    plain = [value.shape for value in values]
    values = [
        value.reshape((2, -1) + value.shape[1:]) if value.shape[0] % 32 == 0 else value[None]
        for value in values
    ]
    shapes = [jax.ShapeDtypeStruct((peers,) + value.shape, value.dtype) for value in values]
    shapes += [
        jax.ShapeDtypeStruct((mats, peers) + values[index].shape, values[index].dtype)
        for index, _ in relays
    ]
    place = pl.BlockSpec(memory_space=space)
    unread = pl.BlockSpec(memory_space=pl.ANY)
    arrays = len(values)
    results = pl.pallas_call(
        functools.partial(gather_kernel, arrays, len(ahead), tuple(relays)),
        out_shape=shapes,
        in_specs=[place] * arrays + [unread] * len(ahead),
        out_specs=[place] * arrays + [unread] * len(relays),
        scratch_shapes=line_semaphores(values)
        + [
            pltpu.SemaphoreType.DMA((arrays,)),
            pltpu.SemaphoreType.DMA((max(1, len(relays)), peers)),
            pltpu.SemaphoreType.DMA((max(1, len(relays)), mats, peers)),
            pltpu.SemaphoreType.DMA((max(1, len(relays)), peers)),
        ],
        compiler_params=pltpu.CompilerParams(collective_id=identity, has_side_effects=True),
        name="gather_seq",
    )(*values, *ahead)
    gathered = [result.reshape((peers,) + shape) for result, shape in zip(results, plain)]
    relayed = [
        result.reshape((mats, peers) + plain[index])
        for result, (index, _) in zip(results[arrays:], relays)
    ]
    return gathered + relayed


def lookup_kernel(
    ids, table, small, out, smalls, found, give, got, keep, taken, passes, arrivals, sends,
    receives, small_sends, small_receives, small_own,
):
    outers, mats = taken.shape[0], taken.shape[1]
    me = lax.axis_index("seq")
    here = lax.axis_index("mat")
    outer, inner = me // 2, me % 2
    partner = {"seq": outer * 2 + 1 - inner}
    tokens = 256
    lanes = lax.broadcasted_iota(jnp.int32, (128, 128), 1)

    def device(to_outer, to_mat):
        return {"seq": to_outer * 2 + inner, "mat": to_mat}

    def hand(lap, place):
        return pltpu.make_async_remote_copy(
            src_ref=give.at[lap, place],
            dst_ref=got.at[lap, place],
            send_sem=passes.at[lap, place],
            recv_sem=arrivals.at[lap, place],
            device_id=partner,
            device_id_type=MESH,
        )

    def send(to_outer, to_mat, from_outer, from_mat):
        return pltpu.make_async_remote_copy(
            src_ref=keep.at[to_outer, to_mat],
            dst_ref=taken.at[from_outer, from_mat],
            send_sem=sends.at[to_outer, to_mat],
            recv_sem=receives.at[from_outer, from_mat],
            device_id=device(to_outer, to_mat),
            device_id_type=MESH,
        )

    def share(to_mat, from_mat):
        return pltpu.make_async_remote_copy(
            src_ref=small,
            dst_ref=smalls.at[from_mat],
            send_sem=small_sends.at[to_mat],
            recv_sem=small_receives.at[from_mat],
            device_id={"mat": to_mat},
            device_id_type=MESH,
        )

    own_small = pltpu.make_async_copy(small, smalls.at[here], small_own)
    own_small.start()
    barrier = pltpu.get_barrier_semaphore()

    def greet(lap, _):
        pl.semaphore_signal(
            barrier,
            inc=1,
            device_id=device((outer + lap // mats) % outers, (here + lap % mats) % mats),
            device_id_type=MESH,
        )
        return _

    pl.semaphore_signal(barrier, inc=1, device_id=partner, device_id_type=MESH)
    lax.fori_loop(1, outers * mats, greet, 0)
    pl.semaphore_wait(barrier, outers * mats)

    def share_start(lap, _):
        share((here + lap) % mats, here).start()
        return 0

    lax.fori_loop(1, mats, share_start, 0)

    def find(block):
        def rows(index, _):
            for step in range(8):
                row = index * 8 + step
                entry = ids[block * mats * tokens + row]
                found[pl.ds(row, 1), :] = table[pl.ds(entry, 1), :]
            return 0

        lax.fori_loop(0, mats * tokens // 8, rows, 0)

    def store(target):
        for place in range(mats):
            base = place * tokens
            target[place, 0:tokens, :] = found[base : base + tokens, 0:128].astype(BF16)
            low = found[base : base + 128, 128:256]
            high = pltpu.roll(found[base + 128 : base + tokens, 128:256], 64, 1)
            target[place, tokens : tokens + 128, :] = jnp.where(lanes < 64, low, high).astype(BF16)

    def outer_of(lap):
        return (outer + 1 + lap) % outers

    def hand_over(lap):
        find(outer_of(lap) * 2 + 1 - inner)
        store(give.at[lap])
        for place in range(mats):
            hand(lap, place).start()

    def compute(lap, _):
        to_outer = outer_of(lap)

        @pl.when(lap + 1 < outers)
        def _():
            hand_over(lap + 1)

        find(to_outer * 2 + inner)
        store(keep.at[to_outer])
        for place in range(mats):
            hand(lap, place).wait_recv()
            keep[to_outer, place] = keep[to_outer, place] + got[lap, place]
            own = jnp.logical_and(to_outer == outer, place == here)

            @pl.when(jnp.logical_not(own))
            def _():
                send(to_outer, place, outer, here).start()

            @pl.when(own)
            def _():
                taken[outer, here] = keep[to_outer, place]

        return 0

    hand_over(0)
    lax.fori_loop(0, outers, compute, 0)

    def finish(lap, _):
        to_outer, to_mat = (outer + lap // mats) % outers, (here + lap % mats) % mats
        send(to_outer, to_mat, to_outer, to_mat).wait_recv()
        send(to_outer, to_mat, outer, here).wait_send()
        return _

    lax.fori_loop(1, outers * mats, finish, 0)

    def end(lap, _):
        for place in range(mats):
            hand(lap, place).wait_send()
        return 0

    lax.fori_loop(0, outers, end, 0)

    def share_end(lap, _):
        before = (here + mats - lap) % mats
        share(before, before).wait_recv()
        share((here + lap) % mats, here).wait_send()
        return 0

    lax.fori_loop(1, mats, share_end, 0)
    own_small.wait()
    for place in range(mats):

        def gather(source, total):
            return total + taken[source, place].astype(F32)

        out[place] = lax.fori_loop(0, outers, gather, jnp.zeros((384, 128), F32)).astype(BF16)


def lookup(ids, table, small, identity):
    outers, mats = lax.axis_size("seq") // 2, lax.axis_size("mat")
    entries, part = table.shape
    padded = (entries // 8 + 1) * 8
    table = table.astype(BF16).astype(F32)
    table = jnp.pad(table, ((0, padded - entries), (0, 256 - part)))
    ids = jnp.where((ids >= 0) & (ids < entries), ids, entries)
    vmem = pl.BlockSpec(memory_space=pltpu.VMEM)
    blocks = pltpu.VMEM((outers, mats, 384, 128), BF16)
    return pl.pallas_call(
        lookup_kernel,
        out_shape=[
            jax.ShapeDtypeStruct((mats, 384, 128), BF16),
            jax.ShapeDtypeStruct((mats,) + small.shape, BF16),
        ],
        in_specs=[pl.BlockSpec(memory_space=pltpu.SMEM), vmem, vmem],
        out_specs=[vmem, vmem],
        scratch_shapes=[
            pltpu.VMEM((mats * 256, 256), F32),
            blocks,
            blocks,
            blocks,
            blocks,
            *[pltpu.SemaphoreType.DMA((outers, mats))] * 4,
            pltpu.SemaphoreType.DMA((mats,)),
            pltpu.SemaphoreType.DMA((mats,)),
            pltpu.SemaphoreType.DMA,
        ],
        compiler_params=pltpu.CompilerParams(
            collective_id=identity, has_side_effects=True, vmem_limit_bytes=56 * 1024 * 1024
        ),
        name="lookup",
    )(ids, table, small)


def scatter_rows_kernel(
    entries, ids, rows, others, first_rider, second_rider, out, squares, whole, buffer, *rest
):
    line = Line([rows], [buffer], rest[: Line.SEMAPHORES])
    rider_sends, rider_receives, rider_own = rest[Line.SEMAPHORES :]
    places = lax.axis_size("mat")
    here = lax.axis_index("mat")
    riders = ((first_rider, UP_PLACE), (second_rider, DOWN_PLACE))

    def ride(rider, origin):
        source, place = riders[rider]
        return pltpu.make_async_remote_copy(
            src_ref=source,
            dst_ref=whole.at[origin],
            send_sem=rider_sends.at[rider],
            recv_sem=rider_receives.at[origin],
            device_id={"mat": place},
            device_id_type=MESH,
        )

    def stay(rider):
        source, place = riders[rider]
        return pltpu.make_async_copy(source, whole.at[place], rider_own)

    mats = rows.shape[0]
    lanes = lax.broadcasted_iota(jnp.int32, (128, 128), 1)

    def add(block, source):
        parts = []
        for place in range(mats):
            tail = source[place, 256:384, :].astype(F32)
            low = jnp.where(lanes < 64, tail, 0.0)
            high = jnp.where(lanes < 64, pltpu.roll(tail, 64, 1), 0.0)
            tails = jnp.concatenate([low, high], axis=0).astype(BF16)
            parts.append(jnp.concatenate([source[place, 0:256, :], tails], axis=1))
        values = jnp.concatenate(parts, axis=0)
        names = jnp.concatenate(
            [ids[pl.ds(block * 2 * mats + half, 1), :] for half in range(2 * mats)], axis=1
        )
        group = lax.shift_right_arithmetic(names, 7)
        spot = lax.broadcasted_iota(jnp.int32, (128, names.shape[1]), 0)
        hits = jnp.where(spot == jnp.bitwise_and(names, 127), 1.0, 0.0).astype(BF16)

        def piece(index, _):
            first = pl.multiple_of(index * VOCAB_TILE, VOCAB_TILE)
            masked = []
            for step in range(VOCAB_TILE // 128):
                chosen = jnp.where(group == index * (VOCAB_TILE // 128) + step, 1.0, 0.0)
                masked.append(hits * chosen.astype(BF16))
            out[pl.ds(first, VOCAB_TILE), :] += dot(
                jnp.concatenate(masked, axis=0), values, 1, 0
            )
            return 0

        lax.fori_loop(0, out.shape[0] // VOCAB_TILE, piece, 0)

    barrier = pltpu.get_barrier_semaphore()
    greeted = line.greet(barrier)

    def greet_mat(lap, _):
        pl.semaphore_signal(
            barrier, inc=1, device_id={"mat": (here + lap) % places}, device_id_type=MESH
        )
        return _

    lax.fori_loop(1, places, greet_mat, 0)
    out[...] = jnp.zeros_like(out)
    pl.semaphore_wait(barrier, greeted + places - 1)
    line.begin()
    for rider, (_, place) in enumerate(riders):

        @pl.when(here != place)
        def _():
            ride(rider, here).start()

        @pl.when(here == place)
        def _():
            stay(rider).start()

    def use(block):
        add(block, buffer.at[block])

    add(line.block(line.outer), rows)

    def step(lap, _):
        line.forward(lap)

        @pl.when(lap == 1)
        def _():
            line.take(line.outer)
            use(line.across(line.outer))

        @pl.when(lap > 1)
        def _():
            line.each(lap - 1, use)

        return 0

    lax.fori_loop(1, line.outers, step, 0)
    line.each(line.outers - 1, use)
    line.end()
    for rider, (_, place) in enumerate(riders):

        @pl.when(here != place)
        def _():
            ride(rider, here).wait_send()

        @pl.when(here == place)
        def _():
            stay(rider).wait()
            for origin in range(places):
                if origin != place:
                    ride(rider, origin).wait_recv()

    part = others.shape[0]

    def finish(index, total):
        cut = pl.ds(pl.multiple_of(index * VOCAB_TILE, VOCAB_TILE), VOCAB_TILE)
        more = others[:, cut].astype(F32).T
        more = jnp.concatenate([more, jnp.zeros((VOCAB_TILE, 256 - part), F32)], axis=1)
        values = out[cut, :] + more
        out[cut, :] = values
        entry = lax.broadcasted_iota(jnp.int32, values.shape, 0) + index * VOCAB_TILE
        values = jnp.where(entry < entries, values, 0.0)
        return total + jnp.sum(values * values, axis=0, keepdims=True)

    total = lax.fori_loop(0, out.shape[0] // VOCAB_TILE, finish, jnp.zeros((1, 256), F32))
    squares[...] = jnp.broadcast_to(total, (8, 256))


def scatter_rows(ids, rows, others, entries, identity, riders):
    peers = lax.axis_size("seq")
    mats = lax.axis_size("mat")
    padded = -(-entries // VOCAB_TILE) * VOCAB_TILE
    unread = pl.BlockSpec(memory_space=pl.ANY)
    place = pl.BlockSpec(memory_space=pltpu.VMEM)
    return pl.pallas_call(
        functools.partial(scatter_rows_kernel, entries),
        out_shape=[
            jax.ShapeDtypeStruct((padded, 256), F32),
            jax.ShapeDtypeStruct((8, 256), F32),
            jax.ShapeDtypeStruct((mats,) + riders[0].shape, BF16),
        ],
        in_specs=[place, place, place, unread, unread],
        out_specs=[place, place, unread],
        scratch_shapes=[
            pltpu.VMEM((peers,) + rows.shape, BF16),
            *line_semaphores([rows]),
            pltpu.SemaphoreType.DMA((2,)),
            pltpu.SemaphoreType.DMA((mats,)),
            pltpu.SemaphoreType.DMA,
        ],
        compiler_params=pltpu.CompilerParams(
            collective_id=identity, has_side_effects=True, vmem_limit_bytes=48 * 1024 * 1024
        ),
        name="scatter_rows",
    )(ids, rows, jnp.pad(others, ((0, 0), (0, padded - entries))), *riders)


def swap_seq(value, identity, ahead=()):
    return exchange([value], [False], identity, ahead=ahead)[0]


def move_rows(value, steps):
    count = lax.axis_size("seq")
    leading, last = (max(0, -steps), min(count, count - steps))
    return lax.ppermute(value, "seq", [(source, source + steps) for source in range(leading, last)])


def normalize(values, gain):
    scale = lax.rsqrt(jnp.mean(values * values, axis=-1, keepdims=True) + 1e-05)
    hat = values * scale
    return hat * gain, hat, scale


def normalize_back(hat, scale, gain, grad):
    gain_grad = jnp.sum(grad * hat, axis=0)
    hat_grad = grad * gain
    return gain_grad, scale * (hat_grad - hat * jnp.mean(hat_grad * hat, axis=-1, keepdims=True))


def silu_back(values):
    sig = jax.nn.sigmoid(values)
    return sig * (1.0 + values * (1.0 - sig))


def padded_rows(flat):
    size = flat.shape[-1]
    room = -(-size // 16384) * 16384 - size
    flat = jnp.pad(flat, [(0, 0)] * (flat.ndim - 1) + [(0, room)])
    return flat.reshape(flat.shape[:-1] + (-1, 1024))


def pack_small(parts):
    return padded_rows(jnp.concatenate([part.astype(BF16).reshape(-1) for part in parts]))


def unpack_small(every, parts):
    every = every.reshape(every.shape[0], -1)
    result, offset = [], 0
    for part in parts:
        size = part.size
        result.append(every[:, offset : offset + size].reshape((-1,) + part.shape))
        offset += size
    return result


def columns(stacked):
    count, rows, width = stacked.shape
    return stacked.transpose(1, 0, 2).reshape(rows, count * width)


def step_grads(weights, moments, embedded, route, lengths, slots, weight_mask, targets, loss_all):
    table, w_in, w_out, w_up, w_down, w_x, w_step, w_route, chan_low, gains_low = weights
    channel = chan_low.astype(F32)
    gains = gains_low.astype(F32)
    me = lax.axis_index("seq")
    count = lax.axis_size("seq")
    micros, tokens = route.shape
    inner = w_in.shape[1] // 2
    vocab_part = table.shape[0]
    first_pos = me * tokens
    vocab_start = me * vocab_part
    ext_pos = first_pos - (CONV - 1) + jnp.arange(tokens + CONV - 1, dtype=jnp.int32)
    bounds = jnp.cumsum(lengths, axis=1)
    ext_doc = jnp.sum((ext_pos[None, :, None] >= bounds[:, None, :-1]).astype(jnp.int32), axis=2)
    ext_doc = jnp.where(ext_pos[None] >= 0, ext_doc, -1)
    starts = jnp.concatenate([jnp.zeros((micros, 1), jnp.int32), bounds[:, :-1]], axis=1)
    keeping = 1.0 - jnp.any(
        ext_pos[None, CONV - 1 :, None] == starts[:, None, :], axis=2
    ).astype(F32)
    own_doc = ext_doc[:, CONV - 1 :]
    same = [
        (ext_doc[:, tap : tap + tokens] == own_doc).astype(F32)[:, :, None] for tap in range(CONV)
    ]
    place = me.astype(jnp.int32).reshape(1)

    x0 = embedded.astype(F32)

    u, hat0, scale0 = normalize(x0, gains[0])
    u_low = u.astype(BF16)
    xz = dot(u_low, w_in, 1, 0).reshape(micros, tokens, 2 * inner)
    raw, z = xz[:, :, :inner], xz[:, :, inner:]
    edge = move_rows(raw[:, tokens - (CONV - 1) :], 1)
    padded = jnp.concatenate([edge, raw], axis=1)
    conv = channel[CONV] + jnp.zeros((micros, tokens, inner), F32)
    for tap in range(CONV):
        conv = conv + channel[tap] * padded[:, tap : tap + tokens] * same[tap]
    act = jax.nn.silu(conv)
    act_low = act.reshape(-1, inner).astype(BF16)
    projected = dot(act_low, w_x, 1, 0)
    rank_low = projected[:, :RANK].astype(BF16)
    pre = dot(rank_low, w_step, 1, 0).reshape(micros, tokens, inner) + channel[CONV + 1]
    dt = jax.nn.softplus(pre)
    rate = -jnp.exp(channel[CONV + 3 :])
    wide = projected.reshape(micros, tokens, -1)[:, :, :, None]
    wide_shape = (micros, tokens, STATES, 128)
    inject = jnp.broadcast_to(wide[:, :, RANK : RANK + STATES], wide_shape)
    readout = jnp.broadcast_to(wide[:, :, RANK + STATES :], wide_shape)
    totals = jnp.concatenate(
        [
            jnp.sum(dt, axis=1),
            jnp.broadcast_to(jnp.prod(keeping, axis=1)[:, None], (micros, inner)),
            jnp.zeros((TOTAL_ROWS - 2 * micros, inner), F32),
        ]
    )
    ends_all, totals_all = gather_seq(
        [scan_end(keeping, dt, act, inject, rate), totals], 1
    )
    y, hs, start = scan_forward(
        place, keeping, dt, act, inject, readout, rate, ends_all, totals_all
    )
    skip = channel[CONV + 2]
    z_silu = jax.nn.silu(z)
    core = y + skip * act
    mixed_low = (core * z_silu).reshape(-1, inner).astype(BF16)
    x1 = x0 + dot(mixed_low, w_out, 1, 0)

    experts = w_route.shape[1]
    capacity = max(2, 2 * tokens // experts)
    local_experts = w_up.shape[0]
    s, hat1, scale1 = normalize(x1, gains[1])
    s_low = s.astype(BF16)
    scores = dot(s_low, w_route, 1, 0)
    chosen = route.reshape(-1)[:, None] == jnp.arange(experts, dtype=jnp.int32)[None, :]
    gate = jax.nn.sigmoid(jnp.sum(jnp.where(chosen, scores, 0.0), axis=1))
    onehot = chosen.astype(jnp.int32).reshape(micros, tokens, experts)
    ranking = jnp.sum(jnp.cumsum(onehot, axis=1) * onehot, axis=2) - 1
    placed = route * capacity + ranking
    all_slots = experts * capacity
    sender = (
        placed[:, None, :] == jnp.arange(all_slots, dtype=jnp.int32)[None, :, None]
    ).astype(BF16)

    moved = []

    def swap_seq(value, identity, ahead=(), riders=(), through=()):
        result = exchange(
            [value], [False], identity, ahead=ahead, riders=riders, through=through
        )
        moved.extend(result[1:])
        return result[0]

    def to_experts(rows, identity, ahead=(), riders=()):
        sent = jnp.einsum(
            "mst,mtd->msd", sender, rows.reshape(micros, tokens, D), preferred_element_type=F32
        ).astype(BF16)
        sent = sent.reshape(micros, count, -1, D).transpose(1, 0, 2, 3).reshape(count, -1, D)
        arrived = swap_seq(sent, identity, ahead, riders).reshape(count, micros, local_experts, capacity, D)
        return arrived.transpose(2, 0, 1, 3, 4).reshape(local_experts, -1, D)

    def from_experts(rows, identity, ahead=(), riders=(), through=()):
        rows = rows.reshape(local_experts, count, micros, capacity, D).transpose(1, 2, 0, 3, 4)
        back = swap_seq(rows.reshape(count, -1, D), identity, ahead, riders, through)
        back = back.reshape(count, micros, -1, D)
        back = back.transpose(1, 0, 2, 3).reshape(micros, all_slots, D)
        return jnp.einsum("mst,msd->mtd", sender, back, preferred_element_type=F32).reshape(-1, D)

    taken = to_experts(s_low, 2, (), [moments[0]])
    hidden_pre = jnp.einsum("erk,ekn->ern", taken, w_up, preferred_element_type=F32)
    gelu = functools.partial(jax.nn.gelu, approximate=False)
    hidden_low = gelu(hidden_pre).astype(BF16)
    result = jnp.einsum("erk,ekn->ern", hidden_low, w_down, preferred_element_type=F32)
    combined = from_experts(result.astype(BF16), 3, (), [moments[1]])
    x2 = x1 + gate[:, None] * combined

    final, hat2, scale2 = normalize(x2, gains[2])
    own_count = slots.shape[1]
    local_rows = slots - first_pos
    select = (
        local_rows[:, :, None] == jnp.arange(tokens, dtype=jnp.int32)[None, None, :]
    ).astype(BF16)
    picked_rows = jnp.einsum(
        "mst,mtd->msd",
        select,
        final.astype(BF16).reshape(micros, tokens, D),
        preferred_element_type=F32,
    ).astype(BF16)
    rows = gather_seq([picked_rows.reshape(-1, D)], 4)[0].reshape(count * micros * own_count, D)

    def by_device(values):
        return values.reshape(micros, count, own_count).transpose(1, 0, 2).reshape(-1)

    targets = by_device(targets)
    counted = by_device(weight_mask).astype(F32)
    logits = dot(rows, table, 1, 1)
    column = vocab_start + jnp.arange(vocab_part, dtype=jnp.int32)
    valid = column < VOCAB_REAL
    masked = jnp.where(valid[None, :], logits, -1e30)
    largest = jnp.max(masked, axis=1)
    expsum = jnp.sum(jnp.exp(masked - largest[:, None]), axis=1)
    hitting = column[None, :] == targets[:, None]
    target_logit = jnp.sum(jnp.where(hitting, logits, 0.0), axis=1)
    stats = exchange(
        [jnp.stack([largest, expsum, target_logit] + [jnp.zeros_like(largest)] * 5)], [True], 5
    )[0]
    top = jnp.max(stats[:, 0], axis=0)
    lse = top + jnp.log(jnp.sum(stats[:, 1] * jnp.exp(stats[:, 0] - top[None]), axis=0))
    unweighted = lse - jnp.sum(stats[:, 2], axis=0)

    def own(values):
        return lax.dynamic_index_in_dim(
            values.reshape(count, micros, own_count), me, 0, keepdims=False
        )

    rows_here = own(unweighted)
    counted_here = own(counted)
    loss_here = jnp.sum(rows_here * counted_here)
    count_here = jnp.sum(counted_here)
    probability = jnp.where(valid[None, :], jnp.exp(masked - lse[:, None]), 0.0)
    logit_grad = (
        (counted / loss_all)[:, None] * (probability - hitting.astype(F32))
    ).astype(BF16)
    rows_grad = swap_seq(
        dot(logit_grad, table, 1, 0).astype(BF16).reshape(count, -1, D), 6, (), [moments[2]]
    )
    rows_grad = jnp.sum(rows_grad.astype(F32), axis=0).reshape(micros, own_count, D)
    table_grad = dot(rows, logit_grad, 0, 0).astype(BF16)
    final_grad = jnp.einsum(
        "mst,msd->mtd",
        select.astype(F32),
        rows_grad,
        precision=lax.Precision.HIGHEST,
        preferred_element_type=F32,
    ).reshape(-1, D)
    gain_two, x2_grad = normalize_back(hat2, scale2, gains[2], final_grad)

    gate_grad = jnp.sum(x2_grad * combined, axis=1)
    out_grad = to_experts((gate[:, None] * x2_grad).astype(BF16), 7, [table_grad])
    hidden_grad = jnp.einsum("ern,ekn->erk", out_grad, w_down, preferred_element_type=F32)
    down_grad = jnp.einsum("erk,ern->ekn", hidden_low, out_grad, preferred_element_type=F32)
    _, gelu_back = jax.vjp(gelu, hidden_pre)
    pre_grad = gelu_back(hidden_grad)[0].astype(BF16)
    up_grad = jnp.einsum("erk,ern->ekn", taken, pre_grad, preferred_element_type=F32)
    taken_grad = jnp.einsum("ern,ekn->erk", pre_grad, w_up, preferred_element_type=F32)
    s_table = scatter_mat(table_grad, 0)
    up_grad, down_grad = hold([up_grad.astype(BF16), down_grad.astype(BF16)], s_table)
    s_grad = from_experts(taken_grad.astype(BF16), 8, [up_grad, down_grad])
    s_up = scatter_mat(up_grad, 2)
    s_down = scatter_mat(down_grad, 1)
    score_grad = jnp.where(chosen, (gate_grad * gate * (1.0 - gate))[:, None], 0.0).astype(BF16)
    route_grad = dot(s_low, score_grad, 0, 0)
    s_grad = s_grad + dot(score_grad, w_route, 1, 1)
    gain_one, more = normalize_back(hat1, scale1, gains[1], s_grad)
    x1_grad = x2_grad + more

    x1_grad_low = x1_grad.astype(BF16)
    mixed_grad = dot(x1_grad_low, w_out, 1, 1).reshape(micros, tokens, inner)
    out_weight_grad = dot(mixed_low, x1_grad_low, 0, 0)
    y_grad = mixed_grad * z_silu
    z_grad = mixed_grad * core * silu_back(z)
    out_weight_grad = out_weight_grad.astype(BF16)
    s_out = scatter_mat(out_weight_grad, 0)
    starts_all = gather_seq(
        [scan_start(keeping, dt, y_grad, readout, rate, [out_weight_grad])], 9
    )[0]
    dt_grad, act_grad, inject_grad, readout_grad, rate_grad = scan_backward(
        place, keeping, dt, act, y_grad, inject, readout, rate, totals_all, starts_all, start, hs,
        [],
    )
    skip_grad = jnp.sum(y_grad * act, axis=(0, 1))
    act_grad = act_grad + y_grad * skip
    pre_dt = dt_grad * jax.nn.sigmoid(pre)
    pre_dt_low = pre_dt.reshape(-1, inner).astype(BF16)
    step_weight_grad = dot(rank_low, pre_dt_low, 0, 0)
    projected_grad = jnp.concatenate(
        [
            dot(pre_dt_low, w_step, 1, 1),
            jnp.sum(inject_grad, axis=3).reshape(-1, STATES),
            jnp.sum(readout_grad, axis=3).reshape(-1, STATES),
        ],
        axis=1,
    ).astype(BF16)
    x_weight_grad = dot(act_low, projected_grad, 0, 0)
    act_grad = act_grad + dot(projected_grad, w_x, 1, 1).reshape(micros, tokens, inner)
    conv_grad = act_grad * silu_back(conv)
    chan_rows = [
        jnp.sum(conv_grad * padded[:, tap : tap + tokens] * same[tap], axis=(0, 1))
        for tap in range(CONV)
    ]
    chan_rows += [jnp.sum(conv_grad, axis=(0, 1)), jnp.sum(pre_dt, axis=(0, 1)), skip_grad]
    chan_grad = jnp.concatenate(
        [jnp.stack(chan_rows), jnp.sum(rate_grad, axis=0) * rate], axis=0
    )
    padded_grad = jnp.zeros((micros, tokens + CONV - 1, inner), F32)
    for tap in range(CONV):
        padded_grad = padded_grad + jnp.pad(
            channel[tap] * conv_grad * same[tap], ((0, 0), (tap, CONV - 1 - tap), (0, 0))
        )
    edge_grad = move_rows(padded_grad[:, : CONV - 1], -1)
    raw_grad = padded_grad[:, CONV - 1 :] + jnp.pad(
        edge_grad, ((0, 0), (tokens - (CONV - 1), 0), (0, 0))
    )
    xz_grad = jnp.concatenate([raw_grad, z_grad], axis=2).reshape(-1, 2 * inner).astype(BF16)
    in_grad = dot(u_low, xz_grad, 0, 0)
    gain_zero, more = normalize_back(hat0, scale0, gains[0], dot(xz_grad, w_in, 1, 1))
    x0_grad = (x1_grad + more).astype(BF16)
    grads = (
        s_table,
        scatter_mat(in_grad, 1),
        s_out,
        s_up,
        s_down,
        x_weight_grad,
        step_weight_grad,
        route_grad,
        chan_grad,
        jnp.stack([gain_zero, gain_one, gain_two]),
    )
    return grads, moved, x0_grad, loss_here, count_here, rows_here


def scatter_mat(grad, dim):
    return lax.psum_scatter(grad.astype(BF16), "mat", scatter_dimension=dim, tiled=True)


def ortho_kernel(
    place, scale, moment_a, moment_b, moment_c, experts, inward, outward, out,
    current, rounded, gram, low, poly, slope, trace,
):
    blocks, size, _ = experts.shape
    tile = TILE
    tiles = size // tile
    cuts = size // CUT
    row = lax.broadcasted_iota(jnp.int32, (tile, size), 0)
    column = lax.broadcasted_iota(jnp.int32, (tile, size), 1)
    turned = jnp.logical_or(place[0] == DOWN_PLACE, place[0] == OUT_PLACE)

    def band(index):
        return pl.ds(pl.multiple_of(index * tile, tile), tile)

    def load(block, index, moment, grad, turn):
        values = MOMENTUM * moment.astype(F32) + scale[0] * grad.astype(F32)
        values = values.astype(BF16).astype(F32)
        trace[...] += jnp.sum(values * values, axis=0, keepdims=True)
        if turn:
            values = values.T
            current[block, :, pl.ds(index * CUT, CUT)] = values
            rounded[0, block, :, pl.ds(index * CUT, CUT)] = values.astype(BF16)
        else:
            current[block, pl.ds(index * CUT, CUT), :] = values
            rounded[0, block, pl.ds(index * CUT, CUT), :] = values.astype(BF16)

    moments = (moment_a, moment_b, moment_c)
    trace[...] = jnp.zeros_like(trace)

    def load_block(block, _):
        for index in range(cuts):
            rows = pl.ds(index * CUT, CUT)

            @pl.when(place[0] == UP_PLACE)
            def _():
                load(block, index, moments[index][block], experts[block, rows, :], False)

            @pl.when(place[0] == DOWN_PLACE)
            def _():
                load(block, index, moments[index][block], experts[block, rows, :], True)

            @pl.when(place[0] == IN_PLACE)
            def _():
                load(block, index, moments[index][block], inward[block, rows, :], False)

            @pl.when(place[0] == OUT_PLACE)
            def _():
                room = outward.shape[1] - index * CUT
                if room >= CUT:
                    grad = outward[block, rows, :].astype(F32)
                elif room > 0:
                    grad = outward[block, pl.ds(index * CUT, room), :].astype(F32)
                    grad = jnp.concatenate([grad, jnp.zeros((CUT - room, size), F32)], axis=0)
                else:
                    grad = jnp.zeros((CUT, size), F32)
                load(block, index, moments[index][block], grad, True)

        return 0

    lax.fori_loop(0, blocks, load_block, 0)
    total = jnp.sum(trace[...])
    factor = 1.0 / (jnp.sqrt(total + jnp.zeros((8, 128), F32)) + 1e-07)[0:1, 0:1]

    def sweep(step, gain):
        now = step % 2

        def make_gram(index, diagonal):
            total = jnp.zeros((tile, size), F32)
            for block in range(blocks):
                total = total + dot(
                    rounded[now, block, band(index), :], rounded[now, block], 1, 1
                )
            total = total * gain
            mask = column == row + index * tile
            gram[band(index), :] = total
            low[band(index), :] = jnp.where(mask, 0.0, total).astype(BF16)
            return diagonal + jnp.sum(jnp.where(mask, total, 0.0), axis=0, keepdims=True)

        diagonal = lax.fori_loop(0, tiles, make_gram, jnp.zeros((1, size), F32))

        def make_poly(index, _):
            mask = column == row + index * tile
            values = gram[band(index), :]
            own = jnp.sum(jnp.where(mask, values, 0.0), axis=1, keepdims=True)
            rest = jnp.where(mask, own * own, (own + diagonal) * values)
            total = COEF_B * values + COEF_C * (dot(low[band(index), :], low[...], 1, 0) + rest)
            poly[band(index), :] = jnp.where(mask, 0.0, total).astype(BF16)
            part = jnp.sum(jnp.where(mask, total, 0.0), axis=1, keepdims=True)
            slope[band(index), :] = jnp.broadcast_to(part + COEF_A, (tile, 128))
            return _

        lax.fori_loop(0, tiles, make_poly, 0)

        def advance(lap, _):
            block, index = lap // tiles, lap % tiles
            scaled = spread(slope[band(index), :], size) * current[block, band(index), :]
            values = scaled + dot(poly[band(index), :], rounded[now, block], 1, 0)
            current[block, band(index), :] = values
            rounded[1 - now, block, band(index), :] = values.astype(BF16)
            return _

        def advance_first(lap, _):
            block, index = lap // tiles, lap % tiles
            scaled = spread(slope[band(index), :], size) * current[block, band(index), :]
            product = dot(poly[band(index), :], rounded[now, block], 1, 0)
            values = (scaled + product) * factor
            current[block, band(index), :] = values
            rounded[1 - now, block, band(index), :] = values.astype(BF16)
            return _

        @pl.when(step == 0)
        def _():
            lax.fori_loop(0, blocks * tiles, advance_first, 0)

        @pl.when(step > 0)
        def _():
            lax.fori_loop(0, blocks * tiles, advance, 0)

        return jnp.ones_like(gain)

    lax.fori_loop(0, ORTHO_STEPS, sweep, factor * factor)

    def store(block, _):
        @pl.when(turned)
        def _():
            for index in range(cuts):
                cut = pl.ds(index * CUT, CUT)
                out[block, :, cut] = current[block, cut, :].T.astype(BF16)

        @pl.when(jnp.logical_not(turned))
        def _():
            for index in range(cuts):
                cut = pl.ds(index * CUT, CUT)
                out[block, cut, :] = current[block, cut, :].astype(BF16)

        return 0

    lax.fori_loop(0, blocks, store, 0)


def orthogonalize(scale, moments, experts, inward, outward):
    blocks, size, width = experts.shape
    vmem = pl.BlockSpec(memory_space=pltpu.VMEM)
    smem = pl.BlockSpec(memory_space=pltpu.SMEM)
    place = lax.axis_index("mat").astype(jnp.int32).reshape(1)
    return pl.pallas_call(
        ortho_kernel,
        out_shape=jax.ShapeDtypeStruct(experts.shape, BF16),
        in_specs=[smem, smem] + [vmem] * 6,
        out_specs=vmem,
        scratch_shapes=[
            pltpu.VMEM((blocks, size, width), F32),
            pltpu.VMEM((2, blocks, size, width), BF16),
            pltpu.VMEM((size, size), F32),
            pltpu.VMEM((size, size), BF16),
            pltpu.VMEM((size, size), BF16),
            pltpu.VMEM((size, 128), F32),
            pltpu.VMEM((1, size), F32),
        ],
        compiler_params=pltpu.CompilerParams(vmem_limit_bytes=56 * 1024 * 1024),
        name="orthogonalize",
    )(place, scale.reshape(1), *moments, experts, inward, outward)


def adamw_update(weight, mean, square, grad, rate, decay):
    mean = BETA_ONE * mean + (1.0 - BETA_ONE) * grad
    square = BETA_TWO * square + (1.0 - BETA_TWO) * grad * grad
    ratio = (
        mean
        / (1.0 - BETA_ONE**STEP_COUNT)
        / (jnp.sqrt(square / (1.0 - BETA_TWO**STEP_COUNT)) + ADAM_EPS)
    )
    return (weight * (1.0 - rate * decay) - rate * ratio, mean, square)


def table_kernel(scale, grad, weight, mean, square, _ahead, new_weight, new_mean, new_square):
    part = weight.shape[0]
    turned = grad[...].T[:part] * scale[0]
    results = adamw_update(weight[...], mean[...], square[...], turned, 0.05, 0.1)
    new_weight[...], new_mean[...], new_square[...] = results


def update_table(scale, grad, weight, mean, square, ahead):
    part, entries = weight.shape
    flat = pl.BlockSpec((part, VOCAB_TILE), lambda i: (0, i))
    return pl.pallas_call(
        table_kernel,
        grid=(-(-entries // VOCAB_TILE),),
        in_specs=[
            pl.BlockSpec(memory_space=pltpu.SMEM),
            pl.BlockSpec((VOCAB_TILE, 256), lambda i: (i, 0)),
            flat,
            flat,
            flat,
            pl.BlockSpec(memory_space=pl.ANY),
        ],
        out_specs=[flat] * 3,
        out_shape=[jax.ShapeDtypeStruct(weight.shape, F32)] * 3,
        compiler_params=kernel_params(),
        cost_estimate=pl.CostEstimate(
            flops=20 * entries * 256,
            bytes_accessed=7 * entries * 256 * 4,
            transcendentals=2 * entries * 256,
        ),
        name="update_table",
    )(scale.reshape(1), grad, weight, mean, square, ahead)


def local(
    token_ids,
    expert_route,
    doc_lengths,
    loss_slots,
    loss_weight,
    target_ids,
    embedding,
    embedding_mom,
    embedding_sq,
    in_project,
    in_project_mom,
    out_project,
    out_project_mom,
    expert_up,
    expert_up_mom,
    expert_down,
    expert_down_mom,
    x_project,
    x_project_mom,
    x_project_sq,
    step_project,
    step_project_mom,
    step_project_sq,
    router_weight,
    router_mom,
    router_sq,
    channel_param,
    channel_mom,
    channel_sq,
    norm_gains,
    gains_mom,
    gains_sq,
):
    micros = token_ids.shape[0]
    mats = lax.axis_size("mat")
    seq_count = lax.axis_size("seq")
    tokens = expert_route.shape[2]
    vocab_part, part = embedding.shape
    ids = exchange([token_ids.reshape(-1, 128)], [True], 12, ("mat",))[0]
    ids = ids.reshape(mats, micros, seq_count, tokens)
    ids = ids.transpose(2, 0, 1, 3).reshape(-1) - lax.axis_index("seq") * vocab_part
    parts = [x_project, step_project, router_weight, channel_param, norm_gains]
    found, small = lookup(ids, embedding, pack_small(parts), 10)
    found, w_table, w_out, w_up, w_down = lax.optimization_barrier(
        (
            found,
            embedding.astype(BF16),
            out_project.astype(BF16),
            expert_up.astype(BF16),
            expert_down.astype(BF16),
        )
    )
    small = unpack_small(small, parts)
    weights = (
        lax.all_gather(w_table, "mat", axis=1, tiled=True),
        lax.all_gather(in_project.astype(BF16), "mat", axis=1, tiled=True),
        lax.all_gather(w_out, "mat", axis=0, tiled=True),
        lax.all_gather(w_up, "mat", axis=2, tiled=True),
        lax.all_gather(w_down, "mat", axis=1, tiled=True),
        small[0].reshape(-1, small[0].shape[2]),
        columns(small[1]),
        small[2].reshape(-1, small[2].shape[2]),
        columns(small[3]),
        columns(small[4]),
    )
    half = micros * tokens // 2
    tails = found[:, 2 * half :].reshape(mats, half, 2, part - 128).transpose(0, 2, 1, 3)
    heads = found[:, : 2 * half].reshape(mats, 2, half, 128)
    embedded = jnp.concatenate([heads, tails], axis=3).transpose(1, 2, 0, 3)
    embedded = embedded.reshape(micros * tokens, mats * part)
    loss_all = micros * lax.axis_size("mat") * loss_weight.shape[2]
    moments = jnp.stack(
        [
            expert_up_mom[0],
            in_project_mom,
            expert_down_mom[0],
            jnp.pad(out_project_mom, ((0, D - out_project_mom.shape[0]), (0, 0))),
        ]
    ).astype(BF16)
    grads, moved, x0_grad, loss_part, count_part, rows_here = step_grads(
        weights,
        jnp.split(moments, 3, axis=1),
        embedded,
        expert_route[:, 0, :, 0],
        doc_lengths[:, 0],
        loss_slots[:, 0],
        loss_weight[:, 0],
        target_ids[:, 0],
        loss_all,
    )
    row_loss = rows_here[:, None, :]
    s_table, s_in, s_out, s_up, s_down, g_x, g_step, g_route, g_chan, g_gain = grads
    pieces = (
        g_x.reshape(mats, -1),
        g_step.reshape(g_step.shape[0], mats, -1).transpose(1, 0, 2).reshape(mats, -1),
        g_route.reshape(mats, -1),
        g_chan.reshape(g_chan.shape[0], mats, -1).transpose(1, 0, 2).reshape(mats, -1),
        g_gain.reshape(g_gain.shape[0], mats, -1).transpose(1, 0, 2).reshape(mats, -1),
    )
    packed = jnp.concatenate(pieces, axis=1)
    unit = seq_count * 2048
    packed = jnp.pad(packed, ((0, 0), (0, -packed.shape[1] % unit)))
    packed = packed.astype(BF16).reshape(mats, -1, 128)
    x0_parts = x0_grad.reshape(2, -1, mats, part).transpose(2, 0, 1, 3)
    x0_heads = x0_parts[..., :128].reshape(mats, -1, 128)
    x0_tails = jnp.concatenate([x0_parts[:, 0, :, 128:], x0_parts[:, 1, :, 128:]], axis=2)
    x0_rows = 3 * micros * tokens // 2
    mixed = lax.all_to_all(
        jnp.concatenate([x0_heads, x0_tails, packed], axis=1),
        "mat",
        split_axis=0,
        concat_axis=0,
        tiled=True,
    )
    packed = jnp.sum(mixed[:, x0_rows:].astype(F32), axis=0).astype(BF16)
    g_table, table_squares, whole_experts = scatter_rows(
        ids.reshape(-1, 128),
        mixed[:, :x0_rows],
        s_table,
        vocab_part,
        13,
        [s_up[0], s_down[0]],
    )
    s_in, s_out, packed = exchange(
        [
            s_in.reshape(seq_count, -1, D),
            s_out.reshape(seq_count, -1, D),
            packed.reshape(seq_count, -1, 128),
        ],
        [False, False, False],
        14,
        ahead=[g_table],
    )
    s_in = jnp.sum(s_in.astype(F32), axis=0)
    s_out = jnp.sum(s_out.astype(F32), axis=0)
    packed = jnp.sum(packed.astype(F32), axis=0)
    s_up = s_up.astype(F32)
    s_down = s_down.astype(F32)
    squares = sum(jnp.sum(g * g) for g in (s_up, s_down, s_in, s_out, packed))
    squares = squares + jnp.sum(table_squares[0])
    tallies = jnp.stack([squares, loss_part, count_part])
    tallies = jnp.broadcast_to(jnp.pad(tallies, (0, 5))[:, None], (8, 128))
    g_in, g_out, packed, totals, whole_in, whole_out = gather_seq(
        [s_in.astype(BF16), s_out.astype(BF16), packed, tallies],
        15,
        relays=[(0, IN_PLACE), (1, OUT_PLACE)],
    )
    g_in = g_in.reshape(-1, D).astype(F32)
    g_out = g_out.reshape(-1, D).astype(F32)
    totals = exchange([jnp.sum(totals, axis=0)], [True], 11, ("mat",))[0]
    totals = jnp.sum(totals[:, :, 0], axis=0)
    packed = packed.reshape(-1)
    shards, offset = [], 0
    for piece, like in zip(
        pieces, (x_project, step_project, router_weight, channel_param, norm_gains)
    ):
        shards.append(packed[offset : offset + piece.shape[1]].reshape(like.shape))
        offset += piece.shape[1]
    squares, loss_total, loss_count = totals[0], totals[1], totals[2]
    grad_norm = jnp.sqrt(squares)
    scale = jnp.minimum(1.0, CLIP_NORM / (grad_norm + 1e-06))
    mom_in = MOMENTUM * in_project_mom + g_in * scale
    mom_out = MOMENTUM * out_project_mom + g_out * scale
    mom_up = MOMENTUM * expert_up_mom + s_up * scale
    mom_down = MOMENTUM * expert_down_mom + s_down * scale
    ortho = orthogonalize(
        scale,
        moved,
        whole_experts,
        whole_in.reshape(mats, D, -1),
        whole_out.reshape(mats, -1, D),
    )
    table_new = update_table(
        scale, g_table, embedding.T, embedding_mom.T, embedding_sq.T, ortho
    )
    table_new = [values.T for values in table_new]
    ortho = lax.all_to_all(ortho, "mat", split_axis=0, concat_axis=0, tiled=True).astype(F32)
    shrink = 1.0 - LR_MUON * DECAY_MUON
    new_up = expert_up * shrink - LR_MUON * 0.2 * math.sqrt(max(D, FF)) * ortho[UP_PLACE][None]
    new_in = in_project * shrink - LR_MUON * 0.2 * math.sqrt(max(D, 2 * DI)) * ortho[IN_PLACE]
    new_down = (
        expert_down * shrink - LR_MUON * 0.2 * math.sqrt(max(D, FF)) * ortho[DOWN_PLACE][None]
    )
    new_out = (
        out_project * shrink
        - LR_MUON * 0.2 * math.sqrt(max(D, DI)) * ortho[OUT_PLACE, : out_project.shape[0]]
    )
    x_new = adamw_update(x_project, x_project_mom, x_project_sq, shards[0] * scale, 0.06, 0.1)
    step_new = adamw_update(
        step_project, step_project_mom, step_project_sq, shards[1] * scale, 0.06, 0.1
    )
    route_new = adamw_update(router_weight, router_mom, router_sq, shards[2] * scale, 0.06, 0.1)
    chan_new = adamw_update(channel_param, channel_mom, channel_sq, shards[3] * scale, 1.0, 0.0)
    gains_new = adamw_update(norm_gains, gains_mom, gains_sq, shards[4] * scale, 0.4, 0.0)
    return (
        loss_total,
        loss_count,
        grad_norm,
        row_loss,
        *table_new,
        new_in,
        mom_in,
        new_out,
        mom_out,
        new_up,
        mom_up,
        new_down,
        mom_down,
        *x_new,
        *step_new,
        *route_new,
        *chan_new,
        *gains_new,
    )


def solution(mesh):
    in_specs = (
        P(None, "mat", None),
        P(None, "mat", "seq", None),
        P(None, "mat", None),
        P(None, "mat", "seq"),
        P(None, "mat", None),
        P(None, "mat", None),
        P("seq", "mat"),
        P("seq", "mat"),
        P("seq", "mat"),
        P(None, "mat"),
        P(None, "mat"),
        P("mat", None),
        P("mat", None),
        P("seq", None, "mat"),
        P("seq", None, "mat"),
        P("seq", "mat", None),
        P("seq", "mat", None),
        P("mat", None),
        P("mat", None),
        P("mat", None),
        P(None, "mat"),
        P(None, "mat"),
        P(None, "mat"),
        P("mat", None),
        P("mat", None),
        P("mat", None),
        P(None, "mat"),
        P(None, "mat"),
        P(None, "mat"),
        P(None, "mat"),
        P(None, "mat"),
        P(None, "mat"),
    )
    out_specs = (
        P(),
        P(),
        P(),
        P(None, "mat", "seq"),
        P("seq", "mat"),
        P("seq", "mat"),
        P("seq", "mat"),
        P(None, "mat"),
        P(None, "mat"),
        P("mat", None),
        P("mat", None),
        P("seq", None, "mat"),
        P("seq", None, "mat"),
        P("seq", "mat", None),
        P("seq", "mat", None),
        P("mat", None),
        P("mat", None),
        P("mat", None),
        P(None, "mat"),
        P(None, "mat"),
        P(None, "mat"),
        P("mat", None),
        P("mat", None),
        P("mat", None),
        P(None, "mat"),
        P(None, "mat"),
        P(None, "mat"),
        P(None, "mat"),
        P(None, "mat"),
        P(None, "mat"),
    )
    return jax.shard_map(local, mesh=mesh, in_specs=in_specs, out_specs=out_specs, check_vma=False)
```

```python
import functools
import math

import jax
import jax.numpy as jnp
from jax import lax
from jax.experimental import pallas as pl
from jax.experimental.pallas import tpu as pltpu
from jax.sharding import PartitionSpec as P

D = 768
DI = 1536
FF = 3072
VOCAB_REAL = 50257
CONV = 4
ORTHO_STEPS = 5
STEP_COUNT = 10
STATES = 16
RANK = 48

CLIP_NORM = 0.004
COEF_A = 3.4445
COEF_B = -4.775
COEF_C = 2.0315
MOMENTUM = 0.95
LR_MUON = 0.2
DECAY_MUON = 0.01
BETA_ONE = 0.9
BETA_TWO = 0.95
ADAM_EPS = 1e-08
F32 = jnp.float32
BF16 = jnp.bfloat16
LANES = 512
UNROLL = 8
TILE = 256
VOCAB_TILE = 640
UP_PLACE, IN_PLACE, DOWN_PLACE, OUT_PLACE = 0, 1, 2, 3
TOTAL_ROWS = 8
PAD = 8
HIDDEN = 512
MESH = pl.DeviceIdType.MESH


def dot(left, right, left_dim, right_dim, **kw):
    return lax.dot_general(
        left, right, (((left_dim,), (right_dim,)), ((), ())), preferred_element_type=F32, **kw
    )


def spread(values, width):
    return jnp.concatenate([values] * (width // 128), axis=1)


def same_document(lengths, place, micro, tokens, width):
    position = place[0] * tokens + lax.broadcasted_iota(jnp.int32, (tokens, 128), 0)
    bounds, bound = [], 0
    for index in range(lengths.shape[1] - 1):
        bound = bound + lengths[micro, index]
        bounds.append(bound)
    masks = []
    for tap in range(CONV):
        source = position - (CONV - 1) + tap
        inside = source >= 0
        for bound in bounds:
            inside = jnp.logical_and(inside, (source >= bound) == (position >= bound))
        masks.append(spread(jnp.where(inside, 1.0, 0.0), width))
    return masks


def fill_padded(padded, edge, raw):
    padded[PAD - (CONV - 1) : PAD, :] = edge[0]
    padded[PAD:, :] = raw[0]


def conv_kernel(lengths, place, raw, edge, channel, w_x, conv_out, act_out, projected, padded):
    micro, group = pl.program_id(0), pl.program_id(1)
    tokens, width = raw.shape[1], raw.shape[2]
    fill_padded(padded, edge, raw)
    masks = same_document(lengths, place, micro, tokens, width)
    conv = jnp.broadcast_to(channel[CONV : CONV + 1, :], (tokens, width))
    for tap in range(CONV):
        shifted = padded[pl.ds(PAD - (CONV - 1) + tap, tokens), :]
        conv = conv + channel[tap : tap + 1, :] * shifted * masks[tap]
    act = conv * lax.logistic(conv)
    conv_out[0] = conv
    act_out[0] = act

    @pl.when(group == 0)
    def _():
        projected[...] = jnp.zeros_like(projected)

    projected[0] += dot(act.astype(BF16), w_x[...], 1, 0)


def conv_back_kernel(
    lengths, place, raw, edge, channel, w_x, conv, act, act_grad, y_grad, projected_grad,
    raw_out, head_out, x_out, rows_out, padded, total,
):
    micro = pl.program_id(1)
    tokens, width = raw.shape[1], raw.shape[2]
    fill_padded(padded, edge, raw)
    masks = same_document(lengths, place, micro, tokens, width)
    grad = act_grad[0] + y_grad[0] * channel[CONV + 2 : CONV + 3, :]
    grad = grad + dot(projected_grad[0], w_x[...], 1, 1)
    values = conv[0]
    sig = lax.logistic(values)
    grad = grad * (sig * (1.0 + values * (1.0 - sig)))

    @pl.when(micro == 0)
    def _():
        x_out[...] = jnp.zeros_like(x_out)
        rows_out[...] = jnp.zeros_like(rows_out)

    x_out[...] += dot(act[0].astype(BF16), projected_grad[0], 0, 0)
    total[...] = jnp.zeros_like(total)
    for tap in range(CONV):
        span = pl.ds(PAD - (CONV - 1) + tap, tokens)
        kept = grad * masks[tap]
        rows_out[tap : tap + 1, :] += jnp.sum(kept * padded[span, :], axis=0, keepdims=True)
        total[span, :] += channel[tap : tap + 1, :] * kept
    rows_out[CONV : CONV + 1, :] += jnp.sum(grad, axis=0, keepdims=True)
    raw_out[0] = total[PAD:, :]
    head_out[0] = total[PAD - (CONV - 1) : PAD, :]


def end_kernel(keep, projected, w_step, channel, act, inject, pre_out, dt_out, out, totals):
    micro = pl.program_id(1)
    micros = pl.num_programs(1)
    tokens, width = act.shape[1], act.shape[2]
    rates = -jnp.exp(channel[CONV + 3 :, :])
    pre = dot(projected[0][:, :RANK].astype(BF16), w_step[...], 1, 0)
    pre = pre + channel[CONV + 1 : CONV + 2, :]
    step_size = jnp.maximum(pre, 0.0) + jnp.log1p(jnp.exp(-jnp.abs(pre)))
    pre_out[0] = pre
    dt_out[0] = step_size

    def block(step, carry):
        state, alive = carry
        for inner in range(UNROLL):
            t = step * UNROLL + inner
            d = dt_out[0, pl.ds(t, 1), :]
            w = d * act[0, pl.ds(t, 1), :]
            k = keep[micro, t]
            state = jnp.exp(rates * d) * k * state + spread(inject[0, t], width) * w
            alive = alive * k
        return state, alive

    state, alive = lax.fori_loop(
        0, tokens // UNROLL, block, (jnp.zeros((STATES, width), F32), jnp.float32(1.0))
    )
    out[...] = state.astype(BF16)

    @pl.when(micro == 0)
    def _():
        totals[...] = jnp.zeros_like(totals)

    totals[pl.ds(micro, 1), :] = jnp.sum(step_size, axis=0, keepdims=True)
    totals[pl.ds(micros + micro, 1), :] = jnp.zeros((1, width), F32) + alive


def forward_kernel(
    place, keep, dt, act, inject, readout, rate, ends, totals, y_out, h_out, start_out
):
    micro = pl.program_id(0)
    micros = pl.num_programs(0)
    tokens, width = dt.shape[1], dt.shape[2]
    rates = rate[...]
    me = place[0]

    def fold(source, state):
        total = totals[source, pl.ds(micro, 1), :]
        alive = totals[source, pl.ds(micros + micro, 1), :]
        return jnp.exp(rates * total) * alive * state + ends[source].astype(F32)

    state = lax.fori_loop(0, me, fold, jnp.zeros((STATES, width), F32))
    start_out[0] = state

    def block(step, state):
        for inner in range(UNROLL):
            t = step * UNROLL + inner
            d = dt[0, pl.ds(t, 1), :]
            w = d * act[0, pl.ds(t, 1), :]
            state = jnp.exp(rates * d) * keep[micro, t] * state + spread(inject[0, t], width) * w
            h_out[0, t] = state
            y_out[0, pl.ds(t, 1), :] = jnp.sum(
                spread(readout[0, t], width) * state, axis=0, keepdims=True
            )
        return state

    lax.fori_loop(0, tokens // UNROLL, block, state)


def start_kernel(keep, dt, dy, readout, rate, out):
    micro = pl.program_id(0)
    tokens, width = dt.shape[1], dt.shape[2]
    rates = rate[...]

    def block(step, state):
        for inner in range(UNROLL):
            t = tokens - 1 - (step * UNROLL + inner)
            d = dt[0, pl.ds(t, 1), :]
            state = state + spread(readout[0, t], width) * dy[0, pl.ds(t, 1), :]
            state = jnp.exp(rates * d) * keep[micro, t] * state
        return state

    state = lax.fori_loop(0, tokens // UNROLL, block, jnp.zeros((STATES, width), F32))
    out[...] = state.astype(BF16)


def backward_kernel(
    place,
    keep,
    dt,
    act,
    dy,
    inject,
    readout,
    rate,
    totals,
    starts,
    start,
    hs,
    ddt_out,
    da_out,
    db_out,
    dc_out,
    drate_out,
):
    micro = pl.program_id(0)
    micros = pl.num_programs(0)
    group = pl.program_id(1)
    tokens, width = dt.shape[1], dt.shape[2]
    rates = rate[...]
    me = place[0]
    count = totals.shape[0]

    def fold(lap, state):
        source = count - 1 - lap
        total = totals[source, pl.ds(micro, 1), :]
        alive = totals[source, pl.ds(micros + micro, 1), :]
        return jnp.exp(rates * total) * alive * state + starts[source].astype(F32)

    grad = lax.fori_loop(0, count - 1 - me, fold, jnp.zeros((STATES, width), F32))

    @pl.when(group == 0)
    def _():
        db_out[...] = jnp.zeros_like(db_out)
        dc_out[...] = jnp.zeros_like(dc_out)

    def gather_lanes(values):
        total = values[:, 0:128]
        for tile in range(1, width // 128):
            total = total + values[:, tile * 128 : (tile + 1) * 128]
        return total

    def one(t, before, carry):
        grad, drate, state = carry
        d = dt[0, pl.ds(t, 1), :]
        x = act[0, pl.ds(t, 1), :]
        g_y = dy[0, pl.ds(t, 1), :]
        w = d * x
        grad = grad + spread(readout[0, t], width) * g_y
        db_out[0, t] += gather_lanes(grad * w)
        dc_out[0, t] += gather_lanes(state * g_y)
        dw = jnp.sum(grad * spread(inject[0, t], width), axis=0, keepdims=True)
        grad = jnp.exp(rates * d) * keep[micro, t] * grad
        effect = grad * before
        drate = drate + effect * d
        ddt_out[0, pl.ds(t, 1), :] = (
            jnp.sum(effect * rates, axis=0, keepdims=True) + dw * x
        )
        da_out[0, pl.ds(t, 1), :] = dw * d
        return grad, drate, before

    def block(step, carry):
        for inner in range(UNROLL):
            t = tokens - 1 - (step * UNROLL + inner)
            carry = one(t, hs[0, t - 1], carry)
        return carry

    carry = (grad, jnp.zeros((STATES, width), F32), hs[0, tokens - 1])
    carry = lax.fori_loop(0, tokens // UNROLL - 1, block, carry)
    for t in range(UNROLL - 1, -1, -1):
        carry = one(t, hs[0, t - 1] if t else start[0], carry)
    drate_out[0] = carry[1]


def specs(tokens, seq_count):
    rows = pl.BlockSpec((1, tokens, LANES), lambda m, g: (m, 0, g))
    wide = pl.BlockSpec((1, tokens, STATES, 128), lambda m, g: (m, 0, 0, 0))
    rate = pl.BlockSpec((STATES, LANES), lambda m, g: (0, g))
    state = pl.BlockSpec((1, STATES, LANES), lambda m, g: (m, 0, g))
    edge = pl.BlockSpec((STATES, LANES), lambda m, g: (m, g))
    edges = pl.BlockSpec((seq_count, STATES, LANES), lambda m, g: (0, m, g))
    totals = pl.BlockSpec((seq_count, TOTAL_ROWS, LANES), lambda m, g: (0, 0, g))
    every = pl.BlockSpec((1, tokens, STATES, LANES), lambda m, g: (m, 0, 0, g))
    scalars = pl.BlockSpec(memory_space=pltpu.SMEM)
    return rows, wide, rate, state, edge, edges, totals, every, scalars


def kernel_params():
    return pltpu.CompilerParams(vmem_limit_bytes=48 * 1024 * 1024)


def convolve(lengths, place, xz, edge, channel, w_x):
    micros, tokens, inner = xz.shape[0], xz.shape[1], xz.shape[2] // 2
    scalars = pl.BlockSpec(memory_space=pltpu.SMEM)
    rows = pl.BlockSpec((1, tokens, LANES), lambda m, g: (m, 0, g))
    shape = jax.ShapeDtypeStruct((micros, tokens, inner), F32)
    columns_x = w_x.shape[1]
    return pl.pallas_call(
        conv_kernel,
        grid=(micros, inner // LANES),
        in_specs=[
            scalars,
            scalars,
            rows,
            pl.BlockSpec((1, CONV - 1, LANES), lambda m, g: (m, 0, g)),
            pl.BlockSpec((channel.shape[0], LANES), lambda m, g: (0, g)),
            pl.BlockSpec((LANES, columns_x), lambda m, g: (g, 0)),
        ],
        out_specs=[rows, rows, pl.BlockSpec((1, tokens, columns_x), lambda m, g: (m, 0, 0))],
        out_shape=[shape, shape, jax.ShapeDtypeStruct((micros, tokens, columns_x), F32)],
        scratch_shapes=[pltpu.VMEM((PAD + tokens, LANES), F32)],
        compiler_params=kernel_params(),
        name="mixer_conv",
    )(lengths, place, xz, edge, channel, w_x)


def convolve_back(
    lengths, place, xz, edge, channel, w_x, conv, act, act_grad, y_grad, projected_grad
):
    micros, tokens, inner = conv.shape
    scalars = pl.BlockSpec(memory_space=pltpu.SMEM)
    rows = pl.BlockSpec((1, tokens, LANES), lambda g, m: (m, 0, g))
    ends = pl.BlockSpec((1, CONV - 1, LANES), lambda g, m: (m, 0, g))
    columns_x = w_x.shape[1]
    weight = pl.BlockSpec((LANES, columns_x), lambda g, m: (g, 0))
    return pl.pallas_call(
        conv_back_kernel,
        grid=(inner // LANES, micros),
        in_specs=[
            scalars,
            scalars,
            rows,
            ends,
            pl.BlockSpec((channel.shape[0], LANES), lambda g, m: (0, g)),
            weight,
            rows,
            rows,
            rows,
            rows,
            pl.BlockSpec((1, tokens, columns_x), lambda g, m: (m, 0, 0)),
        ],
        out_specs=[rows, ends, weight, pl.BlockSpec((8, LANES), lambda g, m: (0, g))],
        out_shape=[
            jax.ShapeDtypeStruct((micros, tokens, inner), F32),
            jax.ShapeDtypeStruct((micros, CONV - 1, inner), F32),
            jax.ShapeDtypeStruct((inner, columns_x), F32),
            jax.ShapeDtypeStruct((8, inner), F32),
        ],
        scratch_shapes=[pltpu.VMEM((PAD + tokens, LANES), F32)] * 2,
        compiler_params=kernel_params(),
        name="mixer_conv_back",
    )(lengths, place, xz, edge, channel, w_x, conv, act, act_grad, y_grad, projected_grad)


def scan_end(keep, projected, w_step, channel, act, inject):
    micros, tokens, inner = act.shape
    rows = pl.BlockSpec((1, tokens, LANES), lambda g, m: (m, 0, g))
    columns_x = projected.shape[2]
    shape = jax.ShapeDtypeStruct((micros, tokens, inner), F32)
    return pl.pallas_call(
        end_kernel,
        grid=(inner // LANES, micros),
        in_specs=[
            pl.BlockSpec(memory_space=pltpu.SMEM),
            pl.BlockSpec((1, tokens, columns_x), lambda g, m: (m, 0, 0)),
            pl.BlockSpec((RANK, LANES), lambda g, m: (0, g)),
            pl.BlockSpec((channel.shape[0], LANES), lambda g, m: (0, g)),
            rows,
            pl.BlockSpec((1, tokens, STATES, 128), lambda g, m: (m, 0, 0, 0)),
        ],
        out_specs=[
            rows,
            rows,
            pl.BlockSpec((STATES, LANES), lambda g, m: (m, g)),
            pl.BlockSpec((TOTAL_ROWS, LANES), lambda g, m: (0, g)),
        ],
        out_shape=[
            shape,
            shape,
            jax.ShapeDtypeStruct((micros * STATES, inner), BF16),
            jax.ShapeDtypeStruct((TOTAL_ROWS, inner), F32),
        ],
        compiler_params=kernel_params(),
        name="scan_end",
    )(keep, projected, w_step, channel, act, inject)


def scan_forward(place, keep, dt, act, inject, readout, rate, ends_all, totals_all):
    micros, tokens, inner = dt.shape
    rows, wide, rated, state, _, edges, totals, every, scalars = specs(tokens, ends_all.shape[0])
    return pl.pallas_call(
        forward_kernel,
        grid=(micros, inner // LANES),
        in_specs=[scalars, scalars, rows, rows, wide, wide, rated, edges, totals],
        out_specs=[rows, every, state],
        out_shape=[
            jax.ShapeDtypeStruct((micros, tokens, inner), F32),
            jax.ShapeDtypeStruct((micros, tokens, STATES, inner), F32),
            jax.ShapeDtypeStruct((micros, STATES, inner), F32),
        ],
        compiler_params=kernel_params(),
        name="scan_forward",
    )(place, keep, dt, act, inject, readout, rate, ends_all, totals_all)


def scan_start(keep, dt, dy, readout, rate, ahead):
    micros, tokens, inner = dt.shape
    rows, wide, rated, _, edge, _, _, _, scalars = specs(tokens, 1)
    unread = pl.BlockSpec(memory_space=pl.ANY)

    def body(keep, dt, dy, readout, rate, *rest):
        start_kernel(keep, dt, dy, readout, rate, rest[-1])

    return pl.pallas_call(
        body,
        grid=(micros, inner // LANES),
        in_specs=[scalars, rows, rows, wide, rated] + [unread] * len(ahead),
        out_specs=edge,
        out_shape=jax.ShapeDtypeStruct((micros * STATES, inner), BF16),
        compiler_params=kernel_params(),
        name="scan_start",
    )(keep, dt, dy, readout, rate, *ahead)


def scan_backward(
    place, keep, dt, act, dy, inject, readout, rate, totals_all, starts_all, start, hs, ahead
):
    micros, tokens, inner = dt.shape
    rows, wide, rated, state, _, edges, totals, every, scalars = specs(tokens, totals_all.shape[0])
    unread = pl.BlockSpec(memory_space=pl.ANY)

    def body(*refs):
        backward_kernel(*refs[:12], *refs[12 + len(ahead) :])

    return pl.pallas_call(
        body,
        grid=(micros, inner // LANES),
        in_specs=[
            scalars, scalars, rows, rows, rows, wide, wide, rated, totals, edges, state, every,
        ]
        + [unread] * len(ahead),
        out_specs=[rows, rows, wide, wide, state],
        out_shape=[
            jax.ShapeDtypeStruct((micros, tokens, inner), F32),
            jax.ShapeDtypeStruct((micros, tokens, inner), F32),
            jax.ShapeDtypeStruct((micros, tokens, STATES, 128), F32),
            jax.ShapeDtypeStruct((micros, tokens, STATES, 128), F32),
            jax.ShapeDtypeStruct((micros, STATES, inner), F32),
        ],
        compiler_params=kernel_params(),
        name="scan_backward",
    )(place, keep, dt, act, dy, inject, readout, rate, totals_all, starts_all, start, hs, *ahead)


def expert_kernel(taken, w_up, w_down, hidden_out, slope_out, out, total):
    step = pl.program_id(1)
    values = dot(taken[0], w_up[0], 1, 0)
    below = 0.5 + 0.5 * lax.erf(values * math.sqrt(0.5))
    hidden = (values * below).astype(BF16)
    density = jnp.exp(-0.5 * values * values) * (1.0 / math.sqrt(2.0 * math.pi))
    hidden_out[0] = hidden
    slope_out[0] = below + values * density

    @pl.when(step == 0)
    def _():
        total[...] = jnp.zeros_like(total)

    total[...] += dot(hidden, w_down[0], 1, 0)

    @pl.when(step == pl.num_programs(1) - 1)
    def _():
        out[0] = total[...].astype(BF16)


def expert_back_kernel(
    taken, grad, w_up, w_down, hidden, slope, up_out, down_out, taken_out, total
):
    step = pl.program_id(1)
    pre_grad = (dot(grad[0], w_down[0], 1, 1) * slope[0]).astype(BF16)
    down_out[0] = dot(hidden[0], grad[0], 0, 0).astype(BF16)
    up_out[0] = dot(taken[0], pre_grad, 0, 0).astype(BF16)

    @pl.when(step == 0)
    def _():
        total[...] = jnp.zeros_like(total)

    total[...] += dot(pre_grad, w_up[0], 1, 1)

    @pl.when(step == pl.num_programs(1) - 1)
    def _():
        taken_out[0] = total[...].astype(BF16)


def expert_specs(rows, width):
    whole = pl.BlockSpec((1, rows, width), lambda e, j: (e, 0, 0))
    up = pl.BlockSpec((1, width, HIDDEN), lambda e, j: (e, 0, j))
    down = pl.BlockSpec((1, HIDDEN, width), lambda e, j: (e, j, 0))
    units = pl.BlockSpec((1, rows, HIDDEN), lambda e, j: (e, 0, j))
    return whole, up, down, units


def run_experts(taken, w_up, w_down):
    experts, rows, width = taken.shape
    hidden = w_up.shape[2]
    whole, up, down, units = expert_specs(rows, width)
    return pl.pallas_call(
        expert_kernel,
        grid=(experts, hidden // HIDDEN),
        in_specs=[whole, up, down],
        out_specs=[units, units, whole],
        out_shape=[
            jax.ShapeDtypeStruct((experts, rows, hidden), BF16),
            jax.ShapeDtypeStruct((experts, rows, hidden), F32),
            jax.ShapeDtypeStruct(taken.shape, BF16),
        ],
        scratch_shapes=[pltpu.VMEM((rows, width), F32)],
        compiler_params=kernel_params(),
        name="experts",
    )(taken, w_up, w_down)


def run_experts_back(taken, grad, w_up, w_down, hidden, slope):
    experts, rows, width = taken.shape
    whole, up, down, units = expert_specs(rows, width)
    return pl.pallas_call(
        expert_back_kernel,
        grid=(experts, hidden.shape[2] // HIDDEN),
        in_specs=[whole, whole, up, down, units, units],
        out_specs=[up, down, whole],
        out_shape=[
            jax.ShapeDtypeStruct(w_up.shape, BF16),
            jax.ShapeDtypeStruct(w_down.shape, BF16),
            jax.ShapeDtypeStruct(taken.shape, BF16),
        ],
        scratch_shapes=[pltpu.VMEM((rows, width), F32)],
        compiler_params=kernel_params(),
        name="experts_back",
    )(taken, grad, w_up, w_down, hidden, slope)


def head_columns(width):
    return lax.broadcasted_iota(jnp.int32, (1, width), 1) + pl.program_id(0) * width


def head_kernel(limits, rows, table, targets, logits_out, stats, largest, summed, wanted):
    step = pl.program_id(0)
    tile = table.shape[1]
    column = head_columns(tile)
    logits = dot(rows[...], table[...], 1, 0)
    logits = jnp.where(column < limits[1], logits, -1e30)
    logits_out[...] = logits
    named = targets[...] - limits[0]
    named = jnp.where(named < limits[1], named, -1)

    @pl.when(step == 0)
    def _():
        largest[...] = jnp.full_like(largest, -1e30)
        summed[...] = jnp.zeros_like(summed)
        wanted[...] = jnp.zeros_like(wanted)

    parts = [logits[:, first : first + 128] for first in range(0, tile, 128)]
    before = largest[...]
    top = functools.reduce(jnp.maximum, parts, before)
    total = summed[...] * jnp.exp(before - top)
    found = wanted[...]
    for index, part in enumerate(parts):
        total = total + jnp.exp(part - top)
        spot = column[:, index * 128 : (index + 1) * 128]
        found = found + jnp.where(spot == named, part, 0.0)
    largest[...], summed[...], wanted[...] = top, total, found

    @pl.when(step == pl.num_programs(0) - 1)
    def _():
        most = jnp.max(top, axis=1, keepdims=True)
        stats[...] = jnp.zeros_like(stats)
        stats[:, 0:1] = most
        stats[:, 1:2] = jnp.sum(total * jnp.exp(top - most), axis=1, keepdims=True)
        stats[:, 2:3] = jnp.sum(found, axis=1, keepdims=True)


def head_back_kernel(
    limits, rows, table, targets, scalars, logits, table_out, rows_out, total
):
    step = pl.program_id(0)
    column = head_columns(table.shape[1])
    inside = column < limits[1]
    probability = jnp.exp(logits[...] - scalars[:, 0:1])
    hit = jnp.where(column == targets[...] - limits[0], 1.0, 0.0)
    grad = scalars[:, 1:2] * (probability - hit)
    grad = jnp.where(inside, grad, 0.0).astype(BF16)

    @pl.when(step == 0)
    def _():
        total[...] = jnp.zeros_like(total)

    table_out[...] = dot(rows[...], grad, 1, 0).astype(BF16)

    @pl.when(step < pl.num_programs(0) - 1)
    def _():
        total[...] += dot(grad, table[...], 1, 1)

    @pl.when(step == pl.num_programs(0) - 1)
    def _():
        weight = jnp.where(inside, table[...].astype(F32), 0.0).astype(BF16)
        rows_out[...] = (total[...] + dot(grad, weight, 1, 1)).astype(BF16)


def head_specs(rows, table):
    count, width = rows.shape
    tile = 1280 if count <= 512 else 640
    whole = pl.BlockSpec((count, width), lambda j: (0, 0))
    part = pl.BlockSpec((width, tile), lambda j: (0, j))
    column = pl.BlockSpec((count, 1), lambda j: (0, 0))
    few = pl.BlockSpec((count, 8), lambda j: (0, 0))
    logits = pl.BlockSpec((count, tile), lambda j: (0, j))
    return whole, part, column, few, logits, (-(-table.shape[1] // tile),)


def head(limits, rows, table, targets):
    whole, part, column, few, logits, grid = head_specs(rows, table)
    return pl.pallas_call(
        head_kernel,
        grid=grid,
        in_specs=[pl.BlockSpec(memory_space=pltpu.SMEM), whole, part, column],
        out_specs=[logits, few],
        out_shape=[
            jax.ShapeDtypeStruct((rows.shape[0], table.shape[1]), F32),
            jax.ShapeDtypeStruct((rows.shape[0], 8), F32),
        ],
        scratch_shapes=[pltpu.VMEM((rows.shape[0], 128), F32)] * 3,
        compiler_params=kernel_params(),
        name="head",
    )(limits, rows, table, targets)


def head_back(limits, rows, table, targets, scalars, logits):
    whole, part, column, few, logit, grid = head_specs(rows, table)
    turned = pl.BlockSpec((rows.shape[1], rows.shape[0]), lambda j: (0, 0))
    return pl.pallas_call(
        head_back_kernel,
        grid=grid,
        in_specs=[
            pl.BlockSpec(memory_space=pltpu.SMEM), turned, part, column, few, logit,
        ],
        out_specs=[part, whole],
        out_shape=[
            jax.ShapeDtypeStruct(table.shape, BF16),
            jax.ShapeDtypeStruct(rows.shape, BF16),
        ],
        scratch_shapes=[pltpu.VMEM(rows.shape, F32)],
        compiler_params=kernel_params(),
        name="head_back",
    )(limits, rows.T, table, targets, scalars, logits)


def exchange_kernel(groups, gathers, ahead, *refs):
    arrays = len(groups)
    inputs, outputs = refs[:arrays], refs[arrays + ahead : 2 * arrays + ahead]
    sends, receives, own_sem = refs[2 * arrays + ahead :]

    def place_of(axes):
        if len(axes) == 1:
            return lax.axis_size(axes[0]), lax.axis_index(axes[0]), lambda peer: {axes[0]: peer}
        width = lax.axis_size(axes[1])
        return (
            lax.axis_size(axes[0]) * width,
            lax.axis_index(axes[0]) * width + lax.axis_index(axes[1]),
            lambda peer: {axes[0]: peer // width, axes[1]: peer % width},
        )

    def source(index, peer):
        return inputs[index] if gathers[index] else inputs[index].at[peer]

    def copy(index, device, peer, block):
        return pltpu.make_async_remote_copy(
            src_ref=source(index, peer),
            dst_ref=outputs[index].at[block],
            send_sem=sends.at[index, peer],
            recv_sem=receives.at[index, block],
            device_id=device(peer),
            device_id_type=MESH,
        )

    barrier = pltpu.get_barrier_semaphore()
    total = 0
    for axes in sorted(set(groups)):
        peers, me, device = place_of(axes)

        def greet(lap, _):
            pl.semaphore_signal(
                barrier, inc=1, device_id=device((me + lap) % peers), device_id_type=MESH
            )
            return _

        lax.fori_loop(1, peers, greet, 0)
        total += peers - 1
    own = []
    for index, axes in enumerate(groups):
        me = place_of(axes)[1]
        own.append(
            pltpu.make_async_copy(source(index, me), outputs[index].at[me], own_sem.at[index])
        )
        own[-1].start()
    pl.semaphore_wait(barrier, total)
    for index, axes in enumerate(groups):
        peers, me, device = place_of(axes)

        def begin(lap, _):
            copy(index, device, (me + lap) % peers, me).start()
            return _

        lax.fori_loop(1, peers, begin, 0)
    for index, axes in enumerate(groups):
        peers, me, device = place_of(axes)
        own[index].wait()

        def end(lap, _):
            before = (me + peers - lap) % peers
            copy(index, device, before, before).wait_recv()
            copy(index, device, (me + lap) % peers, me).wait_send()
            return _

        lax.fori_loop(1, peers, end, 0)


def exchange(values, gathers, identity, axes=("seq",), space=pltpu.VMEM, ahead=()):
    groups = [axes] * len(values)
    peers = [math.prod(lax.axis_size(axis) for axis in group) for group in groups]
    place = pl.BlockSpec(memory_space=space)
    unread = pl.BlockSpec(memory_space=pl.ANY)
    shapes = [
        jax.ShapeDtypeStruct(((count,) if gather else ()) + value.shape, value.dtype)
        for value, gather, count in zip(values, gathers, peers)
    ]
    arrays = len(values)
    return pl.pallas_call(
        functools.partial(exchange_kernel, tuple(groups), tuple(gathers), len(ahead)),
        out_shape=shapes,
        in_specs=[place] * arrays + [unread] * len(ahead),
        out_specs=[place] * arrays,
        scratch_shapes=[
            pltpu.SemaphoreType.DMA((arrays, max(peers))),
            pltpu.SemaphoreType.DMA((arrays, max(peers))),
            pltpu.SemaphoreType.DMA((arrays,)),
        ],
        compiler_params=pltpu.CompilerParams(collective_id=identity, has_side_effects=True),
        name="exchange",
    )(*values, *ahead)


def hold(values, ahead):
    unread = pl.BlockSpec(memory_space=pl.ANY)
    return pl.pallas_call(
        lambda *refs: None,
        out_shape=[jax.ShapeDtypeStruct(value.shape, value.dtype) for value in values],
        in_specs=[unread] * (len(values) + len(ahead)),
        out_specs=[unread] * len(values),
        input_output_aliases={index: index for index in range(len(values))},
        name="hold",
    )(*values, *ahead)


class Line:
    SEMAPHORES = 6

    def __init__(self, inputs, outputs, semaphores):
        self.inputs, self.outputs = inputs, outputs
        self.sends, self.receives = semaphores[0::2], semaphores[1::2]
        self.outers = lax.axis_size("seq") // 2
        me = lax.axis_index("seq")
        self.outer, self.inner = me // 2, me % 2
        self.later = self.outer + 1 < self.outers
        self.earlier = self.outer > 0

    def block(self, outer):
        return outer * 2 + self.inner

    def across(self, outer):
        return outer * 2 + 1 - self.inner

    def target(self, way):
        step = (2, -2, 1 - 2 * self.inner)[way]
        return {"seq": self.outer * 2 + self.inner + step}

    def pieces(self):
        for index, source in enumerate(self.inputs):
            for piece in range(source.shape[0]):
                yield index, piece

    def copy(self, way, index, outer, piece, place, first=False):
        source = self.outputs[index].at[place, piece]
        return pltpu.make_async_remote_copy(
            src_ref=self.inputs[index].at[piece] if first else source,
            dst_ref=self.outputs[index].at[place, piece],
            send_sem=self.sends[way].at[index, outer, piece],
            recv_sem=self.receives[way].at[index, outer, piece],
            device_id=self.target(way),
            device_id_type=MESH,
        )

    def ways(self):
        return ((0, self.later), (1, self.earlier))

    def greet(self, barrier):
        for way, exists in self.ways():

            @pl.when(exists)
            def _():
                pl.semaphore_signal(
                    barrier, inc=1, device_id=self.target(way), device_id_type=MESH
                )

        pl.semaphore_signal(barrier, inc=1, device_id=self.target(2), device_id_type=MESH)
        return 1 + self.later.astype(jnp.int32) + self.earlier.astype(jnp.int32)

    def begin(self):
        mine = self.block(self.outer)
        for index, piece in self.pieces():
            for way, exists in self.ways():

                @pl.when(exists)
                def _():
                    self.copy(way, index, self.outer, piece, mine, True).start()

            self.copy(2, index, self.outer, piece, mine, True).start()

    def forward(self, lap):
        for index, piece in self.pieces():
            for way, exists in self.ways():
                outer = self.outer + (-lap, lap)[way]
                place = self.block(outer)

                @pl.when(jnp.logical_and(outer >= 0, outer < self.outers))
                def _():
                    self.copy(way, index, outer, piece, place).wait_recv()

                    @pl.when(exists)
                    def _():
                        self.copy(way, index, outer, piece, place).start()

                    self.copy(2, index, outer, piece, place).start()

    def take(self, outer):
        for index, piece in self.pieces():
            self.copy(2, index, outer, piece, self.across(outer)).wait_recv()

    def each(self, lap, use, partners=None):
        for way in range(2):
            outer = self.outer + (-lap, lap)[way]

            @pl.when(jnp.logical_and(outer >= 0, outer < self.outers))
            def _():
                if partners is not True:
                    use(self.block(outer))
                if partners is not False:
                    self.take(outer)
                    use(self.across(outer))

    def end(self):
        def one(outer, _):
            for index, piece in self.pieces():
                place = self.block(outer)

                @pl.when(jnp.logical_and(self.later, outer <= self.outer))
                def _():
                    self.copy(0, index, outer, piece, place).wait_send()

                @pl.when(jnp.logical_and(self.earlier, outer >= self.outer))
                def _():
                    self.copy(1, index, outer, piece, place).wait_send()

                self.copy(2, index, outer, piece, place).wait_send()
            return 0

        lax.fori_loop(0, self.outers, one, 0)


def line_semaphores(values):
    shape = (len(values), lax.axis_size("seq") // 2, max(value.shape[0] for value in values))
    return [pltpu.SemaphoreType.DMA(shape)] * Line.SEMAPHORES


def gather_kernel(arrays, ahead, relays, *refs):
    inputs = refs[:arrays]
    outputs = refs[arrays + ahead : 2 * arrays + ahead]
    wholes = refs[2 * arrays + ahead : 2 * arrays + ahead + len(relays)]
    rest = refs[2 * arrays + ahead + len(relays) :]
    line = Line(inputs, outputs, rest[: Line.SEMAPHORES])
    own_sem, relay_sends, relay_receives, relay_own = rest[Line.SEMAPHORES :]
    mats, here = lax.axis_size("mat"), lax.axis_index("mat")
    me = lax.axis_index("seq")

    def relayed(relay, block, origin):
        index, place = relays[relay]
        return pltpu.make_async_remote_copy(
            src_ref=outputs[index].at[block],
            dst_ref=wholes[relay].at[origin, block],
            send_sem=relay_sends.at[relay, block],
            recv_sem=relay_receives.at[relay, origin, block],
            device_id={"mat": place},
            device_id_type=MESH,
        )

    def kept(relay, block):
        index, place = relays[relay]
        return pltpu.make_async_copy(
            outputs[index].at[block], wholes[relay].at[place, block], relay_own.at[relay, block]
        )

    def relay_all(block):
        for relay, (_, place) in enumerate(relays):

            @pl.when(here != place)
            def _():
                relayed(relay, block, here).start()

            @pl.when(here == place)
            def _():
                kept(relay, block).start()

    def relay_end(block, _):
        for relay, (_, place) in enumerate(relays):

            @pl.when(here != place)
            def _():
                relayed(relay, block, here).wait_send()

            @pl.when(here == place)
            def _():
                kept(relay, block).wait()
                for origin in range(mats):
                    if origin != place:
                        relayed(relay, block, origin).wait_recv()

        return 0

    barrier = pltpu.get_barrier_semaphore()
    greeted = line.greet(barrier)
    if relays:

        def greet_mat(lap, _):
            pl.semaphore_signal(
                barrier, inc=1, device_id={"mat": (here + lap) % mats}, device_id_type=MESH
            )
            return 0

        lax.fori_loop(1, mats, greet_mat, 0)
        greeted = greeted + mats - 1
    own = [
        pltpu.make_async_copy(inputs[index], outputs[index].at[me], own_sem.at[index])
        for index in range(arrays)
    ]
    for copy in own:
        copy.start()
    pl.semaphore_wait(barrier, greeted)
    line.begin()
    for copy in own:
        copy.wait()
    relay_all(me)

    def step(lap, _):
        line.forward(lap)

        @pl.when(lap > 1)
        def _():
            line.each(lap - 1, relay_all)

        return 0

    lax.fori_loop(1, line.outers, step, 0)
    line.take(line.outer)
    relay_all(line.across(line.outer))
    line.each(line.outers - 1, relay_all)
    line.end()
    if relays:
        lax.fori_loop(0, lax.axis_size("seq"), relay_end, 0)


def gather_seq(values, identity, space=pltpu.VMEM, ahead=(), relays=()):
    peers = lax.axis_size("seq")
    mats = lax.axis_size("mat")
    plain = [value.shape for value in values]
    values = [
        value.reshape((2, -1) + value.shape[1:]) if value.shape[0] % 32 == 0 else value[None]
        for value in values
    ]
    shapes = [jax.ShapeDtypeStruct((peers,) + value.shape, value.dtype) for value in values]
    shapes += [
        jax.ShapeDtypeStruct((mats, peers) + values[index].shape, values[index].dtype)
        for index, _ in relays
    ]
    place = pl.BlockSpec(memory_space=space)
    unread = pl.BlockSpec(memory_space=pl.ANY)
    arrays = len(values)
    results = pl.pallas_call(
        functools.partial(gather_kernel, arrays, len(ahead), tuple(relays)),
        out_shape=shapes,
        in_specs=[place] * arrays + [unread] * len(ahead),
        out_specs=[place] * arrays + [unread] * len(relays),
        scratch_shapes=line_semaphores(values)
        + [
            pltpu.SemaphoreType.DMA((arrays,)),
            pltpu.SemaphoreType.DMA((max(1, len(relays)), peers)),
            pltpu.SemaphoreType.DMA((max(1, len(relays)), mats, peers)),
            pltpu.SemaphoreType.DMA((max(1, len(relays)), peers)),
        ],
        compiler_params=pltpu.CompilerParams(collective_id=identity, has_side_effects=True),
        name="gather_seq",
    )(*values, *ahead)
    gathered = [result.reshape((peers,) + shape) for result, shape in zip(results, plain)]
    relayed = [
        result.reshape((mats, peers) + plain[index])
        for result, (index, _) in zip(results[arrays:], relays)
    ]
    return gathered + relayed


def reduce_kernel(arrays, *refs):
    inputs, outputs = refs[:arrays], refs[arrays : 2 * arrays]
    got, keep = refs[2 * arrays : 3 * arrays], refs[3 * arrays : 4 * arrays]
    passes, arrivals, sends, receives = refs[4 * arrays :]
    outers = lax.axis_size("seq") // 2
    me = lax.axis_index("seq")
    outer, inner = me // 2, me % 2
    partner = {"seq": outer * 2 + 1 - inner}

    def hand(index, place):
        return pltpu.make_async_remote_copy(
            src_ref=inputs[index].at[place * 2 + 1 - inner],
            dst_ref=got[index].at[place],
            send_sem=passes.at[index, place],
            recv_sem=arrivals.at[index, place],
            device_id=partner,
            device_id_type=MESH,
        )

    def send(index, place, origin):
        return pltpu.make_async_remote_copy(
            src_ref=keep[index].at[place],
            dst_ref=outputs[index].at[origin],
            send_sem=sends.at[index, place],
            recv_sem=receives.at[index, origin],
            device_id={"seq": place * 2 + inner},
            device_id_type=MESH,
        )

    barrier = pltpu.get_barrier_semaphore()

    def greet(lap, _):
        pl.semaphore_signal(
            barrier,
            inc=1,
            device_id={"seq": ((outer + lap) % outers) * 2 + inner},
            device_id_type=MESH,
        )
        return 0

    pl.semaphore_signal(barrier, inc=1, device_id=partner, device_id_type=MESH)
    lax.fori_loop(1, outers, greet, 0)
    pl.semaphore_wait(barrier, outers)

    def begin(lap, _):
        for index in range(arrays):
            hand(index, (outer + 1 + lap) % outers).start()
        return 0

    lax.fori_loop(0, outers, begin, 0)

    def add(lap, _):
        place = (outer + 1 + lap) % outers
        for index in range(arrays):
            hand(index, place).wait_recv()
            total = inputs[index][place * 2 + inner].astype(F32) + got[index][place].astype(F32)
            keep[index][place] = total.astype(BF16)

            @pl.when(place != outer)
            def _():
                send(index, place, outer).start()

            @pl.when(place == outer)
            def _():
                outputs[index][outer] = total.astype(BF16)

        return 0

    lax.fori_loop(0, outers, add, 0)

    def end(lap, _):
        place = (outer + lap) % outers
        for index in range(arrays):
            hand(index, place).wait_send()

            @pl.when(place != outer)
            def _():
                send(index, place, place).wait_recv()
                send(index, place, outer).wait_send()

        return 0

    lax.fori_loop(0, outers, end, 0)


def reduce_seq(values, identity, ahead=()):
    outers = lax.axis_size("seq") // 2
    arrays = len(values)
    shapes = [(outers,) + value.shape[1:] for value in values]
    place = pl.BlockSpec(memory_space=pltpu.VMEM)
    unread = pl.BlockSpec(memory_space=pl.ANY)

    def body(*refs):
        reduce_kernel(arrays, *refs[:arrays], *refs[arrays + len(ahead) :])

    results = pl.pallas_call(
        body,
        out_shape=[jax.ShapeDtypeStruct(shape, BF16) for shape in shapes],
        in_specs=[place] * arrays + [unread] * len(ahead),
        out_specs=[place] * arrays,
        scratch_shapes=[pltpu.VMEM(shape, BF16) for shape in shapes * 2]
        + [pltpu.SemaphoreType.DMA((arrays, outers))] * 4,
        compiler_params=pltpu.CompilerParams(
            collective_id=identity, has_side_effects=True, vmem_limit_bytes=48 * 1024 * 1024
        ),
        name="reduce_seq",
    )(*values, *ahead)
    return [jnp.sum(result.astype(F32), axis=0) for result in results]


def lookup_kernel(
    ids, table, small, out, smalls, found, give, got, keep, taken, passes, arrivals, sends,
    receives, small_sends, small_receives, small_own,
):
    outers, mats = taken.shape[0], taken.shape[1]
    me = lax.axis_index("seq")
    here = lax.axis_index("mat")
    outer, inner = me // 2, me % 2
    partner = {"seq": outer * 2 + 1 - inner}
    tokens = 256
    lanes = lax.broadcasted_iota(jnp.int32, (128, 128), 1)

    def device(to_outer, to_mat):
        return {"seq": to_outer * 2 + inner, "mat": to_mat}

    def hand(lap, place):
        return pltpu.make_async_remote_copy(
            src_ref=give.at[lap, place],
            dst_ref=got.at[lap, place],
            send_sem=passes.at[lap, place],
            recv_sem=arrivals.at[lap, place],
            device_id=partner,
            device_id_type=MESH,
        )

    def send(to_outer, to_mat, from_outer, from_mat):
        return pltpu.make_async_remote_copy(
            src_ref=keep.at[to_outer, to_mat],
            dst_ref=taken.at[from_outer, from_mat],
            send_sem=sends.at[to_outer, to_mat],
            recv_sem=receives.at[from_outer, from_mat],
            device_id=device(to_outer, to_mat),
            device_id_type=MESH,
        )

    def share(to_mat, from_mat):
        return pltpu.make_async_remote_copy(
            src_ref=small,
            dst_ref=smalls.at[from_mat],
            send_sem=small_sends.at[to_mat],
            recv_sem=small_receives.at[from_mat],
            device_id={"mat": to_mat},
            device_id_type=MESH,
        )

    own_small = pltpu.make_async_copy(small, smalls.at[here], small_own)
    own_small.start()
    barrier = pltpu.get_barrier_semaphore()

    def greet(lap, _):
        pl.semaphore_signal(
            barrier,
            inc=1,
            device_id=device((outer + lap // mats) % outers, (here + lap % mats) % mats),
            device_id_type=MESH,
        )
        return _

    pl.semaphore_signal(barrier, inc=1, device_id=partner, device_id_type=MESH)
    lax.fori_loop(1, outers * mats, greet, 0)
    pl.semaphore_wait(barrier, outers * mats)

    def share_start(lap, _):
        share((here + lap) % mats, here).start()
        return 0

    lax.fori_loop(1, mats, share_start, 0)

    def find(block):
        def rows(index, _):
            for step in range(8):
                row = index * 8 + step
                entry = ids[block * mats * tokens + row]
                found[pl.ds(row, 1), :] = table[pl.ds(entry, 1), :]
            return 0

        lax.fori_loop(0, mats * tokens // 8, rows, 0)

    def store(target):
        for place in range(mats):
            base = place * tokens
            target[place, 0:tokens, :] = found[base : base + tokens, 0:128].astype(BF16)
            low = found[base : base + 128, 128:256]
            high = pltpu.roll(found[base + 128 : base + tokens, 128:256], 64, 1)
            target[place, tokens : tokens + 128, :] = jnp.where(lanes < 64, low, high).astype(BF16)

    def outer_of(lap):
        return (outer + 1 + lap) % outers

    def hand_over(lap):
        find(outer_of(lap) * 2 + 1 - inner)
        store(give.at[lap])
        for place in range(mats):
            hand(lap, place).start()

    def compute(lap, _):
        to_outer = outer_of(lap)

        @pl.when(lap + 1 < outers)
        def _():
            hand_over(lap + 1)

        find(to_outer * 2 + inner)
        store(keep.at[to_outer])
        for place in range(mats):
            hand(lap, place).wait_recv()
            keep[to_outer, place] = keep[to_outer, place] + got[lap, place]
            own = jnp.logical_and(to_outer == outer, place == here)

            @pl.when(jnp.logical_not(own))
            def _():
                send(to_outer, place, outer, here).start()

            @pl.when(own)
            def _():
                taken[outer, here] = keep[to_outer, place]

        return 0

    hand_over(0)
    lax.fori_loop(0, outers, compute, 0)

    def finish(lap, _):
        to_outer, to_mat = (outer + lap // mats) % outers, (here + lap % mats) % mats
        send(to_outer, to_mat, to_outer, to_mat).wait_recv()
        send(to_outer, to_mat, outer, here).wait_send()
        return _

    lax.fori_loop(1, outers * mats, finish, 0)

    def end(lap, _):
        for place in range(mats):
            hand(lap, place).wait_send()
        return 0

    lax.fori_loop(0, outers, end, 0)

    def share_end(lap, _):
        before = (here + mats - lap) % mats
        share(before, before).wait_recv()
        share((here + lap) % mats, here).wait_send()
        return 0

    lax.fori_loop(1, mats, share_end, 0)
    own_small.wait()
    for place in range(mats):

        def gather(source, total):
            return total + taken[source, place].astype(F32)

        out[place] = lax.fori_loop(0, outers, gather, jnp.zeros((384, 128), F32)).astype(BF16)


def lookup(ids, table, small, identity):
    outers, mats = lax.axis_size("seq") // 2, lax.axis_size("mat")
    entries, part = table.shape
    padded = (entries // 8 + 1) * 8
    table = table.astype(BF16).astype(F32)
    table = jnp.pad(table, ((0, padded - entries), (0, 256 - part)))
    ids = jnp.where((ids >= 0) & (ids < entries), ids, entries)
    vmem = pl.BlockSpec(memory_space=pltpu.VMEM)
    blocks = pltpu.VMEM((outers, mats, 384, 128), BF16)
    return pl.pallas_call(
        lookup_kernel,
        out_shape=[
            jax.ShapeDtypeStruct((mats, 384, 128), BF16),
            jax.ShapeDtypeStruct((mats,) + small.shape, BF16),
        ],
        in_specs=[pl.BlockSpec(memory_space=pltpu.SMEM), vmem, vmem],
        out_specs=[vmem, vmem],
        scratch_shapes=[
            pltpu.VMEM((mats * 256, 256), F32),
            blocks,
            blocks,
            blocks,
            blocks,
            *[pltpu.SemaphoreType.DMA((outers, mats))] * 4,
            pltpu.SemaphoreType.DMA((mats,)),
            pltpu.SemaphoreType.DMA((mats,)),
            pltpu.SemaphoreType.DMA,
        ],
        compiler_params=pltpu.CompilerParams(
            collective_id=identity, has_side_effects=True, vmem_limit_bytes=56 * 1024 * 1024
        ),
        name="lookup",
    )(ids, table, small)


def scatter_rows_kernel(
    entries, ids, rows, others, first_rider, second_rider, out, squares, whole, buffer, near, *rest
):
    line = Line([rows], [buffer], rest[: Line.SEMAPHORES])
    rider_sends, rider_receives, rider_own, near_own = rest[Line.SEMAPHORES :]
    places = lax.axis_size("mat")
    here = lax.axis_index("mat")
    riders = ((first_rider, UP_PLACE), (second_rider, DOWN_PLACE))

    def ride(rider, origin):
        source, place = riders[rider]
        return pltpu.make_async_remote_copy(
            src_ref=source,
            dst_ref=whole.at[origin],
            send_sem=rider_sends.at[rider],
            recv_sem=rider_receives.at[origin],
            device_id={"mat": place},
            device_id_type=MESH,
        )

    def stay(rider):
        source, place = riders[rider]
        return pltpu.make_async_copy(source, whole.at[place], rider_own)

    mats = rows.shape[0]
    lanes = lax.broadcasted_iota(jnp.int32, (128, 128), 1)
    nears = [
        pltpu.make_async_copy(source, near.at[rider], near_own.at[rider])
        for rider, (source, _) in enumerate(riders)
    ]
    for copy in nears:
        copy.start()

    def add(block, source):
        parts = []
        for place in range(mats):
            tail = source[place, 256:384, :].astype(F32)
            low = jnp.where(lanes < 64, tail, 0.0)
            high = jnp.where(lanes < 64, pltpu.roll(tail, 64, 1), 0.0)
            tails = jnp.concatenate([low, high], axis=0).astype(BF16)
            parts.append(jnp.concatenate([source[place, 0:256, :], tails], axis=1))
        values = jnp.concatenate(parts, axis=0)
        names = jnp.concatenate(
            [ids[pl.ds(block * 2 * mats + half, 1), :] for half in range(2 * mats)], axis=1
        )
        group = lax.shift_right_arithmetic(names, 7)
        spot = lax.broadcasted_iota(jnp.int32, (128, names.shape[1]), 0)
        hits = jnp.where(spot == jnp.bitwise_and(names, 127), 1.0, 0.0).astype(BF16)

        def piece(index, _):
            first = pl.multiple_of(index * VOCAB_TILE, VOCAB_TILE)
            masked = []
            for step in range(VOCAB_TILE // 128):
                chosen = jnp.where(group == index * (VOCAB_TILE // 128) + step, 1.0, 0.0)
                masked.append(hits * chosen.astype(BF16))
            out[pl.ds(first, VOCAB_TILE), :] += dot(
                jnp.concatenate(masked, axis=0), values, 1, 0
            )
            return 0

        lax.fori_loop(0, out.shape[0] // VOCAB_TILE, piece, 0)

    barrier = pltpu.get_barrier_semaphore()
    greeted = line.greet(barrier)

    def greet_mat(lap, _):
        pl.semaphore_signal(
            barrier, inc=1, device_id={"mat": (here + lap) % places}, device_id_type=MESH
        )
        return _

    lax.fori_loop(1, places, greet_mat, 0)
    pl.semaphore_wait(barrier, greeted + places - 1)
    line.begin()
    for rider, (_, place) in enumerate(riders):

        @pl.when(here != place)
        def _():
            ride(rider, here).start()

        @pl.when(here == place)
        def _():
            stay(rider).start()

    def use(block):
        add(block, buffer.at[block])

    part = others.shape[0]

    def fill(index, _):
        cut = pl.ds(pl.multiple_of(index * VOCAB_TILE, VOCAB_TILE), VOCAB_TILE)
        more = others[:, cut].astype(F32).T
        out[cut, :] = jnp.concatenate(
            [more, jnp.zeros((VOCAB_TILE, 256 - part), F32)], axis=1
        )
        return 0

    lax.fori_loop(0, out.shape[0] // VOCAB_TILE, fill, 0)
    add(line.block(line.outer), rows)

    def square(index, total):
        cut = pl.ds(pl.multiple_of(index * 64, 64), 64)
        for rider in range(len(riders)):
            values = near[rider, cut, :].astype(F32)
            values = jnp.sum(values * values, axis=0, keepdims=True)
            for lane in range(0, values.shape[1], 256):
                total = total + values[:, lane : lane + 256]
        return total

    for copy in nears:
        copy.wait()
    total = lax.fori_loop(0, near.shape[1] // 64, square, jnp.zeros((1, 256), F32))

    def step(lap, _):
        line.forward(lap)

        @pl.when(lap == 1)
        def _():
            line.take(line.outer)
            use(line.across(line.outer))

        @pl.when(lap > 1)
        def _():
            line.each(lap - 1, use)

        return 0

    lax.fori_loop(1, line.outers, step, 0)
    line.each(line.outers - 1, use)
    line.end()
    for rider, (_, place) in enumerate(riders):

        @pl.when(here != place)
        def _():
            ride(rider, here).wait_send()

        @pl.when(here == place)
        def _():
            stay(rider).wait()
            for origin in range(places):
                if origin != place:
                    ride(rider, origin).wait_recv()

    def finish(index, total):
        cut = pl.ds(pl.multiple_of(index * VOCAB_TILE, VOCAB_TILE), VOCAB_TILE)
        values = out[cut, :]
        entry = lax.broadcasted_iota(jnp.int32, values.shape, 0) + index * VOCAB_TILE
        values = jnp.where(entry < entries, values, 0.0)
        return total + jnp.sum(values * values, axis=0, keepdims=True)

    total = lax.fori_loop(0, out.shape[0] // VOCAB_TILE, finish, total)
    squares[...] = jnp.broadcast_to(total, (8, 256))


def scatter_rows(ids, rows, others, entries, identity, riders):
    peers = lax.axis_size("seq")
    mats = lax.axis_size("mat")
    padded = -(-entries // VOCAB_TILE) * VOCAB_TILE
    unread = pl.BlockSpec(memory_space=pl.ANY)
    place = pl.BlockSpec(memory_space=pltpu.VMEM)
    return pl.pallas_call(
        functools.partial(scatter_rows_kernel, entries),
        out_shape=[
            jax.ShapeDtypeStruct((padded, 256), F32),
            jax.ShapeDtypeStruct((8, 256), F32),
            jax.ShapeDtypeStruct((mats,) + riders[0].shape, BF16),
        ],
        in_specs=[place, place, place, unread, unread],
        out_specs=[place, place, unread],
        scratch_shapes=[
            pltpu.VMEM((peers,) + rows.shape, BF16),
            pltpu.VMEM((2,) + riders[0].shape, BF16),
            *line_semaphores([rows]),
            pltpu.SemaphoreType.DMA((2,)),
            pltpu.SemaphoreType.DMA((mats,)),
            pltpu.SemaphoreType.DMA,
            pltpu.SemaphoreType.DMA((2,)),
        ],
        compiler_params=pltpu.CompilerParams(
            collective_id=identity, has_side_effects=True, vmem_limit_bytes=48 * 1024 * 1024
        ),
        name="scatter_rows",
    )(ids, rows, jnp.pad(others, ((0, 0), (0, padded - entries))), *riders)


def swap_seq(value, identity, ahead=()):
    return exchange([value], [False], identity, ahead=ahead)[0]


def move_rows(value, steps):
    count = lax.axis_size("seq")
    leading, last = (max(0, -steps), min(count, count - steps))
    return lax.ppermute(value, "seq", [(source, source + steps) for source in range(leading, last)])


def normalize(values, gain):
    scale = lax.rsqrt(jnp.mean(values * values, axis=-1, keepdims=True) + 1e-05)
    hat = values * scale
    return hat * gain, hat, scale


def normalize_back(hat, scale, gain, grad):
    gain_grad = jnp.sum(grad * hat, axis=0)
    hat_grad = grad * gain
    return gain_grad, scale * (hat_grad - hat * jnp.mean(hat_grad * hat, axis=-1, keepdims=True))


def silu_back(values):
    sig = jax.nn.sigmoid(values)
    return sig * (1.0 + values * (1.0 - sig))


def padded_rows(flat):
    size = flat.shape[-1]
    room = -(-size // 16384) * 16384 - size
    flat = jnp.pad(flat, [(0, 0)] * (flat.ndim - 1) + [(0, room)])
    return flat.reshape(flat.shape[:-1] + (-1, 1024))


def pack_small(parts):
    return padded_rows(jnp.concatenate([part.astype(BF16).reshape(-1) for part in parts]))


def unpack_small(every, parts):
    every = every.reshape(every.shape[0], -1)
    result, offset = [], 0
    for part in parts:
        size = part.size
        result.append(every[:, offset : offset + size].reshape((-1,) + part.shape))
        offset += size
    return result


def columns(stacked):
    count, rows, width = stacked.shape
    return stacked.transpose(1, 0, 2).reshape(rows, count * width)


def step_grads(weights, embedded, route, lengths, slots, weight_mask, targets, loss_all):
    table, w_in, w_out, w_up, w_down, w_x, w_step, w_route, chan_low, gains_low = weights
    channel = chan_low.astype(F32)
    gains = gains_low.astype(F32)
    me = lax.axis_index("seq")
    count = lax.axis_size("seq")
    micros, tokens = route.shape
    inner = w_in.shape[1] // 2
    vocab_part = table.shape[1]
    first_pos = me * tokens
    vocab_start = me * vocab_part
    bounds = jnp.cumsum(lengths, axis=1)
    position = first_pos + jnp.arange(tokens, dtype=jnp.int32)
    opening = position[None, :, None] == bounds[:, None, :-1]
    keeping = 1.0 - jnp.logical_or(
        jnp.any(opening, axis=2), position[None] == 0
    ).astype(F32)
    place = me.astype(jnp.int32).reshape(1)

    x0 = embedded.astype(F32)

    u, hat0, scale0 = normalize(x0, gains[0])
    u_low = u.astype(BF16)
    xz = dot(u_low, w_in, 1, 0).reshape(micros, tokens, 2 * inner)
    z = xz[:, :, inner:]
    edge = move_rows(xz[:, tokens - (CONV - 1) :, :inner], 1)
    conv, act, projected = convolve(lengths, place, xz, edge, channel, w_x)
    rank_low = projected[:, :, :RANK].reshape(-1, RANK).astype(BF16)
    rate = -jnp.exp(channel[CONV + 3 :])
    wide = projected[:, :, :, None]
    wide_shape = (micros, tokens, STATES, 128)
    inject = jnp.broadcast_to(wide[:, :, RANK : RANK + STATES], wide_shape)
    readout = jnp.broadcast_to(wide[:, :, RANK + STATES :], wide_shape)
    pre, dt, ends, totals = scan_end(keeping, projected, w_step, channel, act, inject)
    ends_all, totals_all = gather_seq([ends, totals], 1)
    y, hs, start = scan_forward(
        place, keeping, dt, act, inject, readout, rate, ends_all, totals_all
    )
    skip = channel[CONV + 2]
    z_silu = jax.nn.silu(z)
    core = y + skip * act
    mixed_low = (core * z_silu).reshape(-1, inner).astype(BF16)
    x1 = x0 + dot(mixed_low, w_out, 1, 0)

    experts = w_route.shape[1]
    capacity = max(2, 2 * tokens // experts)
    local_experts = w_up.shape[0]
    s, hat1, scale1 = normalize(x1, gains[1])
    s_low = s.astype(BF16)
    scores = dot(s_low, w_route, 1, 0)
    chosen = route.reshape(-1)[:, None] == jnp.arange(experts, dtype=jnp.int32)[None, :]
    gate = jax.nn.sigmoid(jnp.sum(jnp.where(chosen, scores, 0.0), axis=1))
    onehot = chosen.astype(jnp.int32).reshape(micros, tokens, experts)
    ranking = jnp.sum(jnp.cumsum(onehot, axis=1) * onehot, axis=2) - 1
    placed = route * capacity + ranking
    all_slots = experts * capacity
    sender = (
        placed[:, None, :] == jnp.arange(all_slots, dtype=jnp.int32)[None, :, None]
    ).astype(BF16)

    def to_experts(rows, identity, ahead=()):
        sent = jnp.einsum(
            "mst,mtd->msd", sender, rows.reshape(micros, tokens, D), preferred_element_type=F32
        ).astype(BF16)
        sent = sent.reshape(micros, count, -1, D).transpose(1, 0, 2, 3).reshape(count, -1, D)
        arrived = swap_seq(sent, identity, ahead).reshape(count, micros, local_experts, capacity, D)
        return arrived.transpose(2, 0, 1, 3, 4).reshape(local_experts, -1, D)

    def from_experts(rows, identity, ahead=()):
        rows = rows.reshape(local_experts, count, micros, capacity, D).transpose(1, 2, 0, 3, 4)
        back = swap_seq(rows.reshape(count, -1, D), identity, ahead)
        back = back.reshape(count, micros, -1, D)
        back = back.transpose(1, 0, 2, 3).reshape(micros, all_slots, D)
        return jnp.einsum("mst,msd->mtd", sender, back, preferred_element_type=F32).reshape(-1, D)

    taken = to_experts(s_low, 2)
    hidden, slope, result = run_experts(taken, w_up, w_down)
    combined = from_experts(result, 3)
    x2 = x1 + gate[:, None] * combined

    final, hat2, scale2 = normalize(x2, gains[2])
    own_count = slots.shape[1]
    local_rows = slots - first_pos
    select = (
        local_rows[:, :, None] == jnp.arange(tokens, dtype=jnp.int32)[None, None, :]
    ).astype(BF16)
    picked_rows = jnp.einsum(
        "mst,mtd->msd",
        select,
        final.astype(BF16).reshape(micros, tokens, D),
        preferred_element_type=F32,
    ).astype(BF16)
    rows = gather_seq([picked_rows.reshape(-1, D)], 4)[0].reshape(count * micros * own_count, D)

    def by_device(values):
        return values.reshape(micros, count, own_count).transpose(1, 0, 2).reshape(-1)

    targets = by_device(targets)
    counted = by_device(weight_mask).astype(F32)
    limits = jnp.stack(
        [vocab_start, jnp.minimum(VOCAB_REAL - vocab_start, vocab_part), vocab_part]
    ).astype(jnp.int32)
    logits, stats = head(limits, rows, table, targets[:, None])
    stats = exchange([stats.T], [True], 5)[0]
    top = jnp.max(stats[:, 0], axis=0)
    lse = top + jnp.log(jnp.sum(stats[:, 1] * jnp.exp(stats[:, 0] - top[None]), axis=0))
    unweighted = lse - jnp.sum(stats[:, 2], axis=0)

    def own(values):
        return lax.dynamic_index_in_dim(
            values.reshape(count, micros, own_count), me, 0, keepdims=False
        )

    rows_here = own(unweighted)
    counted_here = own(counted)
    loss_here = jnp.sum(rows_here * counted_here)
    count_here = jnp.sum(counted_here)
    scalars = jnp.pad(jnp.stack([lse, counted / loss_all], axis=1), ((0, 0), (0, 6)))
    table_grad, rows_grad = head_back(limits, rows, table, targets[:, None], scalars, logits)
    rows_grad = rows_grad.reshape(count, -1, D)
    rows_grad = reduce_seq([rows_grad], 6)[0].reshape(micros, own_count, D)
    final_grad = jnp.einsum(
        "mst,msd->mtd",
        select.astype(F32),
        rows_grad,
        precision=lax.Precision.HIGHEST,
        preferred_element_type=F32,
    ).reshape(-1, D)
    gain_two, x2_grad = normalize_back(hat2, scale2, gains[2], final_grad)

    gate_grad = jnp.sum(x2_grad * combined, axis=1)
    out_grad = to_experts((gate[:, None] * x2_grad).astype(BF16), 7, [table_grad])
    up_grad, down_grad, taken_grad = run_experts_back(
        taken, out_grad, w_up, w_down, hidden, slope
    )
    s_table = scatter_mat(table_grad, 0)
    s_grad = from_experts(taken_grad, 8, [table_grad])
    score_grad = jnp.where(chosen, (gate_grad * gate * (1.0 - gate))[:, None], 0.0).astype(BF16)
    route_grad = dot(s_low, score_grad, 0, 0)
    s_grad = s_grad + dot(score_grad, w_route, 1, 1)
    gain_one, more = normalize_back(hat1, scale1, gains[1], s_grad)
    x1_grad = x2_grad + more

    x1_grad_low = x1_grad.astype(BF16)
    up_grad, down_grad = hold([up_grad, down_grad], [s_table, x1_grad_low])
    s_up = scatter_mat(up_grad, 2)
    s_down = scatter_mat(down_grad, 1)
    mixed_grad = dot(x1_grad_low, w_out, 1, 1).reshape(micros, tokens, inner)
    out_weight_grad = dot(mixed_low, x1_grad_low, 0, 0)
    y_grad = mixed_grad * z_silu
    z_grad = mixed_grad * core * silu_back(z)
    out_weight_grad = out_weight_grad.astype(BF16)
    s_out = scatter_mat(out_weight_grad, 0)
    starts_all = gather_seq(
        [scan_start(keeping, dt, y_grad, readout, rate, [out_weight_grad, up_grad, down_grad])], 9
    )[0]
    dt_grad, act_grad, inject_grad, readout_grad, rate_grad = scan_backward(
        place, keeping, dt, act, y_grad, inject, readout, rate, totals_all, starts_all, start, hs,
        [],
    )
    skip_grad = jnp.sum(y_grad * act, axis=(0, 1))
    pre_dt = dt_grad * jax.nn.sigmoid(pre)
    pre_dt_low = pre_dt.reshape(-1, inner).astype(BF16)
    step_weight_grad = dot(rank_low, pre_dt_low, 0, 0)
    projected_grad = jnp.concatenate(
        [
            dot(pre_dt_low, w_step, 1, 1),
            jnp.sum(inject_grad, axis=3).reshape(-1, STATES),
            jnp.sum(readout_grad, axis=3).reshape(-1, STATES),
        ],
        axis=1,
    ).astype(BF16)
    raw_grad, head_grad, x_weight_grad, conv_rows = convolve_back(
        lengths, place, xz, edge, channel, w_x, conv, act, act_grad, y_grad,
        projected_grad.reshape(micros, tokens, -1),
    )
    chan_grad = jnp.concatenate(
        [
            conv_rows[: CONV + 1],
            jnp.sum(pre_dt, axis=(0, 1))[None],
            skip_grad[None],
            jnp.sum(rate_grad, axis=0) * rate,
        ],
        axis=0,
    )
    edge_grad = move_rows(head_grad, -1)
    raw_grad = raw_grad + jnp.pad(
        edge_grad, ((0, 0), (tokens - (CONV - 1), 0), (0, 0))
    )
    xz_grad = jnp.concatenate([raw_grad, z_grad], axis=2).reshape(-1, 2 * inner).astype(BF16)
    in_grad = dot(u_low, xz_grad, 0, 0)
    gain_zero, more = normalize_back(hat0, scale0, gains[0], dot(xz_grad, w_in, 1, 1))
    x0_grad = (x1_grad + more).astype(BF16)
    grads = (
        s_table,
        scatter_mat(in_grad, 1),
        s_out,
        s_up,
        s_down,
        x_weight_grad,
        step_weight_grad,
        route_grad,
        chan_grad,
        jnp.stack([gain_zero, gain_one, gain_two]),
    )
    return grads, x0_grad, loss_here, count_here, rows_here


def scatter_mat(grad, dim):
    return lax.psum_scatter(grad.astype(BF16), "mat", scatter_dimension=dim, tiled=True)


def ortho_kernel(
    place, scale, moments, experts, inward, outward, out,
    moment, grads, current, rounded, gram, low, poly, slope, trace, semaphores,
):
    blocks, size, _ = experts.shape
    tile = TILE
    tiles = size // tile
    eye = lax.broadcasted_iota(jnp.int32, (tile, tile), 0) == lax.broadcasted_iota(
        jnp.int32, (tile, tile), 1
    )
    turned = jnp.logical_or(place[0] == DOWN_PLACE, place[0] == OUT_PLACE)

    def band(index):
        return pl.ds(index * tile, tile)

    fetch = pltpu.make_async_copy(moments, moment, semaphores.at[0])
    fetch.start()

    @pl.when(jnp.logical_or(place[0] == UP_PLACE, place[0] == DOWN_PLACE))
    def _():
        copy = pltpu.make_async_copy(experts, grads, semaphores.at[1])
        copy.start()
        copy.wait()

    @pl.when(place[0] == IN_PLACE)
    def _():
        copy = pltpu.make_async_copy(inward, grads, semaphores.at[1])
        copy.start()
        copy.wait()

    @pl.when(place[0] == OUT_PLACE)
    def _():
        rows = outward.shape[1]
        grads[:, rows:, :] = jnp.zeros((blocks, size - rows, size), BF16)
        copies = [
            pltpu.make_async_copy(
                outward.at[block], grads.at[block, pl.ds(0, rows)], semaphores.at[1 + block]
            )
            for block in range(blocks)
        ]
        for copy in copies:
            copy.start()
        for copy in copies:
            copy.wait()

    fetch.wait()
    trace[...] = jnp.zeros_like(trace)

    def load(lap, _):
        block, index = lap // tiles, lap % tiles
        rows = pl.ds(pl.multiple_of(index * tile, tile), tile)
        values = MOMENTUM * moment[block, rows, :].astype(F32)
        values = values + scale[0] * grads[block, rows, :].astype(F32)
        values = values.astype(BF16).astype(F32)
        trace[...] += jnp.sum(values * values, axis=0, keepdims=True)

        @pl.when(turned)
        def _():
            flipped = values.T
            current[block, :, rows] = flipped
            rounded[0, block, :, rows] = flipped.astype(BF16)

        @pl.when(jnp.logical_not(turned))
        def _():
            current[block, rows, :] = values
            rounded[0, block, rows, :] = values.astype(BF16)

        return 0

    lax.fori_loop(0, blocks * tiles, load, 0)
    total = jnp.sum(trace[...])
    factor = 1.0 / (jnp.sqrt(total + jnp.zeros((8, 128), F32)) + 1e-07)[0:1, 0:1]

    def sweep(step, gain):
        now = step % 2

        diagonal = []
        for index in range(tiles):
            total = jnp.zeros((tile, size - index * tile), F32)
            for block in range(blocks):
                total = total + dot(
                    rounded[now, block, band(index), :],
                    rounded[now, block, index * tile :, :],
                    1,
                    1,
                )
            total = total * gain
            corner = total[:, :tile]
            own = jnp.where(eye, corner, 0.0)
            diagonal.append(jnp.sum(own, axis=0, keepdims=True))
            slope[band(index), :] = jnp.broadcast_to(
                jnp.sum(own, axis=1, keepdims=True), (tile, 128)
            )
            gram[band(index), index * tile :] = total
            low[band(index), band(index)] = (corner - own).astype(BF16)
            for other in range(index + 1, tiles):
                part = total[:, (other - index) * tile : (other - index + 1) * tile]
                flipped = part.T
                low[band(index), band(other)] = part.astype(BF16)
                gram[band(other), band(index)] = flipped
                low[band(other), band(index)] = flipped.astype(BF16)

        for index in range(tiles):
            product = dot(low[band(index), :], low[...], 1, 0)
            own = spread(slope[band(index), :], tile)
            for other in range(tiles):
                values = gram[band(index), band(other)]
                sums = own + diagonal[other]
                total = (COEF_B + COEF_C * sums) * values
                total = total + COEF_C * product[:, other * tile : (other + 1) * tile]
                if other == index:
                    total = jnp.where(eye, total - COEF_C * values * values, total)
                    part = jnp.sum(jnp.where(eye, total, 0.0), axis=1, keepdims=True)
                    total = jnp.where(eye, 0.0, total)
                poly[band(index), band(other)] = total.astype(BF16)
            slope[band(index), :] = jnp.broadcast_to(part + COEF_A, (tile, 128))

        def advance(lap, _):
            block, index = lap // tiles, lap % tiles
            rows = pl.ds(pl.multiple_of(index * tile, tile), tile)
            scaled = spread(slope[rows, :], size) * current[block, rows, :]
            values = scaled + dot(poly[rows, :], rounded[now, block], 1, 0)
            current[block, rows, :] = values
            rounded[1 - now, block, rows, :] = values.astype(BF16)
            return 0

        def advance_first(lap, _):
            block, index = lap // tiles, lap % tiles
            rows = pl.ds(pl.multiple_of(index * tile, tile), tile)
            scaled = spread(slope[rows, :], size) * current[block, rows, :]
            values = (scaled + dot(poly[rows, :], rounded[now, block], 1, 0)) * factor
            current[block, rows, :] = values
            rounded[1 - now, block, rows, :] = values.astype(BF16)
            return 0

        @pl.when(step == 0)
        def _():
            lax.fori_loop(0, blocks * tiles, advance_first, 0)

        @pl.when(step > 0)
        def _():
            lax.fori_loop(0, blocks * tiles, advance, 0)

        return jnp.ones_like(gain)

    lax.fori_loop(0, ORTHO_STEPS, sweep, factor * factor)

    def store(lap, _):
        block, index = lap // tiles, lap % tiles
        rows = pl.ds(pl.multiple_of(index * tile, tile), tile)

        @pl.when(turned)
        def _():
            out[block, :, rows] = current[block, rows, :].T.astype(BF16)

        @pl.when(jnp.logical_not(turned))
        def _():
            out[block, rows, :] = current[block, rows, :].astype(BF16)

        return 0

    lax.fori_loop(0, blocks * tiles, store, 0)


def orthogonalize(scale, moments, experts, inward, outward):
    blocks, size, width = experts.shape
    vmem = pl.BlockSpec(memory_space=pltpu.VMEM)
    smem = pl.BlockSpec(memory_space=pltpu.SMEM)
    unread = pl.BlockSpec(memory_space=pl.ANY)
    place = lax.axis_index("mat").astype(jnp.int32).reshape(1)
    return pl.pallas_call(
        ortho_kernel,
        out_shape=jax.ShapeDtypeStruct(experts.shape, BF16),
        in_specs=[smem, smem] + [unread] * 4,
        out_specs=vmem,
        scratch_shapes=[
            pltpu.VMEM((blocks, size, width), BF16),
            pltpu.VMEM((blocks, size, width), BF16),
            pltpu.VMEM((blocks, size, width), F32),
            pltpu.VMEM((2, blocks, size, width), BF16),
            pltpu.VMEM((size, size), F32),
            pltpu.VMEM((size, size), BF16),
            pltpu.VMEM((size, size), BF16),
            pltpu.VMEM((size, 128), F32),
            pltpu.VMEM((1, size), F32),
            pltpu.SemaphoreType.DMA((1 + blocks,)),
        ],
        compiler_params=pltpu.CompilerParams(vmem_limit_bytes=56 * 1024 * 1024),
        name="orthogonalize",
    )(place, scale.reshape(1), moments, experts, inward, outward)


def adamw_update(weight, mean, square, grad, rate, decay):
    mean = BETA_ONE * mean + (1.0 - BETA_ONE) * grad
    square = BETA_TWO * square + (1.0 - BETA_TWO) * grad * grad
    ratio = (
        mean
        / (1.0 - BETA_ONE**STEP_COUNT)
        / (jnp.sqrt(square / (1.0 - BETA_TWO**STEP_COUNT)) + ADAM_EPS)
    )
    return (weight * (1.0 - rate * decay) - rate * ratio, mean, square)


def table_kernel(scale, grad, weight, mean, square, _ahead, new_weight, new_mean, new_square):
    part = weight.shape[0]
    turned = grad[...].T[:part] * scale[0]
    results = adamw_update(weight[...], mean[...], square[...], turned, 0.05, 0.1)
    new_weight[...], new_mean[...], new_square[...] = results


def update_table(scale, grad, weight, mean, square, ahead):
    part, entries = weight.shape
    flat = pl.BlockSpec((part, VOCAB_TILE), lambda i: (0, i))
    return pl.pallas_call(
        table_kernel,
        grid=(-(-entries // VOCAB_TILE),),
        in_specs=[
            pl.BlockSpec(memory_space=pltpu.SMEM),
            pl.BlockSpec((VOCAB_TILE, 256), lambda i: (i, 0)),
            flat,
            flat,
            flat,
            pl.BlockSpec(memory_space=pl.ANY),
        ],
        out_specs=[flat] * 3,
        out_shape=[jax.ShapeDtypeStruct(weight.shape, F32)] * 3,
        compiler_params=kernel_params(),
        cost_estimate=pl.CostEstimate(
            flops=20 * entries * 256,
            bytes_accessed=7 * entries * 256 * 4,
            transcendentals=2 * entries * 256,
        ),
        name="update_table",
    )(scale.reshape(1), grad, weight, mean, square, ahead)


def local(
    token_ids,
    expert_route,
    doc_lengths,
    loss_slots,
    loss_weight,
    target_ids,
    embedding,
    embedding_mom,
    embedding_sq,
    in_project,
    in_project_mom,
    out_project,
    out_project_mom,
    expert_up,
    expert_up_mom,
    expert_down,
    expert_down_mom,
    x_project,
    x_project_mom,
    x_project_sq,
    step_project,
    step_project_mom,
    step_project_sq,
    router_weight,
    router_mom,
    router_sq,
    channel_param,
    channel_mom,
    channel_sq,
    norm_gains,
    gains_mom,
    gains_sq,
):
    micros = token_ids.shape[0]
    mats = lax.axis_size("mat")
    seq_count = lax.axis_size("seq")
    tokens = expert_route.shape[2]
    vocab_part, part = embedding.shape
    ids = exchange([token_ids.reshape(-1, 128)], [True], 12, ("mat",))[0]
    ids = ids.reshape(mats, micros, seq_count, tokens)
    ids = ids.transpose(2, 0, 1, 3).reshape(-1) - lax.axis_index("seq") * vocab_part
    parts = [x_project, step_project, router_weight, channel_param, norm_gains]
    found, small = lookup(ids, embedding, pack_small(parts), 10)
    found, w_table, w_out, w_up, w_down = lax.optimization_barrier(
        (
            found,
            embedding.T.astype(BF16),
            out_project.astype(BF16),
            expert_up.astype(BF16),
            expert_down.astype(BF16),
        )
    )
    small = unpack_small(small, parts)
    weights = (
        lax.all_gather(w_table, "mat", axis=0, tiled=True),
        lax.all_gather(in_project.astype(BF16), "mat", axis=1, tiled=True),
        lax.all_gather(w_out, "mat", axis=0, tiled=True),
        lax.all_gather(w_up, "mat", axis=2, tiled=True),
        lax.all_gather(w_down, "mat", axis=1, tiled=True),
        small[0].reshape(-1, small[0].shape[2]),
        columns(small[1]),
        small[2].reshape(-1, small[2].shape[2]),
        columns(small[3]),
        columns(small[4]),
    )
    half = micros * tokens // 2
    tails = found[:, 2 * half :].reshape(mats, half, 2, part - 128).transpose(0, 2, 1, 3)
    heads = found[:, : 2 * half].reshape(mats, 2, half, 128)
    embedded = jnp.concatenate([heads, tails], axis=3).transpose(1, 2, 0, 3)
    embedded = embedded.reshape(micros * tokens, mats * part)
    loss_all = micros * lax.axis_size("mat") * loss_weight.shape[2]
    moments = jnp.stack(
        [
            expert_up_mom[0],
            in_project_mom,
            expert_down_mom[0],
            jnp.pad(out_project_mom, ((0, D - out_project_mom.shape[0]), (0, 0))),
        ]
    ).astype(BF16)
    moments = lax.all_to_all(moments, "mat", split_axis=0, concat_axis=0, tiled=True)
    grads, x0_grad, loss_part, count_part, rows_here = step_grads(
        weights,
        embedded,
        expert_route[:, 0, :, 0],
        doc_lengths[:, 0],
        loss_slots[:, 0],
        loss_weight[:, 0],
        target_ids[:, 0],
        loss_all,
    )
    row_loss = rows_here[:, None, :]
    s_table, s_in, s_out, s_up, s_down, g_x, g_step, g_route, g_chan, g_gain = grads
    pieces = (
        g_x.reshape(mats, -1),
        g_step.reshape(g_step.shape[0], mats, -1).transpose(1, 0, 2).reshape(mats, -1),
        g_route.reshape(mats, -1),
        g_chan.reshape(g_chan.shape[0], mats, -1).transpose(1, 0, 2).reshape(mats, -1),
        g_gain.reshape(g_gain.shape[0], mats, -1).transpose(1, 0, 2).reshape(mats, -1),
    )
    packed = jnp.concatenate(pieces, axis=1)
    unit = seq_count * 2048
    packed = jnp.pad(packed, ((0, 0), (0, -packed.shape[1] % unit)))
    packed = packed.astype(BF16).reshape(mats, -1, 128)
    x0_parts = x0_grad.reshape(2, -1, mats, part).transpose(2, 0, 1, 3)
    x0_heads = x0_parts[..., :128].reshape(mats, -1, 128)
    x0_tails = jnp.concatenate([x0_parts[:, 0, :, 128:], x0_parts[:, 1, :, 128:]], axis=2)
    x0_heads, moments = lax.optimization_barrier((x0_heads, moments))
    x0_rows = 3 * micros * tokens // 2
    mixed = lax.all_to_all(
        jnp.concatenate([x0_heads, x0_tails, packed], axis=1),
        "mat",
        split_axis=0,
        concat_axis=0,
        tiled=True,
    )
    packed = jnp.sum(mixed[:, x0_rows:].astype(F32), axis=0).astype(BF16)
    g_table, table_squares, whole_experts = scatter_rows(
        ids.reshape(-1, 128),
        mixed[:, :x0_rows],
        s_table,
        vocab_part,
        13,
        [s_up[0], s_down[0]],
    )
    s_in, s_out, packed = reduce_seq(
        [
            s_in.reshape(seq_count, -1, D),
            s_out.reshape(seq_count, -1, D),
            packed.reshape(seq_count, -1, 128),
        ],
        14,
        [g_table],
    )
    s_up = s_up.astype(F32)
    s_down = s_down.astype(F32)
    squares = sum(jnp.sum(g * g) for g in (s_in, s_out, packed))
    squares = squares + jnp.sum(table_squares[0])
    tallies = jnp.stack([squares, loss_part, count_part])
    tallies = jnp.broadcast_to(jnp.pad(tallies, (0, 5))[:, None], (8, 128))
    g_in, g_out, packed, totals, whole_in, whole_out = gather_seq(
        [s_in.astype(BF16), s_out.astype(BF16), packed, tallies],
        15,
        relays=[(0, IN_PLACE), (1, OUT_PLACE)],
    )
    g_in = g_in.reshape(-1, D).astype(F32)
    g_out = g_out.reshape(-1, D).astype(F32)
    totals = exchange([jnp.sum(totals, axis=0)], [True], 11, ("mat",))[0]
    totals = jnp.sum(totals[:, :, 0], axis=0)
    squares, loss_total, loss_count = totals[0], totals[1], totals[2]
    grad_norm = jnp.sqrt(squares)
    scale = jnp.minimum(1.0, CLIP_NORM / (grad_norm + 1e-06))
    mom_in = MOMENTUM * in_project_mom + g_in * scale
    mom_out = MOMENTUM * out_project_mom + g_out * scale
    mom_up = MOMENTUM * expert_up_mom + s_up * scale
    mom_down = MOMENTUM * expert_down_mom + s_down * scale
    ortho = orthogonalize(
        scale,
        moments,
        whole_experts,
        whole_in.reshape(mats, D, -1),
        whole_out.reshape(mats, -1, D),
    )
    packed, ortho = lax.optimization_barrier((packed, ortho))
    packed = packed.reshape(-1)
    shards, offset = [], 0
    for piece, like in zip(
        pieces, (x_project, step_project, router_weight, channel_param, norm_gains)
    ):
        shards.append(packed[offset : offset + piece.shape[1]].reshape(like.shape))
        offset += piece.shape[1]
    table_new = update_table(
        scale, g_table, embedding.T, embedding_mom.T, embedding_sq.T, ortho
    )
    table_new = [values.T for values in table_new]
    ortho = lax.all_to_all(ortho, "mat", split_axis=0, concat_axis=0, tiled=True).astype(F32)
    shrink = 1.0 - LR_MUON * DECAY_MUON
    new_up = expert_up * shrink - LR_MUON * 0.2 * math.sqrt(max(D, FF)) * ortho[UP_PLACE][None]
    new_in = in_project * shrink - LR_MUON * 0.2 * math.sqrt(max(D, 2 * DI)) * ortho[IN_PLACE]
    new_down = (
        expert_down * shrink - LR_MUON * 0.2 * math.sqrt(max(D, FF)) * ortho[DOWN_PLACE][None]
    )
    new_out = (
        out_project * shrink
        - LR_MUON * 0.2 * math.sqrt(max(D, DI)) * ortho[OUT_PLACE, : out_project.shape[0]]
    )
    x_new = adamw_update(x_project, x_project_mom, x_project_sq, shards[0] * scale, 0.06, 0.1)
    step_new = adamw_update(
        step_project, step_project_mom, step_project_sq, shards[1] * scale, 0.06, 0.1
    )
    route_new = adamw_update(router_weight, router_mom, router_sq, shards[2] * scale, 0.06, 0.1)
    chan_new = adamw_update(channel_param, channel_mom, channel_sq, shards[3] * scale, 1.0, 0.0)
    gains_new = adamw_update(norm_gains, gains_mom, gains_sq, shards[4] * scale, 0.4, 0.0)
    return (
        loss_total,
        loss_count,
        grad_norm,
        row_loss,
        *table_new,
        new_in,
        mom_in,
        new_out,
        mom_out,
        new_up,
        mom_up,
        new_down,
        mom_down,
        *x_new,
        *step_new,
        *route_new,
        *chan_new,
        *gains_new,
    )


def solution(mesh):
    in_specs = (
        P(None, "mat", None),
        P(None, "mat", "seq", None),
        P(None, "mat", None),
        P(None, "mat", "seq"),
        P(None, "mat", None),
        P(None, "mat", None),
        P("seq", "mat"),
        P("seq", "mat"),
        P("seq", "mat"),
        P(None, "mat"),
        P(None, "mat"),
        P("mat", None),
        P("mat", None),
        P("seq", None, "mat"),
        P("seq", None, "mat"),
        P("seq", "mat", None),
        P("seq", "mat", None),
        P("mat", None),
        P("mat", None),
        P("mat", None),
        P(None, "mat"),
        P(None, "mat"),
        P(None, "mat"),
        P("mat", None),
        P("mat", None),
        P("mat", None),
        P(None, "mat"),
        P(None, "mat"),
        P(None, "mat"),
        P(None, "mat"),
        P(None, "mat"),
        P(None, "mat"),
    )
    out_specs = (
        P(),
        P(),
        P(),
        P(None, "mat", "seq"),
        P("seq", "mat"),
        P("seq", "mat"),
        P("seq", "mat"),
        P(None, "mat"),
        P(None, "mat"),
        P("mat", None),
        P("mat", None),
        P("seq", None, "mat"),
        P("seq", None, "mat"),
        P("seq", "mat", None),
        P("seq", "mat", None),
        P("mat", None),
        P("mat", None),
        P("mat", None),
        P(None, "mat"),
        P(None, "mat"),
        P(None, "mat"),
        P("mat", None),
        P("mat", None),
        P("mat", None),
        P(None, "mat"),
        P(None, "mat"),
        P(None, "mat"),
        P(None, "mat"),
        P(None, "mat"),
        P(None, "mat"),
    )
    return jax.shard_map(local, mesh=mesh, in_specs=in_specs, out_specs=out_specs, check_vma=False)
```

```python
import functools
import math

import jax
import jax.numpy as jnp
from jax import lax
from jax.experimental import pallas as pl
from jax.experimental.pallas import tpu as pltpu
from jax.sharding import PartitionSpec as P

D = 768
DI = 1536
FF = 3072
VOCAB_REAL = 50257
CONV = 4
ORTHO_STEPS = 5
STEP_COUNT = 10
STATES = 16
RANK = 48

CLIP_NORM = 0.004
COEF_A = 3.4445
COEF_B = -4.775
COEF_C = 2.0315
MOMENTUM = 0.95
LR_MUON = 0.2
DECAY_MUON = 0.01
BETA_ONE = 0.9
BETA_TWO = 0.95
ADAM_EPS = 1e-08
F32 = jnp.float32
BF16 = jnp.bfloat16
LANES = 512
UNROLL = 8
TILE = 256
VOCAB_TILE = 640
UP_PLACE, IN_PLACE, DOWN_PLACE, OUT_PLACE = 0, 1, 2, 3
TOTAL_ROWS = 8
PAD = 8
HIDDEN = 512
MESH = pl.DeviceIdType.MESH


def dot(left, right, left_dim, right_dim, **kw):
    return lax.dot_general(
        left, right, (((left_dim,), (right_dim,)), ((), ())), preferred_element_type=F32, **kw
    )


def spread(values, width):
    return jnp.concatenate([values] * (width // 128), axis=1)


def same_document(lengths, place, micro, tokens, width):
    position = place[0] * tokens + lax.broadcasted_iota(jnp.int32, (tokens, 128), 0)
    bounds, bound = [], 0
    for index in range(lengths.shape[1] - 1):
        bound = bound + lengths[micro, index]
        bounds.append(bound)
    masks = []
    for tap in range(CONV):
        source = position - (CONV - 1) + tap
        inside = source >= 0
        for bound in bounds:
            inside = jnp.logical_and(inside, (source >= bound) == (position >= bound))
        masks.append(spread(jnp.where(inside, 1.0, 0.0), width))
    return masks


def fill_padded(padded, edge, raw):
    padded[PAD - (CONV - 1) : PAD, :] = edge[0]
    padded[PAD:, :] = raw[0]


def conv_kernel(lengths, place, raw, edge, channel, w_x, conv_out, act_out, projected, padded):
    micro, group = pl.program_id(0), pl.program_id(1)
    tokens, width = raw.shape[1], raw.shape[2]
    fill_padded(padded, edge, raw)
    masks = same_document(lengths, place, micro, tokens, width)
    conv = jnp.broadcast_to(channel[CONV : CONV + 1, :], (tokens, width))
    for tap in range(CONV):
        shifted = padded[pl.ds(PAD - (CONV - 1) + tap, tokens), :]
        conv = conv + channel[tap : tap + 1, :] * shifted * masks[tap]
    act = conv * lax.logistic(conv)
    conv_out[0] = conv
    act_out[0] = act

    @pl.when(group == 0)
    def _():
        projected[...] = jnp.zeros_like(projected)

    projected[0] += dot(act.astype(BF16), w_x[...], 1, 0)


def conv_back_kernel(
    lengths, place, raw, edge, channel, w_x, conv, act, act_grad, y_grad, projected_grad,
    raw_out, head_out, x_out, rows_out, padded, total,
):
    micro = pl.program_id(1)
    tokens, width = raw.shape[1], raw.shape[2]
    fill_padded(padded, edge, raw)
    masks = same_document(lengths, place, micro, tokens, width)
    grad = act_grad[0] + y_grad[0] * channel[CONV + 2 : CONV + 3, :]
    grad = grad + dot(projected_grad[0], w_x[...], 1, 1)
    values = conv[0]
    sig = lax.logistic(values)
    grad = grad * (sig * (1.0 + values * (1.0 - sig)))

    @pl.when(micro == 0)
    def _():
        x_out[...] = jnp.zeros_like(x_out)
        rows_out[...] = jnp.zeros_like(rows_out)

    x_out[...] += dot(act[0].astype(BF16), projected_grad[0], 0, 0)
    total[...] = jnp.zeros_like(total)
    for tap in range(CONV):
        span = pl.ds(PAD - (CONV - 1) + tap, tokens)
        kept = grad * masks[tap]
        rows_out[tap : tap + 1, :] += jnp.sum(kept * padded[span, :], axis=0, keepdims=True)
        total[span, :] += channel[tap : tap + 1, :] * kept
    rows_out[CONV : CONV + 1, :] += jnp.sum(grad, axis=0, keepdims=True)
    raw_out[0] = total[PAD:, :]
    head_out[0] = total[PAD - (CONV - 1) : PAD, :]


def end_kernel(keep, projected, w_step, channel, act, inject, pre_out, dt_out, out, totals):
    micro = pl.program_id(1)
    micros = pl.num_programs(1)
    tokens, width = act.shape[1], act.shape[2]
    rates = -jnp.exp(channel[CONV + 3 :, :])
    pre = dot(projected[0][:, :RANK].astype(BF16), w_step[...], 1, 0)
    pre = pre + channel[CONV + 1 : CONV + 2, :]
    step_size = jnp.maximum(pre, 0.0) + jnp.log1p(jnp.exp(-jnp.abs(pre)))
    pre_out[0] = pre
    dt_out[0] = step_size

    def block(step, carry):
        state, alive = carry
        for inner in range(UNROLL):
            t = step * UNROLL + inner
            d = dt_out[0, pl.ds(t, 1), :]
            w = d * act[0, pl.ds(t, 1), :]
            k = keep[micro, t]
            state = jnp.exp(rates * d) * k * state + spread(inject[0, t], width) * w
            alive = alive * k
        return state, alive

    state, alive = lax.fori_loop(
        0, tokens // UNROLL, block, (jnp.zeros((STATES, width), F32), jnp.float32(1.0))
    )
    out[...] = state.astype(BF16)

    @pl.when(micro == 0)
    def _():
        totals[...] = jnp.zeros_like(totals)

    totals[pl.ds(micro, 1), :] = jnp.sum(step_size, axis=0, keepdims=True)
    totals[pl.ds(micros + micro, 1), :] = jnp.zeros((1, width), F32) + alive


def forward_kernel(
    place, keep, dt, act, inject, readout, rate, ends, totals, y_out, h_out, start_out
):
    micro = pl.program_id(0)
    micros = pl.num_programs(0)
    tokens, width = dt.shape[1], dt.shape[2]
    rates = rate[...]
    me = place[0]

    def fold(source, state):
        total = totals[source, pl.ds(micro, 1), :]
        alive = totals[source, pl.ds(micros + micro, 1), :]
        return jnp.exp(rates * total) * alive * state + ends[source].astype(F32)

    state = lax.fori_loop(0, me, fold, jnp.zeros((STATES, width), F32))
    start_out[0] = state

    def block(step, state):
        for inner in range(UNROLL):
            t = step * UNROLL + inner
            d = dt[0, pl.ds(t, 1), :]
            w = d * act[0, pl.ds(t, 1), :]
            state = jnp.exp(rates * d) * keep[micro, t] * state + spread(inject[0, t], width) * w
            h_out[0, t] = state
            y_out[0, pl.ds(t, 1), :] = jnp.sum(
                spread(readout[0, t], width) * state, axis=0, keepdims=True
            )
        return state

    lax.fori_loop(0, tokens // UNROLL, block, state)


def start_kernel(keep, dt, dy, readout, rate, out):
    micro = pl.program_id(0)
    tokens, width = dt.shape[1], dt.shape[2]
    rates = rate[...]

    def block(step, state):
        for inner in range(UNROLL):
            t = tokens - 1 - (step * UNROLL + inner)
            d = dt[0, pl.ds(t, 1), :]
            state = state + spread(readout[0, t], width) * dy[0, pl.ds(t, 1), :]
            state = jnp.exp(rates * d) * keep[micro, t] * state
        return state

    state = lax.fori_loop(0, tokens // UNROLL, block, jnp.zeros((STATES, width), F32))
    out[...] = state.astype(BF16)


def backward_kernel(
    place,
    keep,
    dt,
    act,
    dy,
    inject,
    readout,
    rate,
    totals,
    starts,
    start,
    hs,
    ddt_out,
    da_out,
    db_out,
    dc_out,
    drate_out,
):
    micro = pl.program_id(0)
    micros = pl.num_programs(0)
    group = pl.program_id(1)
    tokens, width = dt.shape[1], dt.shape[2]
    rates = rate[...]
    me = place[0]
    count = totals.shape[0]

    def fold(lap, state):
        source = count - 1 - lap
        total = totals[source, pl.ds(micro, 1), :]
        alive = totals[source, pl.ds(micros + micro, 1), :]
        return jnp.exp(rates * total) * alive * state + starts[source].astype(F32)

    grad = lax.fori_loop(0, count - 1 - me, fold, jnp.zeros((STATES, width), F32))

    @pl.when(group == 0)
    def _():
        db_out[...] = jnp.zeros_like(db_out)
        dc_out[...] = jnp.zeros_like(dc_out)

    def gather_lanes(values):
        total = values[:, 0:128]
        for tile in range(1, width // 128):
            total = total + values[:, tile * 128 : (tile + 1) * 128]
        return total

    def one(t, before, carry):
        grad, drate, state = carry
        d = dt[0, pl.ds(t, 1), :]
        x = act[0, pl.ds(t, 1), :]
        g_y = dy[0, pl.ds(t, 1), :]
        w = d * x
        grad = grad + spread(readout[0, t], width) * g_y
        db_out[0, t] += gather_lanes(grad * w)
        dc_out[0, t] += gather_lanes(state * g_y)
        dw = jnp.sum(grad * spread(inject[0, t], width), axis=0, keepdims=True)
        grad = jnp.exp(rates * d) * keep[micro, t] * grad
        effect = grad * before
        drate = drate + effect * d
        ddt_out[0, pl.ds(t, 1), :] = (
            jnp.sum(effect * rates, axis=0, keepdims=True) + dw * x
        )
        da_out[0, pl.ds(t, 1), :] = dw * d
        return grad, drate, before

    def block(step, carry):
        for inner in range(UNROLL):
            t = tokens - 1 - (step * UNROLL + inner)
            carry = one(t, hs[0, t - 1], carry)
        return carry

    carry = (grad, jnp.zeros((STATES, width), F32), hs[0, tokens - 1])
    carry = lax.fori_loop(0, tokens // UNROLL - 1, block, carry)
    for t in range(UNROLL - 1, -1, -1):
        carry = one(t, hs[0, t - 1] if t else start[0], carry)
    drate_out[0] = carry[1]


def specs(tokens, seq_count):
    rows = pl.BlockSpec((1, tokens, LANES), lambda m, g: (m, 0, g))
    wide = pl.BlockSpec((1, tokens, STATES, 128), lambda m, g: (m, 0, 0, 0))
    rate = pl.BlockSpec((STATES, LANES), lambda m, g: (0, g))
    state = pl.BlockSpec((1, STATES, LANES), lambda m, g: (m, 0, g))
    edge = pl.BlockSpec((STATES, LANES), lambda m, g: (m, g))
    edges = pl.BlockSpec((seq_count, STATES, LANES), lambda m, g: (0, m, g))
    totals = pl.BlockSpec((seq_count, TOTAL_ROWS, LANES), lambda m, g: (0, 0, g))
    every = pl.BlockSpec((1, tokens, STATES, LANES), lambda m, g: (m, 0, 0, g))
    scalars = pl.BlockSpec(memory_space=pltpu.SMEM)
    return rows, wide, rate, state, edge, edges, totals, every, scalars


def kernel_params():
    return pltpu.CompilerParams(vmem_limit_bytes=48 * 1024 * 1024)


def convolve(lengths, place, xz, edge, channel, w_x):
    micros, tokens, inner = xz.shape[0], xz.shape[1], xz.shape[2] // 2
    scalars = pl.BlockSpec(memory_space=pltpu.SMEM)
    rows = pl.BlockSpec((1, tokens, LANES), lambda m, g: (m, 0, g))
    shape = jax.ShapeDtypeStruct((micros, tokens, inner), F32)
    columns_x = w_x.shape[1]
    return pl.pallas_call(
        conv_kernel,
        grid=(micros, inner // LANES),
        in_specs=[
            scalars,
            scalars,
            rows,
            pl.BlockSpec((1, CONV - 1, LANES), lambda m, g: (m, 0, g)),
            pl.BlockSpec((channel.shape[0], LANES), lambda m, g: (0, g)),
            pl.BlockSpec((LANES, columns_x), lambda m, g: (g, 0)),
        ],
        out_specs=[rows, rows, pl.BlockSpec((1, tokens, columns_x), lambda m, g: (m, 0, 0))],
        out_shape=[shape, shape, jax.ShapeDtypeStruct((micros, tokens, columns_x), F32)],
        scratch_shapes=[pltpu.VMEM((PAD + tokens, LANES), F32)],
        compiler_params=kernel_params(),
        name="mixer_conv",
    )(lengths, place, xz, edge, channel, w_x)


def convolve_back(
    lengths, place, xz, edge, channel, w_x, conv, act, act_grad, y_grad, projected_grad
):
    micros, tokens, inner = conv.shape
    scalars = pl.BlockSpec(memory_space=pltpu.SMEM)
    rows = pl.BlockSpec((1, tokens, LANES), lambda g, m: (m, 0, g))
    ends = pl.BlockSpec((1, CONV - 1, LANES), lambda g, m: (m, 0, g))
    columns_x = w_x.shape[1]
    weight = pl.BlockSpec((LANES, columns_x), lambda g, m: (g, 0))
    return pl.pallas_call(
        conv_back_kernel,
        grid=(inner // LANES, micros),
        in_specs=[
            scalars,
            scalars,
            rows,
            ends,
            pl.BlockSpec((channel.shape[0], LANES), lambda g, m: (0, g)),
            weight,
            rows,
            rows,
            rows,
            rows,
            pl.BlockSpec((1, tokens, columns_x), lambda g, m: (m, 0, 0)),
        ],
        out_specs=[rows, ends, weight, pl.BlockSpec((8, LANES), lambda g, m: (0, g))],
        out_shape=[
            jax.ShapeDtypeStruct((micros, tokens, inner), F32),
            jax.ShapeDtypeStruct((micros, CONV - 1, inner), F32),
            jax.ShapeDtypeStruct((inner, columns_x), F32),
            jax.ShapeDtypeStruct((8, inner), F32),
        ],
        scratch_shapes=[pltpu.VMEM((PAD + tokens, LANES), F32)] * 2,
        compiler_params=kernel_params(),
        name="mixer_conv_back",
    )(lengths, place, xz, edge, channel, w_x, conv, act, act_grad, y_grad, projected_grad)


def scan_end(keep, projected, w_step, channel, act, inject):
    micros, tokens, inner = act.shape
    rows = pl.BlockSpec((1, tokens, LANES), lambda g, m: (m, 0, g))
    columns_x = projected.shape[2]
    shape = jax.ShapeDtypeStruct((micros, tokens, inner), F32)
    return pl.pallas_call(
        end_kernel,
        grid=(inner // LANES, micros),
        in_specs=[
            pl.BlockSpec(memory_space=pltpu.SMEM),
            pl.BlockSpec((1, tokens, columns_x), lambda g, m: (m, 0, 0)),
            pl.BlockSpec((RANK, LANES), lambda g, m: (0, g)),
            pl.BlockSpec((channel.shape[0], LANES), lambda g, m: (0, g)),
            rows,
            pl.BlockSpec((1, tokens, STATES, 128), lambda g, m: (m, 0, 0, 0)),
        ],
        out_specs=[
            rows,
            rows,
            pl.BlockSpec((STATES, LANES), lambda g, m: (m, g)),
            pl.BlockSpec((TOTAL_ROWS, LANES), lambda g, m: (0, g)),
        ],
        out_shape=[
            shape,
            shape,
            jax.ShapeDtypeStruct((micros * STATES, inner), BF16),
            jax.ShapeDtypeStruct((TOTAL_ROWS, inner), F32),
        ],
        compiler_params=kernel_params(),
        name="scan_end",
    )(keep, projected, w_step, channel, act, inject)


def scan_forward(place, keep, dt, act, inject, readout, rate, ends_all, totals_all):
    micros, tokens, inner = dt.shape
    rows, wide, rated, state, _, edges, totals, every, scalars = specs(tokens, ends_all.shape[0])
    return pl.pallas_call(
        forward_kernel,
        grid=(micros, inner // LANES),
        in_specs=[scalars, scalars, rows, rows, wide, wide, rated, edges, totals],
        out_specs=[rows, every, state],
        out_shape=[
            jax.ShapeDtypeStruct((micros, tokens, inner), F32),
            jax.ShapeDtypeStruct((micros, tokens, STATES, inner), F32),
            jax.ShapeDtypeStruct((micros, STATES, inner), F32),
        ],
        compiler_params=kernel_params(),
        name="scan_forward",
    )(place, keep, dt, act, inject, readout, rate, ends_all, totals_all)


def scan_start(keep, dt, dy, readout, rate, ahead):
    micros, tokens, inner = dt.shape
    rows, wide, rated, _, edge, _, _, _, scalars = specs(tokens, 1)
    unread = pl.BlockSpec(memory_space=pl.ANY)

    def body(keep, dt, dy, readout, rate, *rest):
        start_kernel(keep, dt, dy, readout, rate, rest[-1])

    return pl.pallas_call(
        body,
        grid=(micros, inner // LANES),
        in_specs=[scalars, rows, rows, wide, rated] + [unread] * len(ahead),
        out_specs=edge,
        out_shape=jax.ShapeDtypeStruct((micros * STATES, inner), BF16),
        compiler_params=kernel_params(),
        name="scan_start",
    )(keep, dt, dy, readout, rate, *ahead)


def scan_backward(
    place, keep, dt, act, dy, inject, readout, rate, totals_all, starts_all, start, hs, ahead
):
    micros, tokens, inner = dt.shape
    rows, wide, rated, state, _, edges, totals, every, scalars = specs(tokens, totals_all.shape[0])
    unread = pl.BlockSpec(memory_space=pl.ANY)

    def body(*refs):
        backward_kernel(*refs[:12], *refs[12 + len(ahead) :])

    return pl.pallas_call(
        body,
        grid=(micros, inner // LANES),
        in_specs=[
            scalars, scalars, rows, rows, rows, wide, wide, rated, totals, edges, state, every,
        ]
        + [unread] * len(ahead),
        out_specs=[rows, rows, wide, wide, state],
        out_shape=[
            jax.ShapeDtypeStruct((micros, tokens, inner), F32),
            jax.ShapeDtypeStruct((micros, tokens, inner), F32),
            jax.ShapeDtypeStruct((micros, tokens, STATES, 128), F32),
            jax.ShapeDtypeStruct((micros, tokens, STATES, 128), F32),
            jax.ShapeDtypeStruct((micros, STATES, inner), F32),
        ],
        compiler_params=kernel_params(),
        name="scan_backward",
    )(place, keep, dt, act, dy, inject, readout, rate, totals_all, starts_all, start, hs, *ahead)


def expert_kernel(taken, w_up, w_down, hidden_out, slope_out, out, total):
    step = pl.program_id(1)
    values = dot(taken[0], w_up[0], 1, 0)
    below = 0.5 + 0.5 * lax.erf(values * math.sqrt(0.5))
    hidden = (values * below).astype(BF16)
    density = jnp.exp(-0.5 * values * values) * (1.0 / math.sqrt(2.0 * math.pi))
    hidden_out[0] = hidden
    slope_out[0] = below + values * density

    @pl.when(step == 0)
    def _():
        total[...] = jnp.zeros_like(total)

    total[...] += dot(hidden, w_down[0], 1, 0)

    @pl.when(step == pl.num_programs(1) - 1)
    def _():
        out[0] = total[...].astype(BF16)


def expert_back_kernel(
    taken, grad, w_up, w_down, hidden, slope, up_out, down_out, taken_out, total
):
    step = pl.program_id(1)
    pre_grad = (dot(grad[0], w_down[0], 1, 1) * slope[0]).astype(BF16)
    down_out[0] = dot(hidden[0], grad[0], 0, 0).astype(BF16)
    up_out[0] = dot(taken[0], pre_grad, 0, 0).astype(BF16)

    @pl.when(step == 0)
    def _():
        total[...] = jnp.zeros_like(total)

    total[...] += dot(pre_grad, w_up[0], 1, 1)

    @pl.when(step == pl.num_programs(1) - 1)
    def _():
        taken_out[0] = total[...].astype(BF16)


def expert_specs(rows, width):
    whole = pl.BlockSpec((1, rows, width), lambda e, j: (e, 0, 0))
    up = pl.BlockSpec((1, width, HIDDEN), lambda e, j: (e, 0, j))
    down = pl.BlockSpec((1, HIDDEN, width), lambda e, j: (e, j, 0))
    units = pl.BlockSpec((1, rows, HIDDEN), lambda e, j: (e, 0, j))
    return whole, up, down, units


def run_experts(taken, w_up, w_down):
    experts, rows, width = taken.shape
    hidden = w_up.shape[2]
    whole, up, down, units = expert_specs(rows, width)
    return pl.pallas_call(
        expert_kernel,
        grid=(experts, hidden // HIDDEN),
        in_specs=[whole, up, down],
        out_specs=[units, units, whole],
        out_shape=[
            jax.ShapeDtypeStruct((experts, rows, hidden), BF16),
            jax.ShapeDtypeStruct((experts, rows, hidden), F32),
            jax.ShapeDtypeStruct(taken.shape, BF16),
        ],
        scratch_shapes=[pltpu.VMEM((rows, width), F32)],
        compiler_params=kernel_params(),
        name="experts",
    )(taken, w_up, w_down)


def run_experts_back(taken, grad, w_up, w_down, hidden, slope):
    experts, rows, width = taken.shape
    whole, up, down, units = expert_specs(rows, width)
    return pl.pallas_call(
        expert_back_kernel,
        grid=(experts, hidden.shape[2] // HIDDEN),
        in_specs=[whole, whole, up, down, units, units],
        out_specs=[up, down, whole],
        out_shape=[
            jax.ShapeDtypeStruct(w_up.shape, BF16),
            jax.ShapeDtypeStruct(w_down.shape, BF16),
            jax.ShapeDtypeStruct(taken.shape, BF16),
        ],
        scratch_shapes=[pltpu.VMEM((rows, width), F32)],
        compiler_params=kernel_params(),
        name="experts_back",
    )(taken, grad, w_up, w_down, hidden, slope)


def head_columns(width):
    return lax.broadcasted_iota(jnp.int32, (1, width), 1) + pl.program_id(0) * width


def head_kernel(limits, rows, table, targets, logits_out, stats, largest, summed, wanted):
    step = pl.program_id(0)
    tile = table.shape[1]
    column = head_columns(tile)
    logits = dot(rows[...], table[...], 1, 0)
    logits = jnp.where(column < limits[1], logits, -1e30)
    logits_out[...] = logits
    named = targets[...] - limits[0]
    named = jnp.where(named < limits[1], named, -1)

    @pl.when(step == 0)
    def _():
        largest[...] = jnp.full_like(largest, -1e30)
        summed[...] = jnp.zeros_like(summed)
        wanted[...] = jnp.zeros_like(wanted)

    parts = [logits[:, first : first + 128] for first in range(0, tile, 128)]
    before = largest[...]
    top = functools.reduce(jnp.maximum, parts, before)
    total = summed[...] * jnp.exp(before - top)
    found = wanted[...]
    for index, part in enumerate(parts):
        total = total + jnp.exp(part - top)
        spot = column[:, index * 128 : (index + 1) * 128]
        found = found + jnp.where(spot == named, part, 0.0)
    largest[...], summed[...], wanted[...] = top, total, found

    @pl.when(step == pl.num_programs(0) - 1)
    def _():
        most = jnp.max(top, axis=1, keepdims=True)
        stats[...] = jnp.zeros_like(stats)
        stats[:, 0:1] = most
        stats[:, 1:2] = jnp.sum(total * jnp.exp(top - most), axis=1, keepdims=True)
        stats[:, 2:3] = jnp.sum(found, axis=1, keepdims=True)


def head_back_kernel(
    limits, rows, table, targets, scalars, logits, table_out, rows_out, total
):
    step = pl.program_id(0)
    column = head_columns(table.shape[1])
    inside = column < limits[1]
    probability = jnp.exp(logits[...] - scalars[:, 0:1])
    hit = jnp.where(column == targets[...] - limits[0], 1.0, 0.0)
    grad = scalars[:, 1:2] * (probability - hit)
    grad = jnp.where(inside, grad, 0.0).astype(BF16)

    @pl.when(step == 0)
    def _():
        total[...] = jnp.zeros_like(total)

    table_out[...] = dot(rows[...], grad, 1, 0).astype(BF16)

    @pl.when(step < pl.num_programs(0) - 1)
    def _():
        total[...] += dot(grad, table[...], 1, 1)

    @pl.when(step == pl.num_programs(0) - 1)
    def _():
        weight = jnp.where(inside, table[...].astype(F32), 0.0).astype(BF16)
        rows_out[...] = (total[...] + dot(grad, weight, 1, 1)).astype(BF16)


def head_specs(rows, table):
    count, width = rows.shape
    tile = 1280 if count <= 512 else 640
    whole = pl.BlockSpec((count, width), lambda j: (0, 0))
    part = pl.BlockSpec((width, tile), lambda j: (0, j))
    column = pl.BlockSpec((count, 1), lambda j: (0, 0))
    few = pl.BlockSpec((count, 8), lambda j: (0, 0))
    logits = pl.BlockSpec((count, tile), lambda j: (0, j))
    return whole, part, column, few, logits, (-(-table.shape[1] // tile),)


def head(limits, rows, table, targets):
    whole, part, column, few, logits, grid = head_specs(rows, table)
    return pl.pallas_call(
        head_kernel,
        grid=grid,
        in_specs=[pl.BlockSpec(memory_space=pltpu.SMEM), whole, part, column],
        out_specs=[logits, few],
        out_shape=[
            jax.ShapeDtypeStruct((rows.shape[0], table.shape[1]), F32),
            jax.ShapeDtypeStruct((rows.shape[0], 8), F32),
        ],
        scratch_shapes=[pltpu.VMEM((rows.shape[0], 128), F32)] * 3,
        compiler_params=kernel_params(),
        name="head",
    )(limits, rows, table, targets)


def head_back(limits, rows, table, targets, scalars, logits):
    whole, part, column, few, logit, grid = head_specs(rows, table)
    turned = pl.BlockSpec((rows.shape[1], rows.shape[0]), lambda j: (0, 0))
    return pl.pallas_call(
        head_back_kernel,
        grid=grid,
        in_specs=[
            pl.BlockSpec(memory_space=pltpu.SMEM), turned, part, column, few, logit,
        ],
        out_specs=[part, whole],
        out_shape=[
            jax.ShapeDtypeStruct(table.shape, BF16),
            jax.ShapeDtypeStruct(rows.shape, BF16),
        ],
        scratch_shapes=[pltpu.VMEM(rows.shape, F32)],
        compiler_params=kernel_params(),
        name="head_back",
    )(limits, rows.T, table, targets, scalars, logits)


def exchange_kernel(groups, gathers, ahead, *refs):
    arrays = len(groups)
    inputs, outputs = refs[:arrays], refs[arrays + ahead : 2 * arrays + ahead]
    sends, receives, own_sem = refs[2 * arrays + ahead :]

    def place_of(axes):
        if len(axes) == 1:
            return lax.axis_size(axes[0]), lax.axis_index(axes[0]), lambda peer: {axes[0]: peer}
        width = lax.axis_size(axes[1])
        return (
            lax.axis_size(axes[0]) * width,
            lax.axis_index(axes[0]) * width + lax.axis_index(axes[1]),
            lambda peer: {axes[0]: peer // width, axes[1]: peer % width},
        )

    def source(index, peer):
        return inputs[index] if gathers[index] else inputs[index].at[peer]

    def copy(index, device, peer, block):
        return pltpu.make_async_remote_copy(
            src_ref=source(index, peer),
            dst_ref=outputs[index].at[block],
            send_sem=sends.at[index, peer],
            recv_sem=receives.at[index, block],
            device_id=device(peer),
            device_id_type=MESH,
        )

    barrier = pltpu.get_barrier_semaphore()
    total = 0
    for axes in sorted(set(groups)):
        peers, me, device = place_of(axes)

        def greet(lap, _):
            pl.semaphore_signal(
                barrier, inc=1, device_id=device((me + lap) % peers), device_id_type=MESH
            )
            return _

        lax.fori_loop(1, peers, greet, 0)
        total += peers - 1
    own = []
    for index, axes in enumerate(groups):
        me = place_of(axes)[1]
        own.append(
            pltpu.make_async_copy(source(index, me), outputs[index].at[me], own_sem.at[index])
        )
        own[-1].start()
    pl.semaphore_wait(barrier, total)
    for index, axes in enumerate(groups):
        peers, me, device = place_of(axes)

        def begin(lap, _):
            copy(index, device, (me + lap) % peers, me).start()
            return _

        lax.fori_loop(1, peers, begin, 0)
    for index, axes in enumerate(groups):
        peers, me, device = place_of(axes)
        own[index].wait()

        def end(lap, _):
            before = (me + peers - lap) % peers
            copy(index, device, before, before).wait_recv()
            copy(index, device, (me + lap) % peers, me).wait_send()
            return _

        lax.fori_loop(1, peers, end, 0)


def exchange(values, gathers, identity, axes=("seq",), space=pltpu.VMEM, ahead=()):
    groups = [axes] * len(values)
    peers = [math.prod(lax.axis_size(axis) for axis in group) for group in groups]
    place = pl.BlockSpec(memory_space=space)
    unread = pl.BlockSpec(memory_space=pl.ANY)
    shapes = [
        jax.ShapeDtypeStruct(((count,) if gather else ()) + value.shape, value.dtype)
        for value, gather, count in zip(values, gathers, peers)
    ]
    arrays = len(values)
    return pl.pallas_call(
        functools.partial(exchange_kernel, tuple(groups), tuple(gathers), len(ahead)),
        out_shape=shapes,
        in_specs=[place] * arrays + [unread] * len(ahead),
        out_specs=[place] * arrays,
        scratch_shapes=[
            pltpu.SemaphoreType.DMA((arrays, max(peers))),
            pltpu.SemaphoreType.DMA((arrays, max(peers))),
            pltpu.SemaphoreType.DMA((arrays,)),
        ],
        compiler_params=pltpu.CompilerParams(collective_id=identity, has_side_effects=True),
        name="exchange",
    )(*values, *ahead)


def hold(values, ahead):
    unread = pl.BlockSpec(memory_space=pl.ANY)
    return pl.pallas_call(
        lambda *refs: None,
        out_shape=[jax.ShapeDtypeStruct(value.shape, value.dtype) for value in values],
        in_specs=[unread] * (len(values) + len(ahead)),
        out_specs=[unread] * len(values),
        input_output_aliases={index: index for index in range(len(values))},
        name="hold",
    )(*values, *ahead)


class Line:
    SEMAPHORES = 6

    def __init__(self, inputs, outputs, semaphores):
        self.inputs, self.outputs = inputs, outputs
        self.sends, self.receives = semaphores[0::2], semaphores[1::2]
        self.outers = lax.axis_size("seq") // 2
        me = lax.axis_index("seq")
        self.outer, self.inner = me // 2, me % 2
        self.later = self.outer + 1 < self.outers
        self.earlier = self.outer > 0

    def block(self, outer):
        return outer * 2 + self.inner

    def across(self, outer):
        return outer * 2 + 1 - self.inner

    def target(self, way):
        step = (2, -2, 1 - 2 * self.inner)[way]
        return {"seq": self.outer * 2 + self.inner + step}

    def pieces(self):
        for index, source in enumerate(self.inputs):
            for piece in range(source.shape[0]):
                yield index, piece

    def copy(self, way, index, outer, piece, place, first=False):
        source = self.outputs[index].at[place, piece]
        return pltpu.make_async_remote_copy(
            src_ref=self.inputs[index].at[piece] if first else source,
            dst_ref=self.outputs[index].at[place, piece],
            send_sem=self.sends[way].at[index, outer, piece],
            recv_sem=self.receives[way].at[index, outer, piece],
            device_id=self.target(way),
            device_id_type=MESH,
        )

    def ways(self):
        return ((0, self.later), (1, self.earlier))

    def greet(self, barrier):
        for way, exists in self.ways():

            @pl.when(exists)
            def _():
                pl.semaphore_signal(
                    barrier, inc=1, device_id=self.target(way), device_id_type=MESH
                )

        pl.semaphore_signal(barrier, inc=1, device_id=self.target(2), device_id_type=MESH)
        return 1 + self.later.astype(jnp.int32) + self.earlier.astype(jnp.int32)

    def begin(self):
        mine = self.block(self.outer)
        for index, piece in self.pieces():
            for way, exists in self.ways():

                @pl.when(exists)
                def _():
                    self.copy(way, index, self.outer, piece, mine, True).start()

            self.copy(2, index, self.outer, piece, mine, True).start()

    def forward(self, lap):
        for index, piece in self.pieces():
            for way, exists in self.ways():
                outer = self.outer + (-lap, lap)[way]
                place = self.block(outer)

                @pl.when(jnp.logical_and(outer >= 0, outer < self.outers))
                def _():
                    self.copy(way, index, outer, piece, place).wait_recv()

                    @pl.when(exists)
                    def _():
                        self.copy(way, index, outer, piece, place).start()

                    self.copy(2, index, outer, piece, place).start()

    def take(self, outer):
        for index, piece in self.pieces():
            self.copy(2, index, outer, piece, self.across(outer)).wait_recv()

    def each(self, lap, use, partners=None):
        for way in range(2):
            outer = self.outer + (-lap, lap)[way]

            @pl.when(jnp.logical_and(outer >= 0, outer < self.outers))
            def _():
                if partners is not True:
                    use(self.block(outer))
                if partners is not False:
                    self.take(outer)
                    use(self.across(outer))

    def end(self):
        def one(outer, _):
            for index, piece in self.pieces():
                place = self.block(outer)

                @pl.when(jnp.logical_and(self.later, outer <= self.outer))
                def _():
                    self.copy(0, index, outer, piece, place).wait_send()

                @pl.when(jnp.logical_and(self.earlier, outer >= self.outer))
                def _():
                    self.copy(1, index, outer, piece, place).wait_send()

                self.copy(2, index, outer, piece, place).wait_send()
            return 0

        lax.fori_loop(0, self.outers, one, 0)


def line_semaphores(values):
    shape = (len(values), lax.axis_size("seq") // 2, max(value.shape[0] for value in values))
    return [pltpu.SemaphoreType.DMA(shape)] * Line.SEMAPHORES


def gather_kernel(arrays, ahead, relays, everyone, *refs):
    if everyone:
        tally, tallies = refs[arrays], refs[2 * arrays + 1 + ahead]
        refs = list(refs)
        del refs[2 * arrays + 1 + ahead], refs[arrays]
    inputs = refs[:arrays]
    outputs = refs[arrays + ahead : 2 * arrays + ahead]
    wholes = refs[2 * arrays + ahead : 2 * arrays + ahead + len(relays)]
    rest = refs[2 * arrays + ahead + len(relays) :]
    line = Line(inputs, outputs, rest[: Line.SEMAPHORES])
    own_sem, relay_sends, relay_receives, relay_own = rest[Line.SEMAPHORES :][:4]
    all_sends, all_receives, all_own = rest[Line.SEMAPHORES + 4 :]
    mats, here = lax.axis_size("mat"), lax.axis_index("mat")
    me = lax.axis_index("seq")
    devices = lax.axis_size("seq") * mats
    number = me * mats + here

    def device(other):
        return {"seq": other // mats, "mat": other % mats}

    def report(other, origin):
        return pltpu.make_async_remote_copy(
            src_ref=tally,
            dst_ref=tallies.at[origin],
            send_sem=all_sends.at[other],
            recv_sem=all_receives.at[origin],
            device_id=device(other),
            device_id_type=MESH,
        )

    def relayed(relay, block, origin):
        index, place = relays[relay]
        return pltpu.make_async_remote_copy(
            src_ref=outputs[index].at[block],
            dst_ref=wholes[relay].at[origin, block],
            send_sem=relay_sends.at[relay, block],
            recv_sem=relay_receives.at[relay, origin, block],
            device_id={"mat": place},
            device_id_type=MESH,
        )

    def kept(relay, block):
        index, place = relays[relay]
        return pltpu.make_async_copy(
            outputs[index].at[block], wholes[relay].at[place, block], relay_own.at[relay, block]
        )

    def relay_all(block):
        for relay, (_, place) in enumerate(relays):

            @pl.when(here != place)
            def _():
                relayed(relay, block, here).start()

            @pl.when(here == place)
            def _():
                kept(relay, block).start()

    def relay_end(block, _):
        for relay, (_, place) in enumerate(relays):

            @pl.when(here != place)
            def _():
                relayed(relay, block, here).wait_send()

            @pl.when(here == place)
            def _():
                kept(relay, block).wait()
                for origin in range(mats):
                    if origin != place:
                        relayed(relay, block, origin).wait_recv()

        return 0

    barrier = pltpu.get_barrier_semaphore()
    if everyone:

        def greet_all(lap, _):
            pl.semaphore_signal(
                barrier, inc=1, device_id=device((number + lap) % devices), device_id_type=MESH
            )
            return 0

        lax.fori_loop(1, devices, greet_all, 0)
        greeted = devices - 1
    else:
        greeted = line.greet(barrier)
    if relays and not everyone:

        def greet_mat(lap, _):
            pl.semaphore_signal(
                barrier, inc=1, device_id={"mat": (here + lap) % mats}, device_id_type=MESH
            )
            return 0

        lax.fori_loop(1, mats, greet_mat, 0)
        greeted = greeted + mats - 1
    own = [
        pltpu.make_async_copy(inputs[index], outputs[index].at[me], own_sem.at[index])
        for index in range(arrays)
    ]
    for copy in own:
        copy.start()
    pl.semaphore_wait(barrier, greeted)
    if everyone:

        def report_all(lap, _):
            report((number + lap) % devices, number).start()
            return 0

        lax.fori_loop(1, devices, report_all, 0)
        own_tally = pltpu.make_async_copy(tally, tallies.at[number], all_own)
        own_tally.start()
    line.begin()
    for copy in own:
        copy.wait()
    relay_all(me)

    def step(lap, _):
        line.forward(lap)

        @pl.when(lap > 1)
        def _():
            line.each(lap - 1, relay_all)

        return 0

    lax.fori_loop(1, line.outers, step, 0)
    line.take(line.outer)
    relay_all(line.across(line.outer))
    line.each(line.outers - 1, relay_all)
    line.end()
    if relays:
        lax.fori_loop(0, lax.axis_size("seq"), relay_end, 0)
    if everyone:

        def report_end(lap, _):
            before = (number + devices - lap) % devices
            report(before, before).wait_recv()
            report((number + lap) % devices, number).wait_send()
            return 0

        lax.fori_loop(1, devices, report_end, 0)
        own_tally.wait()


def gather_seq(values, identity, space=pltpu.VMEM, ahead=(), relays=(), everyone=()):
    peers = lax.axis_size("seq")
    mats = lax.axis_size("mat")
    plain = [value.shape for value in values]
    values = [
        value.reshape((2, -1) + value.shape[1:]) if value.shape[0] % 32 == 0 else value[None]
        for value in values
    ]
    shapes = [jax.ShapeDtypeStruct((peers,) + value.shape, value.dtype) for value in values]
    shapes += [
        jax.ShapeDtypeStruct((mats, peers) + values[index].shape, values[index].dtype)
        for index, _ in relays
    ]
    place = pl.BlockSpec(memory_space=space)
    unread = pl.BlockSpec(memory_space=pl.ANY)
    arrays, more = len(values), len(everyone)
    shapes[arrays:arrays] = [
        jax.ShapeDtypeStruct((peers * mats,) + value.shape, value.dtype) for value in everyone
    ]
    results = pl.pallas_call(
        functools.partial(gather_kernel, arrays, len(ahead), tuple(relays), bool(more)),
        out_shape=shapes,
        in_specs=[place] * (arrays + more) + [unread] * len(ahead),
        out_specs=[place] * (arrays + more) + [unread] * len(relays),
        scratch_shapes=line_semaphores(values)
        + [
            pltpu.SemaphoreType.DMA((arrays,)),
            pltpu.SemaphoreType.DMA((max(1, len(relays)), peers)),
            pltpu.SemaphoreType.DMA((max(1, len(relays)), mats, peers)),
            pltpu.SemaphoreType.DMA((max(1, len(relays)), peers)),
            pltpu.SemaphoreType.DMA((peers * mats,)),
            pltpu.SemaphoreType.DMA((peers * mats,)),
            pltpu.SemaphoreType.DMA,
        ],
        compiler_params=pltpu.CompilerParams(collective_id=identity, has_side_effects=True),
        name="gather_seq",
    )(*values, *everyone, *ahead)
    results = list(results)
    reported = results[arrays : arrays + more]
    del results[arrays : arrays + more]
    gathered = [result.reshape((peers,) + shape) for result, shape in zip(results, plain)]
    relayed = [
        result.reshape((mats, peers) + plain[index])
        for result, (index, _) in zip(results[arrays:], relays)
    ]
    return gathered + relayed + reported


def reduce_kernel(arrays, *refs):
    inputs, outputs = refs[:arrays], refs[arrays : 2 * arrays]
    got, keep = refs[2 * arrays : 3 * arrays], refs[3 * arrays : 4 * arrays]
    passes, arrivals, sends, receives = refs[4 * arrays :]
    outers = lax.axis_size("seq") // 2
    me = lax.axis_index("seq")
    outer, inner = me // 2, me % 2
    partner = {"seq": outer * 2 + 1 - inner}

    def hand(index, place):
        return pltpu.make_async_remote_copy(
            src_ref=inputs[index].at[place * 2 + 1 - inner],
            dst_ref=got[index].at[place],
            send_sem=passes.at[index, place],
            recv_sem=arrivals.at[index, place],
            device_id=partner,
            device_id_type=MESH,
        )

    def send(index, place, origin):
        return pltpu.make_async_remote_copy(
            src_ref=keep[index].at[place],
            dst_ref=outputs[index].at[origin],
            send_sem=sends.at[index, place],
            recv_sem=receives.at[index, origin],
            device_id={"seq": place * 2 + inner},
            device_id_type=MESH,
        )

    barrier = pltpu.get_barrier_semaphore()

    def greet(lap, _):
        pl.semaphore_signal(
            barrier,
            inc=1,
            device_id={"seq": ((outer + lap) % outers) * 2 + inner},
            device_id_type=MESH,
        )
        return 0

    pl.semaphore_signal(barrier, inc=1, device_id=partner, device_id_type=MESH)
    lax.fori_loop(1, outers, greet, 0)
    pl.semaphore_wait(barrier, outers)

    def begin(lap, _):
        for index in range(arrays):
            hand(index, (outer + 1 + lap) % outers).start()
        return 0

    lax.fori_loop(0, outers, begin, 0)

    def add(lap, _):
        place = (outer + 1 + lap) % outers
        for index in range(arrays):
            hand(index, place).wait_recv()
            total = inputs[index][place * 2 + inner].astype(F32) + got[index][place].astype(F32)
            keep[index][place] = total.astype(BF16)

            @pl.when(place != outer)
            def _():
                send(index, place, outer).start()

            @pl.when(place == outer)
            def _():
                outputs[index][outer] = total.astype(BF16)

        return 0

    lax.fori_loop(0, outers, add, 0)

    def end(lap, _):
        place = (outer + lap) % outers
        for index in range(arrays):
            hand(index, place).wait_send()

            @pl.when(place != outer)
            def _():
                send(index, place, place).wait_recv()
                send(index, place, outer).wait_send()

        return 0

    lax.fori_loop(0, outers, end, 0)


def reduce_seq(values, identity, ahead=()):
    outers = lax.axis_size("seq") // 2
    arrays = len(values)
    shapes = [(outers,) + value.shape[1:] for value in values]
    place = pl.BlockSpec(memory_space=pltpu.VMEM)
    unread = pl.BlockSpec(memory_space=pl.ANY)

    def body(*refs):
        reduce_kernel(arrays, *refs[:arrays], *refs[arrays + len(ahead) :])

    results = pl.pallas_call(
        body,
        out_shape=[jax.ShapeDtypeStruct(shape, BF16) for shape in shapes],
        in_specs=[place] * arrays + [unread] * len(ahead),
        out_specs=[place] * arrays,
        scratch_shapes=[pltpu.VMEM(shape, BF16) for shape in shapes * 2]
        + [pltpu.SemaphoreType.DMA((arrays, outers))] * 4,
        compiler_params=pltpu.CompilerParams(
            collective_id=identity, has_side_effects=True, vmem_limit_bytes=48 * 1024 * 1024
        ),
        name="reduce_seq",
    )(*values, *ahead)
    return [jnp.sum(result.astype(F32), axis=0) for result in results]


def lookup_kernel(
    ids, turned, small, out, smalls, table, found, give, got, keep, taken, passes, arrivals, sends,
    receives, small_sends, small_receives, small_own,
):
    outers, mats = taken.shape[0], taken.shape[1]
    me = lax.axis_index("seq")
    here = lax.axis_index("mat")
    outer, inner = me // 2, me % 2
    partner = {"seq": outer * 2 + 1 - inner}
    tokens = 256
    lanes = lax.broadcasted_iota(jnp.int32, (128, 128), 1)

    def device(to_outer, to_mat):
        return {"seq": to_outer * 2 + inner, "mat": to_mat}

    def hand(lap, place):
        return pltpu.make_async_remote_copy(
            src_ref=give.at[lap, place],
            dst_ref=got.at[lap, place],
            send_sem=passes.at[lap, place],
            recv_sem=arrivals.at[lap, place],
            device_id=partner,
            device_id_type=MESH,
        )

    def send(to_outer, to_mat, from_outer, from_mat):
        return pltpu.make_async_remote_copy(
            src_ref=keep.at[to_outer, to_mat],
            dst_ref=taken.at[from_outer, from_mat],
            send_sem=sends.at[to_outer, to_mat],
            recv_sem=receives.at[from_outer, from_mat],
            device_id=device(to_outer, to_mat),
            device_id_type=MESH,
        )

    def share(to_mat, from_mat):
        return pltpu.make_async_remote_copy(
            src_ref=small,
            dst_ref=smalls.at[from_mat],
            send_sem=small_sends.at[to_mat],
            recv_sem=small_receives.at[from_mat],
            device_id={"mat": to_mat},
            device_id_type=MESH,
        )

    own_small = pltpu.make_async_copy(small, smalls.at[here], small_own)
    own_small.start()
    barrier = pltpu.get_barrier_semaphore()

    def greet(lap, _):
        pl.semaphore_signal(
            barrier,
            inc=1,
            device_id=device((outer + lap // mats) % outers, (here + lap % mats) % mats),
            device_id_type=MESH,
        )
        return _

    pl.semaphore_signal(barrier, inc=1, device_id=partner, device_id_type=MESH)
    lax.fori_loop(1, outers * mats, greet, 0)
    pl.semaphore_wait(barrier, outers * mats)

    def share_start(lap, _):
        share((here + lap) % mats, here).start()
        return 0

    lax.fori_loop(1, mats, share_start, 0)
    for first in range(0, table.shape[0], VOCAB_TILE):
        table[first : first + VOCAB_TILE, :] = turned[:, first : first + VOCAB_TILE].T

    def find(block):
        def rows(index, _):
            for step in range(8):
                row = index * 8 + step
                entry = ids[block * mats * tokens + row]
                found[pl.ds(row, 1), :] = table[pl.ds(entry, 1), :]
            return 0

        lax.fori_loop(0, mats * tokens // 8, rows, 0)

    def store(target):
        for place in range(mats):
            base = place * tokens
            target[place, 0:tokens, :] = found[base : base + tokens, 0:128].astype(BF16)
            low = found[base : base + 128, 128:256]
            high = pltpu.roll(found[base + 128 : base + tokens, 128:256], 64, 1)
            target[place, tokens : tokens + 128, :] = jnp.where(lanes < 64, low, high).astype(BF16)

    def outer_of(lap):
        return (outer + 1 + lap) % outers

    def hand_over(lap):
        find(outer_of(lap) * 2 + 1 - inner)
        store(give.at[lap])
        for place in range(mats):
            hand(lap, place).start()

    def compute(lap, _):
        to_outer = outer_of(lap)

        @pl.when(lap + 1 < outers)
        def _():
            hand_over(lap + 1)

        find(to_outer * 2 + inner)
        store(keep.at[to_outer])
        for place in range(mats):
            hand(lap, place).wait_recv()
            keep[to_outer, place] = keep[to_outer, place] + got[lap, place]
            own = jnp.logical_and(to_outer == outer, place == here)

            @pl.when(jnp.logical_not(own))
            def _():
                send(to_outer, place, outer, here).start()

            @pl.when(own)
            def _():
                taken[outer, here] = keep[to_outer, place]

        return 0

    hand_over(0)
    lax.fori_loop(0, outers, compute, 0)

    def finish(lap, _):
        to_outer, to_mat = (outer + lap // mats) % outers, (here + lap % mats) % mats
        send(to_outer, to_mat, to_outer, to_mat).wait_recv()
        send(to_outer, to_mat, outer, here).wait_send()
        return _

    lax.fori_loop(1, outers * mats, finish, 0)

    def end(lap, _):
        for place in range(mats):
            hand(lap, place).wait_send()
        return 0

    lax.fori_loop(0, outers, end, 0)

    def share_end(lap, _):
        before = (here + mats - lap) % mats
        share(before, before).wait_recv()
        share((here + lap) % mats, here).wait_send()
        return 0

    lax.fori_loop(1, mats, share_end, 0)
    own_small.wait()
    for place in range(mats):

        def gather(source, total):
            return total + taken[source, place].astype(F32)

        out[place] = lax.fori_loop(0, outers, gather, jnp.zeros((384, 128), F32)).astype(BF16)


def lookup(ids, table, small, identity):
    outers, mats = lax.axis_size("seq") // 2, lax.axis_size("mat")
    part, entries = table.shape
    padded = (entries // VOCAB_TILE + 1) * VOCAB_TILE
    table = jnp.pad(table, ((0, 256 - part), (0, padded - entries)))
    table = table.astype(BF16).astype(F32)
    ids = jnp.where((ids >= 0) & (ids < entries), ids, entries)
    vmem = pl.BlockSpec(memory_space=pltpu.VMEM)
    blocks = pltpu.VMEM((outers, mats, 384, 128), BF16)
    return pl.pallas_call(
        lookup_kernel,
        out_shape=[
            jax.ShapeDtypeStruct((mats, 384, 128), BF16),
            jax.ShapeDtypeStruct((mats,) + small.shape, BF16),
        ],
        in_specs=[pl.BlockSpec(memory_space=pltpu.SMEM), vmem, vmem],
        out_specs=[vmem, vmem],
        scratch_shapes=[
            pltpu.VMEM((padded, 256), F32),
            pltpu.VMEM((mats * 256, 256), F32),
            blocks,
            blocks,
            blocks,
            blocks,
            *[pltpu.SemaphoreType.DMA((outers, mats))] * 4,
            pltpu.SemaphoreType.DMA((mats,)),
            pltpu.SemaphoreType.DMA((mats,)),
            pltpu.SemaphoreType.DMA,
        ],
        compiler_params=pltpu.CompilerParams(
            collective_id=identity, has_side_effects=True, vmem_limit_bytes=56 * 1024 * 1024
        ),
        name="lookup",
    )(ids, table, small)


def scatter_rows_kernel(
    entries, ids, rows, others, first_rider, second_rider, out, squares, whole, buffer, near, *rest
):
    line = Line([rows], [buffer], rest[: Line.SEMAPHORES])
    rider_sends, rider_receives, rider_own, near_own = rest[Line.SEMAPHORES :]
    places = lax.axis_size("mat")
    here = lax.axis_index("mat")
    riders = ((first_rider, UP_PLACE), (second_rider, DOWN_PLACE))

    def ride(rider, origin):
        source, place = riders[rider]
        return pltpu.make_async_remote_copy(
            src_ref=source,
            dst_ref=whole.at[origin],
            send_sem=rider_sends.at[rider],
            recv_sem=rider_receives.at[origin],
            device_id={"mat": place},
            device_id_type=MESH,
        )

    def stay(rider):
        source, place = riders[rider]
        return pltpu.make_async_copy(source, whole.at[place], rider_own)

    mats = rows.shape[0]
    lanes = lax.broadcasted_iota(jnp.int32, (128, 128), 1)
    nears = [
        pltpu.make_async_copy(source, near.at[rider], near_own.at[rider])
        for rider, (source, _) in enumerate(riders)
    ]
    for copy in nears:
        copy.start()

    def add(block, source):
        parts = []
        for place in range(mats):
            tail = source[place, 256:384, :].astype(F32)
            low = jnp.where(lanes < 64, tail, 0.0)
            high = jnp.where(lanes < 64, pltpu.roll(tail, 64, 1), 0.0)
            tails = jnp.concatenate([low, high], axis=0).astype(BF16)
            parts.append(jnp.concatenate([source[place, 0:256, :], tails], axis=1))
        values = jnp.concatenate(parts, axis=0)
        names = jnp.concatenate(
            [ids[pl.ds(block * 2 * mats + half, 1), :] for half in range(2 * mats)], axis=1
        )
        group = lax.shift_right_arithmetic(names, 7)
        spot = lax.broadcasted_iota(jnp.int32, (128, names.shape[1]), 0)
        hits = jnp.where(spot == jnp.bitwise_and(names, 127), 1.0, 0.0).astype(BF16)

        def piece(index, _):
            first = pl.multiple_of(index * VOCAB_TILE, VOCAB_TILE)
            masked = []
            for step in range(VOCAB_TILE // 128):
                chosen = jnp.where(group == index * (VOCAB_TILE // 128) + step, 1.0, 0.0)
                masked.append(hits * chosen.astype(BF16))
            out[pl.ds(first, VOCAB_TILE), :] += dot(
                jnp.concatenate(masked, axis=0), values, 1, 0
            )
            return 0

        lax.fori_loop(0, out.shape[0] // VOCAB_TILE, piece, 0)

    barrier = pltpu.get_barrier_semaphore()
    greeted = line.greet(barrier)

    def greet_mat(lap, _):
        pl.semaphore_signal(
            barrier, inc=1, device_id={"mat": (here + lap) % places}, device_id_type=MESH
        )
        return _

    lax.fori_loop(1, places, greet_mat, 0)
    pl.semaphore_wait(barrier, greeted + places - 1)
    line.begin()
    for rider, (_, place) in enumerate(riders):

        @pl.when(here != place)
        def _():
            ride(rider, here).start()

        @pl.when(here == place)
        def _():
            stay(rider).start()

    def use(block):
        add(block, buffer.at[block])

    part = others.shape[0]

    def fill(index, _):
        cut = pl.ds(pl.multiple_of(index * VOCAB_TILE, VOCAB_TILE), VOCAB_TILE)
        more = others[:, cut].astype(F32).T
        out[cut, :] = jnp.concatenate(
            [more, jnp.zeros((VOCAB_TILE, 256 - part), F32)], axis=1
        )
        return 0

    lax.fori_loop(0, out.shape[0] // VOCAB_TILE, fill, 0)
    add(line.block(line.outer), rows)

    def square(index, total):
        cut = pl.ds(pl.multiple_of(index * 64, 64), 64)
        for rider in range(len(riders)):
            values = near[rider, cut, :].astype(F32)
            values = jnp.sum(values * values, axis=0, keepdims=True)
            for lane in range(0, values.shape[1], 256):
                total = total + values[:, lane : lane + 256]
        return total

    for copy in nears:
        copy.wait()
    total = lax.fori_loop(0, near.shape[1] // 64, square, jnp.zeros((1, 256), F32))

    def step(lap, _):
        line.forward(lap)

        @pl.when(lap == 1)
        def _():
            line.take(line.outer)
            use(line.across(line.outer))

        @pl.when(lap > 1)
        def _():
            line.each(lap - 1, use)

        return 0

    lax.fori_loop(1, line.outers, step, 0)
    line.each(line.outers - 1, use)
    line.end()
    for rider, (_, place) in enumerate(riders):

        @pl.when(here != place)
        def _():
            ride(rider, here).wait_send()

        @pl.when(here == place)
        def _():
            stay(rider).wait()
            for origin in range(places):
                if origin != place:
                    ride(rider, origin).wait_recv()

    def finish(index, total):
        cut = pl.ds(pl.multiple_of(index * VOCAB_TILE, VOCAB_TILE), VOCAB_TILE)
        values = out[cut, :]
        entry = lax.broadcasted_iota(jnp.int32, values.shape, 0) + index * VOCAB_TILE
        values = jnp.where(entry < entries, values, 0.0)
        return total + jnp.sum(values * values, axis=0, keepdims=True)

    total = lax.fori_loop(0, out.shape[0] // VOCAB_TILE, finish, total)
    squares[...] = jnp.broadcast_to(total, (8, 256))


def scatter_rows(ids, rows, others, entries, identity, riders):
    peers = lax.axis_size("seq")
    mats = lax.axis_size("mat")
    padded = -(-entries // VOCAB_TILE) * VOCAB_TILE
    unread = pl.BlockSpec(memory_space=pl.ANY)
    place = pl.BlockSpec(memory_space=pltpu.VMEM)
    return pl.pallas_call(
        functools.partial(scatter_rows_kernel, entries),
        out_shape=[
            jax.ShapeDtypeStruct((padded, 256), F32),
            jax.ShapeDtypeStruct((8, 256), F32),
            jax.ShapeDtypeStruct((mats,) + riders[0].shape, BF16),
        ],
        in_specs=[place, place, place, unread, unread],
        out_specs=[place, place, unread],
        scratch_shapes=[
            pltpu.VMEM((peers,) + rows.shape, BF16),
            pltpu.VMEM((2,) + riders[0].shape, BF16),
            *line_semaphores([rows]),
            pltpu.SemaphoreType.DMA((2,)),
            pltpu.SemaphoreType.DMA((mats,)),
            pltpu.SemaphoreType.DMA,
            pltpu.SemaphoreType.DMA((2,)),
        ],
        compiler_params=pltpu.CompilerParams(
            collective_id=identity, has_side_effects=True, vmem_limit_bytes=48 * 1024 * 1024
        ),
        name="scatter_rows",
    )(ids, rows, jnp.pad(others, ((0, 0), (0, padded - entries))), *riders)


def swap_seq(value, identity, ahead=()):
    return exchange([value], [False], identity, ahead=ahead)[0]


def move_rows(value, steps):
    count = lax.axis_size("seq")
    leading, last = (max(0, -steps), min(count, count - steps))
    return lax.ppermute(value, "seq", [(source, source + steps) for source in range(leading, last)])


def normalize(values, gain):
    scale = lax.rsqrt(jnp.mean(values * values, axis=-1, keepdims=True) + 1e-05)
    hat = values * scale
    return hat * gain, hat, scale


def normalize_back(hat, scale, gain, grad):
    gain_grad = jnp.sum(grad * hat, axis=0)
    hat_grad = grad * gain
    return gain_grad, scale * (hat_grad - hat * jnp.mean(hat_grad * hat, axis=-1, keepdims=True))


def silu_back(values):
    sig = jax.nn.sigmoid(values)
    return sig * (1.0 + values * (1.0 - sig))


def padded_rows(flat):
    size = flat.shape[-1]
    room = -(-size // 16384) * 16384 - size
    flat = jnp.pad(flat, [(0, 0)] * (flat.ndim - 1) + [(0, room)])
    return flat.reshape(flat.shape[:-1] + (-1, 1024))


def pack_small(parts):
    return padded_rows(jnp.concatenate([part.astype(BF16).reshape(-1) for part in parts]))


def unpack_small(every, parts):
    every = every.reshape(every.shape[0], -1)
    result, offset = [], 0
    for part in parts:
        size = part.size
        result.append(every[:, offset : offset + size].reshape((-1,) + part.shape))
        offset += size
    return result


def columns(stacked):
    count, rows, width = stacked.shape
    return stacked.transpose(1, 0, 2).reshape(rows, count * width)


def step_grads(weights, embedded, route, lengths, slots, weight_mask, targets, loss_all):
    table, w_in, w_out, w_up, w_down, w_x, w_step, w_route, chan_low, gains_low = weights
    channel = chan_low.astype(F32)
    gains = gains_low.astype(F32)
    me = lax.axis_index("seq")
    count = lax.axis_size("seq")
    micros, tokens = route.shape
    inner = w_in.shape[1] // 2
    vocab_part = table.shape[1]
    first_pos = me * tokens
    vocab_start = me * vocab_part
    bounds = jnp.cumsum(lengths, axis=1)
    position = first_pos + jnp.arange(tokens, dtype=jnp.int32)
    opening = position[None, :, None] == bounds[:, None, :-1]
    keeping = 1.0 - jnp.logical_or(
        jnp.any(opening, axis=2), position[None] == 0
    ).astype(F32)
    place = me.astype(jnp.int32).reshape(1)

    x0 = embedded.astype(F32)

    u, hat0, scale0 = normalize(x0, gains[0])
    u_low = u.astype(BF16)
    xz = dot(u_low, w_in, 1, 0).reshape(micros, tokens, 2 * inner)
    z = xz[:, :, inner:]
    edge = move_rows(xz[:, tokens - (CONV - 1) :, :inner], 1)
    conv, act, projected = convolve(lengths, place, xz, edge, channel, w_x)
    rank_low = projected[:, :, :RANK].reshape(-1, RANK).astype(BF16)
    rate = -jnp.exp(channel[CONV + 3 :])
    wide = projected[:, :, :, None]
    wide_shape = (micros, tokens, STATES, 128)
    inject = jnp.broadcast_to(wide[:, :, RANK : RANK + STATES], wide_shape)
    readout = jnp.broadcast_to(wide[:, :, RANK + STATES :], wide_shape)
    pre, dt, ends, totals = scan_end(keeping, projected, w_step, channel, act, inject)
    ends_all, totals_all = gather_seq([ends, totals], 1)
    y, hs, start = scan_forward(
        place, keeping, dt, act, inject, readout, rate, ends_all, totals_all
    )
    skip = channel[CONV + 2]
    z_silu = jax.nn.silu(z)
    core = y + skip * act
    mixed_low = (core * z_silu).reshape(-1, inner).astype(BF16)
    x1 = x0 + dot(mixed_low, w_out, 1, 0)

    experts = w_route.shape[1]
    capacity = max(2, 2 * tokens // experts)
    local_experts = w_up.shape[0]
    s, hat1, scale1 = normalize(x1, gains[1])
    s_low = s.astype(BF16)
    scores = dot(s_low, w_route, 1, 0)
    chosen = route.reshape(-1)[:, None] == jnp.arange(experts, dtype=jnp.int32)[None, :]
    gate = jax.nn.sigmoid(jnp.sum(jnp.where(chosen, scores, 0.0), axis=1))
    onehot = chosen.astype(jnp.int32).reshape(micros, tokens, experts)
    ranking = jnp.sum(jnp.cumsum(onehot, axis=1) * onehot, axis=2) - 1
    placed = route * capacity + ranking
    all_slots = experts * capacity
    sender = (
        placed[:, None, :] == jnp.arange(all_slots, dtype=jnp.int32)[None, :, None]
    ).astype(BF16)

    def to_experts(rows, identity, ahead=()):
        sent = jnp.einsum(
            "mst,mtd->msd", sender, rows.reshape(micros, tokens, D), preferred_element_type=F32
        ).astype(BF16)
        sent = sent.reshape(micros, count, -1, D).transpose(1, 0, 2, 3).reshape(count, -1, D)
        arrived = swap_seq(sent, identity, ahead).reshape(count, micros, local_experts, capacity, D)
        return arrived.transpose(2, 0, 1, 3, 4).reshape(local_experts, -1, D)

    def from_experts(rows, identity, ahead=()):
        rows = rows.reshape(local_experts, count, micros, capacity, D).transpose(1, 2, 0, 3, 4)
        back = swap_seq(rows.reshape(count, -1, D), identity, ahead)
        back = back.reshape(count, micros, -1, D)
        back = back.transpose(1, 0, 2, 3).reshape(micros, all_slots, D)
        return jnp.einsum("mst,msd->mtd", sender, back, preferred_element_type=F32).reshape(-1, D)

    taken = to_experts(s_low, 2)
    hidden, slope, result = run_experts(taken, w_up, w_down)
    combined = from_experts(result, 3)
    x2 = x1 + gate[:, None] * combined

    final, hat2, scale2 = normalize(x2, gains[2])
    own_count = slots.shape[1]
    local_rows = slots - first_pos
    select = (
        local_rows[:, :, None] == jnp.arange(tokens, dtype=jnp.int32)[None, None, :]
    ).astype(BF16)
    picked_rows = jnp.einsum(
        "mst,mtd->msd",
        select,
        final.astype(BF16).reshape(micros, tokens, D),
        preferred_element_type=F32,
    ).astype(BF16)
    rows = gather_seq([picked_rows.reshape(-1, D)], 4)[0].reshape(count * micros * own_count, D)

    def by_device(values):
        return values.reshape(micros, count, own_count).transpose(1, 0, 2).reshape(-1)

    targets = by_device(targets)
    counted = by_device(weight_mask).astype(F32)
    limits = jnp.stack(
        [vocab_start, jnp.minimum(VOCAB_REAL - vocab_start, vocab_part), vocab_part]
    ).astype(jnp.int32)
    logits, stats = head(limits, rows, table, targets[:, None])
    stats = exchange([stats.T], [True], 5)[0]
    top = jnp.max(stats[:, 0], axis=0)
    lse = top + jnp.log(jnp.sum(stats[:, 1] * jnp.exp(stats[:, 0] - top[None]), axis=0))
    unweighted = lse - jnp.sum(stats[:, 2], axis=0)

    def own(values):
        return lax.dynamic_index_in_dim(
            values.reshape(count, micros, own_count), me, 0, keepdims=False
        )

    rows_here = own(unweighted)
    counted_here = own(counted)
    loss_here = jnp.sum(rows_here * counted_here)
    count_here = jnp.sum(counted_here)
    scalars = jnp.pad(jnp.stack([lse, counted / loss_all], axis=1), ((0, 0), (0, 6)))
    table_grad, rows_grad = head_back(limits, rows, table, targets[:, None], scalars, logits)
    rows_grad = rows_grad.reshape(count, -1, D)
    rows_grad = reduce_seq([rows_grad], 6)[0].reshape(micros, own_count, D)
    final_grad = jnp.einsum(
        "mst,msd->mtd",
        select.astype(F32),
        rows_grad,
        precision=lax.Precision.HIGHEST,
        preferred_element_type=F32,
    ).reshape(-1, D)
    gain_two, x2_grad = normalize_back(hat2, scale2, gains[2], final_grad)

    gate_grad = jnp.sum(x2_grad * combined, axis=1)
    out_grad = to_experts((gate[:, None] * x2_grad).astype(BF16), 7, [table_grad])
    up_grad, down_grad, taken_grad = run_experts_back(
        taken, out_grad, w_up, w_down, hidden, slope
    )
    s_table = scatter_mat(table_grad, 0)
    s_grad = from_experts(taken_grad, 8, [table_grad])
    score_grad = jnp.where(chosen, (gate_grad * gate * (1.0 - gate))[:, None], 0.0).astype(BF16)
    route_grad = dot(s_low, score_grad, 0, 0)
    s_grad = s_grad + dot(score_grad, w_route, 1, 1)
    gain_one, more = normalize_back(hat1, scale1, gains[1], s_grad)
    x1_grad = x2_grad + more

    x1_grad_low = x1_grad.astype(BF16)
    mixed_grad = dot(x1_grad_low, w_out, 1, 1).reshape(micros, tokens, inner)
    out_weight_grad = dot(mixed_low, x1_grad_low, 0, 0)
    y_grad = mixed_grad * z_silu
    z_grad = mixed_grad * core * silu_back(z)
    out_weight_grad = out_weight_grad.astype(BF16)
    up_grad, down_grad = hold([up_grad, down_grad], [s_table, out_weight_grad])
    s_up = scatter_mat(up_grad, 2)
    s_down = scatter_mat(down_grad, 1)
    s_out = scatter_mat(out_weight_grad, 0)
    starts_all = gather_seq(
        [scan_start(keeping, dt, y_grad, readout, rate, [out_weight_grad, up_grad, down_grad])], 9
    )[0]
    dt_grad, act_grad, inject_grad, readout_grad, rate_grad = scan_backward(
        place, keeping, dt, act, y_grad, inject, readout, rate, totals_all, starts_all, start, hs,
        [],
    )
    skip_grad = jnp.sum(y_grad * act, axis=(0, 1))
    pre_dt = dt_grad * jax.nn.sigmoid(pre)
    pre_dt_low = pre_dt.reshape(-1, inner).astype(BF16)
    step_weight_grad = dot(rank_low, pre_dt_low, 0, 0)
    projected_grad = jnp.concatenate(
        [
            dot(pre_dt_low, w_step, 1, 1),
            jnp.sum(inject_grad, axis=3).reshape(-1, STATES),
            jnp.sum(readout_grad, axis=3).reshape(-1, STATES),
        ],
        axis=1,
    ).astype(BF16)
    raw_grad, head_grad, x_weight_grad, conv_rows = convolve_back(
        lengths, place, xz, edge, channel, w_x, conv, act, act_grad, y_grad,
        projected_grad.reshape(micros, tokens, -1),
    )
    chan_grad = jnp.concatenate(
        [
            conv_rows[: CONV + 1],
            jnp.sum(pre_dt, axis=(0, 1))[None],
            skip_grad[None],
            jnp.sum(rate_grad, axis=0) * rate,
        ],
        axis=0,
    )
    edge_grad = move_rows(head_grad, -1)
    raw_grad = raw_grad + jnp.pad(
        edge_grad, ((0, 0), (tokens - (CONV - 1), 0), (0, 0))
    )
    xz_grad = jnp.concatenate([raw_grad, z_grad], axis=2).reshape(-1, 2 * inner).astype(BF16)
    in_grad = dot(u_low, xz_grad, 0, 0)
    gain_zero, more = normalize_back(hat0, scale0, gains[0], dot(xz_grad, w_in, 1, 1))
    x0_grad = (x1_grad + more).astype(BF16)
    grads = (
        s_table,
        scatter_mat(in_grad, 1),
        s_out,
        s_up,
        s_down,
        x_weight_grad,
        step_weight_grad,
        route_grad,
        chan_grad,
        jnp.stack([gain_zero, gain_one, gain_two]),
    )
    return grads, x0_grad, loss_here, count_here, rows_here


def scatter_mat(grad, dim):
    return lax.psum_scatter(grad.astype(BF16), "mat", scatter_dimension=dim, tiled=True)


def ortho_kernel(
    place, scale, moments, experts, inward, outward, out,
    moment, grads, current, rounded, gram, low, poly, slope, trace, semaphores,
):
    blocks, size, _ = experts.shape
    tile = TILE
    tiles = size // tile
    eye = lax.broadcasted_iota(jnp.int32, (tile, tile), 0) == lax.broadcasted_iota(
        jnp.int32, (tile, tile), 1
    )
    turned = jnp.logical_or(place[0] == DOWN_PLACE, place[0] == OUT_PLACE)

    def band(index):
        return pl.ds(index * tile, tile)

    fetch = pltpu.make_async_copy(moments, moment, semaphores.at[0])
    fetch.start()

    @pl.when(jnp.logical_or(place[0] == UP_PLACE, place[0] == DOWN_PLACE))
    def _():
        copy = pltpu.make_async_copy(experts, grads, semaphores.at[1])
        copy.start()
        copy.wait()

    @pl.when(place[0] == IN_PLACE)
    def _():
        copy = pltpu.make_async_copy(inward, grads, semaphores.at[1])
        copy.start()
        copy.wait()

    @pl.when(place[0] == OUT_PLACE)
    def _():
        rows = outward.shape[1]
        grads[:, rows:, :] = jnp.zeros((blocks, size - rows, size), BF16)
        copies = [
            pltpu.make_async_copy(
                outward.at[block], grads.at[block, pl.ds(0, rows)], semaphores.at[1 + block]
            )
            for block in range(blocks)
        ]
        for copy in copies:
            copy.start()
        for copy in copies:
            copy.wait()

    fetch.wait()
    trace[...] = jnp.zeros_like(trace)

    def load(lap, _):
        block, index = lap // tiles, lap % tiles
        rows = pl.ds(pl.multiple_of(index * tile, tile), tile)
        values = MOMENTUM * moment[block, rows, :].astype(F32)
        values = values + scale[0] * grads[block, rows, :].astype(F32)
        values = values.astype(BF16).astype(F32)
        trace[...] += jnp.sum(values * values, axis=0, keepdims=True)

        @pl.when(turned)
        def _():
            flipped = values.T
            current[block, :, rows] = flipped
            rounded[0, block, :, rows] = flipped.astype(BF16)

        @pl.when(jnp.logical_not(turned))
        def _():
            current[block, rows, :] = values
            rounded[0, block, rows, :] = values.astype(BF16)

        return 0

    lax.fori_loop(0, blocks * tiles, load, 0)
    total = jnp.sum(trace[...])
    factor = 1.0 / (jnp.sqrt(total + jnp.zeros((8, 128), F32)) + 1e-07)[0:1, 0:1]

    def sweep(step, gain):
        now = step % 2

        diagonal = []
        for index in range(tiles):
            total = jnp.zeros((tile, size - index * tile), F32)
            for block in range(blocks):
                total = total + dot(
                    rounded[now, block, band(index), :],
                    rounded[now, block, index * tile :, :],
                    1,
                    1,
                )
            total = total * gain
            corner = total[:, :tile]
            own = jnp.where(eye, corner, 0.0)
            diagonal.append(jnp.sum(own, axis=0, keepdims=True))
            slope[band(index), :] = jnp.broadcast_to(
                jnp.sum(own, axis=1, keepdims=True), (tile, 128)
            )
            gram[band(index), index * tile :] = total
            low[band(index), band(index)] = (corner - own).astype(BF16)
            for other in range(index + 1, tiles):
                part = total[:, (other - index) * tile : (other - index + 1) * tile]
                flipped = part.T
                low[band(index), band(other)] = part.astype(BF16)
                gram[band(other), band(index)] = flipped
                low[band(other), band(index)] = flipped.astype(BF16)

        for index in range(tiles):
            product = dot(low[band(index), :], low[...], 1, 0)
            own = spread(slope[band(index), :], tile)
            for other in range(tiles):
                values = gram[band(index), band(other)]
                sums = own + diagonal[other]
                total = (COEF_B + COEF_C * sums) * values
                total = total + COEF_C * product[:, other * tile : (other + 1) * tile]
                if other == index:
                    total = jnp.where(eye, total - COEF_C * values * values, total)
                    part = jnp.sum(jnp.where(eye, total, 0.0), axis=1, keepdims=True)
                    total = jnp.where(eye, 0.0, total)
                poly[band(index), band(other)] = total.astype(BF16)
            slope[band(index), :] = jnp.broadcast_to(part + COEF_A, (tile, 128))

        def advance(lap, _):
            block, index = lap // tiles, lap % tiles
            rows = pl.ds(pl.multiple_of(index * tile, tile), tile)
            scaled = spread(slope[rows, :], size) * current[block, rows, :]
            values = scaled + dot(poly[rows, :], rounded[now, block], 1, 0)
            current[block, rows, :] = values
            rounded[1 - now, block, rows, :] = values.astype(BF16)
            return 0

        def advance_first(lap, _):
            block, index = lap // tiles, lap % tiles
            rows = pl.ds(pl.multiple_of(index * tile, tile), tile)
            scaled = spread(slope[rows, :], size) * current[block, rows, :]
            values = (scaled + dot(poly[rows, :], rounded[now, block], 1, 0)) * factor
            current[block, rows, :] = values
            rounded[1 - now, block, rows, :] = values.astype(BF16)
            return 0

        @pl.when(step == 0)
        def _():
            lax.fori_loop(0, blocks * tiles, advance_first, 0)

        @pl.when(step > 0)
        def _():
            lax.fori_loop(0, blocks * tiles, advance, 0)

        return jnp.ones_like(gain)

    lax.fori_loop(0, ORTHO_STEPS, sweep, factor * factor)

    def store(lap, _):
        block, index = lap // tiles, lap % tiles
        rows = pl.ds(pl.multiple_of(index * tile, tile), tile)

        @pl.when(turned)
        def _():
            out[block, :, rows] = current[block, rows, :].T.astype(BF16)

        @pl.when(jnp.logical_not(turned))
        def _():
            out[block, rows, :] = current[block, rows, :].astype(BF16)

        return 0

    lax.fori_loop(0, blocks * tiles, store, 0)


def orthogonalize(scale, moments, experts, inward, outward):
    blocks, size, width = experts.shape
    vmem = pl.BlockSpec(memory_space=pltpu.VMEM)
    smem = pl.BlockSpec(memory_space=pltpu.SMEM)
    unread = pl.BlockSpec(memory_space=pl.ANY)
    place = lax.axis_index("mat").astype(jnp.int32).reshape(1)
    return pl.pallas_call(
        ortho_kernel,
        out_shape=jax.ShapeDtypeStruct(experts.shape, BF16),
        in_specs=[smem, smem] + [unread] * 4,
        out_specs=vmem,
        scratch_shapes=[
            pltpu.VMEM((blocks, size, width), BF16),
            pltpu.VMEM((blocks, size, width), BF16),
            pltpu.VMEM((blocks, size, width), F32),
            pltpu.VMEM((2, blocks, size, width), BF16),
            pltpu.VMEM((size, size), F32),
            pltpu.VMEM((size, size), BF16),
            pltpu.VMEM((size, size), BF16),
            pltpu.VMEM((size, 128), F32),
            pltpu.VMEM((1, size), F32),
            pltpu.SemaphoreType.DMA((1 + blocks,)),
        ],
        compiler_params=pltpu.CompilerParams(vmem_limit_bytes=56 * 1024 * 1024),
        name="orthogonalize",
    )(place, scale.reshape(1), moments, experts, inward, outward)


def adamw_update(weight, mean, square, grad, rate, decay):
    mean = BETA_ONE * mean + (1.0 - BETA_ONE) * grad
    square = BETA_TWO * square + (1.0 - BETA_TWO) * grad * grad
    ratio = (
        mean
        / (1.0 - BETA_ONE**STEP_COUNT)
        / (jnp.sqrt(square / (1.0 - BETA_TWO**STEP_COUNT)) + ADAM_EPS)
    )
    return (weight * (1.0 - rate * decay) - rate * ratio, mean, square)


def table_kernel(scale, grad, weight, mean, square, _ahead, new_weight, new_mean, new_square):
    part = weight.shape[0]
    turned = grad[...].T[:part] * scale[0]
    results = adamw_update(weight[...], mean[...], square[...], turned, 0.05, 0.1)
    new_weight[...], new_mean[...], new_square[...] = results


def update_table(scale, grad, weight, mean, square, ahead):
    part, entries = weight.shape
    flat = pl.BlockSpec((part, VOCAB_TILE), lambda i: (0, i))
    return pl.pallas_call(
        table_kernel,
        grid=(-(-entries // VOCAB_TILE),),
        in_specs=[
            pl.BlockSpec(memory_space=pltpu.SMEM),
            pl.BlockSpec((VOCAB_TILE, 256), lambda i: (i, 0)),
            flat,
            flat,
            flat,
            pl.BlockSpec(memory_space=pl.ANY),
        ],
        out_specs=[flat] * 3,
        out_shape=[jax.ShapeDtypeStruct(weight.shape, F32)] * 3,
        compiler_params=kernel_params(),
        cost_estimate=pl.CostEstimate(
            flops=20 * entries * 256,
            bytes_accessed=7 * entries * 256 * 4,
            transcendentals=2 * entries * 256,
        ),
        name="update_table",
    )(scale.reshape(1), grad, weight, mean, square, ahead)


def local(
    token_ids,
    expert_route,
    doc_lengths,
    loss_slots,
    loss_weight,
    target_ids,
    embedding,
    embedding_mom,
    embedding_sq,
    in_project,
    in_project_mom,
    out_project,
    out_project_mom,
    expert_up,
    expert_up_mom,
    expert_down,
    expert_down_mom,
    x_project,
    x_project_mom,
    x_project_sq,
    step_project,
    step_project_mom,
    step_project_sq,
    router_weight,
    router_mom,
    router_sq,
    channel_param,
    channel_mom,
    channel_sq,
    norm_gains,
    gains_mom,
    gains_sq,
):
    micros = token_ids.shape[0]
    mats = lax.axis_size("mat")
    seq_count = lax.axis_size("seq")
    tokens = expert_route.shape[2]
    vocab_part, part = embedding.shape
    ids = exchange([token_ids.reshape(-1, 128)], [True], 12, ("mat",))[0]
    ids = ids.reshape(mats, micros, seq_count, tokens)
    ids = ids.transpose(2, 0, 1, 3).reshape(-1) - lax.axis_index("seq") * vocab_part
    parts = [x_project, step_project, router_weight, channel_param, norm_gains]
    found, small = lookup(ids, embedding.T, pack_small(parts), 10)
    found, w_table, w_out, w_up, w_down = lax.optimization_barrier(
        (
            found,
            embedding.T.astype(BF16),
            out_project.astype(BF16),
            expert_up.astype(BF16),
            expert_down.astype(BF16),
        )
    )
    small = unpack_small(small, parts)
    weights = (
        lax.all_gather(w_table, "mat", axis=0, tiled=True),
        lax.all_gather(in_project.astype(BF16), "mat", axis=1, tiled=True),
        lax.all_gather(w_out, "mat", axis=0, tiled=True),
        lax.all_gather(w_up, "mat", axis=2, tiled=True),
        lax.all_gather(w_down, "mat", axis=1, tiled=True),
        small[0].reshape(-1, small[0].shape[2]),
        columns(small[1]),
        small[2].reshape(-1, small[2].shape[2]),
        columns(small[3]),
        columns(small[4]),
    )
    half = micros * tokens // 2
    tails = found[:, 2 * half :].reshape(mats, half, 2, part - 128).transpose(0, 2, 1, 3)
    heads = found[:, : 2 * half].reshape(mats, 2, half, 128)
    embedded = jnp.concatenate([heads, tails], axis=3).transpose(1, 2, 0, 3)
    embedded = embedded.reshape(micros * tokens, mats * part)
    loss_all = micros * lax.axis_size("mat") * loss_weight.shape[2]
    moments = jnp.stack(
        [
            expert_up_mom[0],
            in_project_mom,
            expert_down_mom[0],
            jnp.pad(out_project_mom, ((0, D - out_project_mom.shape[0]), (0, 0))),
        ]
    ).astype(BF16)
    moments = lax.all_to_all(moments, "mat", split_axis=0, concat_axis=0, tiled=True)
    grads, x0_grad, loss_part, count_part, rows_here = step_grads(
        weights,
        embedded,
        expert_route[:, 0, :, 0],
        doc_lengths[:, 0],
        loss_slots[:, 0],
        loss_weight[:, 0],
        target_ids[:, 0],
        loss_all,
    )
    row_loss = rows_here[:, None, :]
    s_table, s_in, s_out, s_up, s_down, g_x, g_step, g_route, g_chan, g_gain = grads
    pieces = (
        g_x.reshape(mats, -1),
        g_step.reshape(g_step.shape[0], mats, -1).transpose(1, 0, 2).reshape(mats, -1),
        g_route.reshape(mats, -1),
        g_chan.reshape(g_chan.shape[0], mats, -1).transpose(1, 0, 2).reshape(mats, -1),
        g_gain.reshape(g_gain.shape[0], mats, -1).transpose(1, 0, 2).reshape(mats, -1),
    )
    packed = jnp.concatenate(pieces, axis=1)
    unit = seq_count * 2048
    packed = jnp.pad(packed, ((0, 0), (0, -packed.shape[1] % unit)))
    packed = packed.astype(BF16).reshape(mats, -1, 128)
    x0_parts = x0_grad.reshape(2, -1, mats, part).transpose(2, 0, 1, 3)
    x0_heads = x0_parts[..., :128].reshape(mats, -1, 128)
    x0_tails = jnp.concatenate([x0_parts[:, 0, :, 128:], x0_parts[:, 1, :, 128:]], axis=2)
    x0_heads, moments = lax.optimization_barrier((x0_heads, moments))
    x0_rows = 3 * micros * tokens // 2
    mixed = lax.all_to_all(
        jnp.concatenate([x0_heads, x0_tails, packed], axis=1),
        "mat",
        split_axis=0,
        concat_axis=0,
        tiled=True,
    )
    packed = jnp.sum(mixed[:, x0_rows:].astype(F32), axis=0).astype(BF16)
    g_table, table_squares, whole_experts = scatter_rows(
        ids.reshape(-1, 128),
        mixed[:, :x0_rows],
        s_table,
        vocab_part,
        13,
        [s_up[0], s_down[0]],
    )
    s_in, s_out, packed = reduce_seq(
        [
            s_in.reshape(seq_count, -1, D),
            s_out.reshape(seq_count, -1, D),
            packed.reshape(seq_count, -1, 128),
        ],
        14,
        [g_table],
    )
    s_up = s_up.astype(F32)
    s_down = s_down.astype(F32)
    squares = sum(jnp.sum(g * g) for g in (s_in, s_out, packed))
    squares = squares + jnp.sum(table_squares[0])
    tallies = jnp.stack([squares, loss_part, count_part])
    tallies = jnp.broadcast_to(jnp.pad(tallies, (0, 5))[:, None], (8, 128))
    g_in, g_out, packed, whole_in, whole_out, totals = gather_seq(
        [s_in.astype(BF16), s_out.astype(BF16), packed.astype(BF16)],
        15,
        relays=[(0, IN_PLACE), (1, OUT_PLACE)],
        everyone=[tallies],
    )
    g_in = g_in.reshape(-1, D).astype(F32)
    g_out = g_out.reshape(-1, D).astype(F32)
    totals = jnp.sum(totals[:, :, 0], axis=0)
    squares, loss_total, loss_count = totals[0], totals[1], totals[2]
    grad_norm = jnp.sqrt(squares)
    scale = jnp.minimum(1.0, CLIP_NORM / (grad_norm + 1e-06))
    mom_in = MOMENTUM * in_project_mom + g_in * scale
    mom_out = MOMENTUM * out_project_mom + g_out * scale
    mom_up = MOMENTUM * expert_up_mom + s_up * scale
    mom_down = MOMENTUM * expert_down_mom + s_down * scale
    ortho = orthogonalize(
        scale,
        moments,
        whole_experts,
        whole_in.reshape(mats, D, -1),
        whole_out.reshape(mats, -1, D),
    )
    packed, ortho = lax.optimization_barrier((packed, ortho))
    packed = packed.reshape(-1).astype(F32)
    shards, offset = [], 0
    for piece, like in zip(
        pieces, (x_project, step_project, router_weight, channel_param, norm_gains)
    ):
        shards.append(packed[offset : offset + piece.shape[1]].reshape(like.shape))
        offset += piece.shape[1]
    table_new = update_table(
        scale, g_table, embedding.T, embedding_mom.T, embedding_sq.T, ortho
    )
    table_new = [values.T for values in table_new]
    ortho = lax.all_to_all(ortho, "mat", split_axis=0, concat_axis=0, tiled=True)
    shrink = 1.0 - LR_MUON * DECAY_MUON
    new_up = expert_up * shrink - LR_MUON * 0.2 * math.sqrt(max(D, FF)) * ortho[UP_PLACE][None].astype(F32)
    new_in = in_project * shrink - LR_MUON * 0.2 * math.sqrt(max(D, 2 * DI)) * ortho[IN_PLACE].astype(F32)
    new_down = (
        expert_down * shrink - LR_MUON * 0.2 * math.sqrt(max(D, FF)) * ortho[DOWN_PLACE][None].astype(F32)
    )
    new_out = (
        out_project * shrink
        - LR_MUON * 0.2 * math.sqrt(max(D, DI)) * ortho[OUT_PLACE, : out_project.shape[0]].astype(F32)
    )
    x_new = adamw_update(x_project, x_project_mom, x_project_sq, shards[0] * scale, 0.06, 0.1)
    step_new = adamw_update(
        step_project, step_project_mom, step_project_sq, shards[1] * scale, 0.06, 0.1
    )
    route_new = adamw_update(router_weight, router_mom, router_sq, shards[2] * scale, 0.06, 0.1)
    chan_new = adamw_update(channel_param, channel_mom, channel_sq, shards[3] * scale, 1.0, 0.0)
    gains_new = adamw_update(norm_gains, gains_mom, gains_sq, shards[4] * scale, 0.4, 0.0)
    return (
        loss_total,
        loss_count,
        grad_norm,
        row_loss,
        *table_new,
        new_in,
        mom_in,
        new_out,
        mom_out,
        new_up,
        mom_up,
        new_down,
        mom_down,
        *x_new,
        *step_new,
        *route_new,
        *chan_new,
        *gains_new,
    )


def solution(mesh):
    in_specs = (
        P(None, "mat", None),
        P(None, "mat", "seq", None),
        P(None, "mat", None),
        P(None, "mat", "seq"),
        P(None, "mat", None),
        P(None, "mat", None),
        P("seq", "mat"),
        P("seq", "mat"),
        P("seq", "mat"),
        P(None, "mat"),
        P(None, "mat"),
        P("mat", None),
        P("mat", None),
        P("seq", None, "mat"),
        P("seq", None, "mat"),
        P("seq", "mat", None),
        P("seq", "mat", None),
        P("mat", None),
        P("mat", None),
        P("mat", None),
        P(None, "mat"),
        P(None, "mat"),
        P(None, "mat"),
        P("mat", None),
        P("mat", None),
        P("mat", None),
        P(None, "mat"),
        P(None, "mat"),
        P(None, "mat"),
        P(None, "mat"),
        P(None, "mat"),
        P(None, "mat"),
    )
    out_specs = (
        P(),
        P(),
        P(),
        P(None, "mat", "seq"),
        P("seq", "mat"),
        P("seq", "mat"),
        P("seq", "mat"),
        P(None, "mat"),
        P(None, "mat"),
        P("mat", None),
        P("mat", None),
        P("seq", None, "mat"),
        P("seq", None, "mat"),
        P("seq", "mat", None),
        P("seq", "mat", None),
        P("mat", None),
        P("mat", None),
        P("mat", None),
        P(None, "mat"),
        P(None, "mat"),
        P(None, "mat"),
        P("mat", None),
        P("mat", None),
        P("mat", None),
        P(None, "mat"),
        P(None, "mat"),
        P(None, "mat"),
        P(None, "mat"),
        P(None, "mat"),
        P(None, "mat"),
    )
    return jax.shard_map(local, mesh=mesh, in_specs=in_specs, out_specs=out_specs, check_vma=False)
```

```python
import functools
import math

import jax
import jax.numpy as jnp
from jax import lax
from jax.experimental import pallas as pl
from jax.experimental.pallas import tpu as pltpu
from jax.sharding import PartitionSpec as P

D = 768
DI = 1536
FF = 3072
VOCAB_REAL = 50257
CONV = 4
ORTHO_STEPS = 5
STEP_COUNT = 10
STATES = 16
RANK = 48

CLIP_NORM = 0.004
COEF_A = 3.4445
COEF_B = -4.775
COEF_C = 2.0315
MOMENTUM = 0.95
LR_MUON = 0.2
DECAY_MUON = 0.01
BETA_ONE = 0.9
BETA_TWO = 0.95
ADAM_EPS = 1e-08
F32 = jnp.float32
BF16 = jnp.bfloat16
LANES = 512
UNROLL = 8
TILE = 256
VOCAB_TILE = 640
UP_PLACE, IN_PLACE, DOWN_PLACE, OUT_PLACE = 0, 1, 2, 3
TOTAL_ROWS = 8
PAD = 8
HIDDEN = 512
MESH = pl.DeviceIdType.MESH


def dot(left, right, left_dim, right_dim, **kw):
    return lax.dot_general(
        left, right, (((left_dim,), (right_dim,)), ((), ())), preferred_element_type=F32, **kw
    )


def spread(values, width):
    return jnp.concatenate([values] * (width // 128), axis=1)


def same_document(lengths, place, micro, tokens, width):
    position = place[0] * tokens + lax.broadcasted_iota(jnp.int32, (tokens, 128), 0)
    bounds, bound = [], 0
    for index in range(lengths.shape[1] - 1):
        bound = bound + lengths[micro, index]
        bounds.append(bound)
    masks = []
    for tap in range(CONV):
        source = position - (CONV - 1) + tap
        inside = source >= 0
        for bound in bounds:
            inside = jnp.logical_and(inside, (source >= bound) == (position >= bound))
        masks.append(spread(jnp.where(inside, 1.0, 0.0), width))
    return masks


def fill_padded(padded, edge, raw):
    padded[PAD - (CONV - 1) : PAD, :] = edge[0]
    padded[PAD:, :] = raw[0]


def conv_kernel(lengths, place, raw, edge, channel, w_x, conv_out, act_out, projected, padded):
    micro, group = pl.program_id(0), pl.program_id(1)
    tokens, width = raw.shape[1], raw.shape[2]
    fill_padded(padded, edge, raw)
    masks = same_document(lengths, place, micro, tokens, width)
    conv = jnp.broadcast_to(channel[CONV : CONV + 1, :], (tokens, width))
    for tap in range(CONV):
        shifted = padded[pl.ds(PAD - (CONV - 1) + tap, tokens), :]
        conv = conv + channel[tap : tap + 1, :] * shifted * masks[tap]
    act = conv * lax.logistic(conv)
    conv_out[0] = conv
    act_out[0] = act

    @pl.when(group == 0)
    def _():
        projected[...] = jnp.zeros_like(projected)

    projected[0] += dot(act.astype(BF16), w_x[...], 1, 0)


def conv_back_kernel(
    lengths, place, raw, edge, channel, w_x, conv, act, act_grad, y_grad, projected_grad,
    raw_out, head_out, x_out, rows_out, padded, total,
):
    micro = pl.program_id(1)
    tokens, width = raw.shape[1], raw.shape[2]
    fill_padded(padded, edge, raw)
    masks = same_document(lengths, place, micro, tokens, width)
    grad = act_grad[0] + y_grad[0] * channel[CONV + 2 : CONV + 3, :]
    grad = grad + dot(projected_grad[0], w_x[...], 1, 1)
    values = conv[0]
    sig = lax.logistic(values)
    grad = grad * (sig * (1.0 + values * (1.0 - sig)))

    @pl.when(micro == 0)
    def _():
        x_out[...] = jnp.zeros_like(x_out)
        rows_out[...] = jnp.zeros_like(rows_out)

    x_out[...] += dot(act[0].astype(BF16), projected_grad[0], 0, 0)
    total[...] = jnp.zeros_like(total)
    for tap in range(CONV):
        span = pl.ds(PAD - (CONV - 1) + tap, tokens)
        kept = grad * masks[tap]
        rows_out[tap : tap + 1, :] += jnp.sum(kept * padded[span, :], axis=0, keepdims=True)
        total[span, :] += channel[tap : tap + 1, :] * kept
    rows_out[CONV : CONV + 1, :] += jnp.sum(grad, axis=0, keepdims=True)
    raw_out[0] = total[PAD:, :]
    head_out[0] = total[PAD - (CONV - 1) : PAD, :]


def end_kernel(keep, projected, w_step, channel, act, inject, pre_out, dt_out, out, totals):
    micro = pl.program_id(1)
    micros = pl.num_programs(1)
    tokens, width = act.shape[1], act.shape[2]
    rates = -jnp.exp(channel[CONV + 3 :, :])
    pre = dot(projected[0][:, :RANK].astype(BF16), w_step[...], 1, 0)
    pre = pre + channel[CONV + 1 : CONV + 2, :]
    step_size = jnp.maximum(pre, 0.0) + jnp.log1p(jnp.exp(-jnp.abs(pre)))
    pre_out[0] = pre
    dt_out[0] = step_size

    def block(step, carry):
        state, alive = carry
        for inner in range(UNROLL):
            t = step * UNROLL + inner
            d = dt_out[0, pl.ds(t, 1), :]
            w = d * act[0, pl.ds(t, 1), :]
            k = keep[micro, t]
            state = jnp.exp(rates * d) * k * state + spread(inject[0, t], width) * w
            alive = alive * k
        return state, alive

    state, alive = lax.fori_loop(
        0, tokens // UNROLL, block, (jnp.zeros((STATES, width), F32), jnp.float32(1.0))
    )
    out[...] = state.astype(BF16)

    @pl.when(micro == 0)
    def _():
        totals[...] = jnp.zeros_like(totals)

    totals[pl.ds(micro, 1), :] = jnp.sum(step_size, axis=0, keepdims=True)
    totals[pl.ds(micros + micro, 1), :] = jnp.zeros((1, width), F32) + alive


def forward_kernel(
    place, keep, dt, act, inject, readout, rate, ends, totals, y_out, h_out, start_out
):
    micro = pl.program_id(0)
    micros = pl.num_programs(0)
    tokens, width = dt.shape[1], dt.shape[2]
    rates = rate[...]
    me = place[0]

    def fold(source, state):
        total = totals[source, pl.ds(micro, 1), :]
        alive = totals[source, pl.ds(micros + micro, 1), :]
        return jnp.exp(rates * total) * alive * state + ends[source].astype(F32)

    state = lax.fori_loop(0, me, fold, jnp.zeros((STATES, width), F32))
    start_out[0] = state

    def block(step, state):
        for inner in range(UNROLL):
            t = step * UNROLL + inner
            d = dt[0, pl.ds(t, 1), :]
            w = d * act[0, pl.ds(t, 1), :]
            state = jnp.exp(rates * d) * keep[micro, t] * state + spread(inject[0, t], width) * w
            h_out[0, t] = state
            y_out[0, pl.ds(t, 1), :] = jnp.sum(
                spread(readout[0, t], width) * state, axis=0, keepdims=True
            )
        return state

    lax.fori_loop(0, tokens // UNROLL, block, state)


def start_kernel(keep, dt, dy, readout, rate, out):
    micro = pl.program_id(0)
    tokens, width = dt.shape[1], dt.shape[2]
    rates = rate[...]

    def block(step, state):
        for inner in range(UNROLL):
            t = tokens - 1 - (step * UNROLL + inner)
            d = dt[0, pl.ds(t, 1), :]
            state = state + spread(readout[0, t], width) * dy[0, pl.ds(t, 1), :]
            state = jnp.exp(rates * d) * keep[micro, t] * state
        return state

    state = lax.fori_loop(0, tokens // UNROLL, block, jnp.zeros((STATES, width), F32))
    out[...] = state.astype(BF16)


def backward_kernel(
    place,
    keep,
    dt,
    act,
    dy,
    inject,
    readout,
    rate,
    totals,
    starts,
    start,
    hs,
    ddt_out,
    da_out,
    db_out,
    dc_out,
    drate_out,
):
    micro = pl.program_id(0)
    micros = pl.num_programs(0)
    group = pl.program_id(1)
    tokens, width = dt.shape[1], dt.shape[2]
    rates = rate[...]
    me = place[0]
    count = totals.shape[0]

    def fold(lap, state):
        source = count - 1 - lap
        total = totals[source, pl.ds(micro, 1), :]
        alive = totals[source, pl.ds(micros + micro, 1), :]
        return jnp.exp(rates * total) * alive * state + starts[source].astype(F32)

    grad = lax.fori_loop(0, count - 1 - me, fold, jnp.zeros((STATES, width), F32))

    @pl.when(group == 0)
    def _():
        db_out[...] = jnp.zeros_like(db_out)
        dc_out[...] = jnp.zeros_like(dc_out)

    def gather_lanes(values):
        total = values[:, 0:128]
        for tile in range(1, width // 128):
            total = total + values[:, tile * 128 : (tile + 1) * 128]
        return total

    def one(t, before, carry):
        grad, drate, state = carry
        d = dt[0, pl.ds(t, 1), :]
        x = act[0, pl.ds(t, 1), :]
        g_y = dy[0, pl.ds(t, 1), :]
        w = d * x
        grad = grad + spread(readout[0, t], width) * g_y
        db_out[0, t] += gather_lanes(grad * w)
        dc_out[0, t] += gather_lanes(state * g_y)
        dw = jnp.sum(grad * spread(inject[0, t], width), axis=0, keepdims=True)
        grad = jnp.exp(rates * d) * keep[micro, t] * grad
        effect = grad * before
        drate = drate + effect * d
        ddt_out[0, pl.ds(t, 1), :] = (
            jnp.sum(effect * rates, axis=0, keepdims=True) + dw * x
        )
        da_out[0, pl.ds(t, 1), :] = dw * d
        return grad, drate, before

    def block(step, carry):
        for inner in range(UNROLL):
            t = tokens - 1 - (step * UNROLL + inner)
            carry = one(t, hs[0, t - 1], carry)
        return carry

    carry = (grad, jnp.zeros((STATES, width), F32), hs[0, tokens - 1])
    carry = lax.fori_loop(0, tokens // UNROLL - 1, block, carry)
    for t in range(UNROLL - 1, -1, -1):
        carry = one(t, hs[0, t - 1] if t else start[0], carry)
    drate_out[0] = carry[1]


def specs(tokens, seq_count):
    rows = pl.BlockSpec((1, tokens, LANES), lambda m, g: (m, 0, g))
    wide = pl.BlockSpec((1, tokens, STATES, 128), lambda m, g: (m, 0, 0, 0))
    rate = pl.BlockSpec((STATES, LANES), lambda m, g: (0, g))
    state = pl.BlockSpec((1, STATES, LANES), lambda m, g: (m, 0, g))
    edge = pl.BlockSpec((STATES, LANES), lambda m, g: (m, g))
    edges = pl.BlockSpec((seq_count, STATES, LANES), lambda m, g: (0, m, g))
    totals = pl.BlockSpec((seq_count, TOTAL_ROWS, LANES), lambda m, g: (0, 0, g))
    every = pl.BlockSpec((1, tokens, STATES, LANES), lambda m, g: (m, 0, 0, g))
    scalars = pl.BlockSpec(memory_space=pltpu.SMEM)
    return rows, wide, rate, state, edge, edges, totals, every, scalars


def kernel_params():
    return pltpu.CompilerParams(vmem_limit_bytes=48 * 1024 * 1024)


def convolve(lengths, place, xz, edge, channel, w_x):
    micros, tokens, inner = xz.shape[0], xz.shape[1], xz.shape[2] // 2
    scalars = pl.BlockSpec(memory_space=pltpu.SMEM)
    rows = pl.BlockSpec((1, tokens, LANES), lambda m, g: (m, 0, g))
    shape = jax.ShapeDtypeStruct((micros, tokens, inner), F32)
    columns_x = w_x.shape[1]
    return pl.pallas_call(
        conv_kernel,
        grid=(micros, inner // LANES),
        in_specs=[
            scalars,
            scalars,
            rows,
            pl.BlockSpec((1, CONV - 1, LANES), lambda m, g: (m, 0, g)),
            pl.BlockSpec((channel.shape[0], LANES), lambda m, g: (0, g)),
            pl.BlockSpec((LANES, columns_x), lambda m, g: (g, 0)),
        ],
        out_specs=[rows, rows, pl.BlockSpec((1, tokens, columns_x), lambda m, g: (m, 0, 0))],
        out_shape=[shape, shape, jax.ShapeDtypeStruct((micros, tokens, columns_x), F32)],
        scratch_shapes=[pltpu.VMEM((PAD + tokens, LANES), F32)],
        compiler_params=kernel_params(),
        name="mixer_conv",
    )(lengths, place, xz, edge, channel, w_x)


def convolve_back(
    lengths, place, xz, edge, channel, w_x, conv, act, act_grad, y_grad, projected_grad
):
    micros, tokens, inner = conv.shape
    scalars = pl.BlockSpec(memory_space=pltpu.SMEM)
    rows = pl.BlockSpec((1, tokens, LANES), lambda g, m: (m, 0, g))
    ends = pl.BlockSpec((1, CONV - 1, LANES), lambda g, m: (m, 0, g))
    columns_x = w_x.shape[1]
    weight = pl.BlockSpec((LANES, columns_x), lambda g, m: (g, 0))
    return pl.pallas_call(
        conv_back_kernel,
        grid=(inner // LANES, micros),
        in_specs=[
            scalars,
            scalars,
            rows,
            ends,
            pl.BlockSpec((channel.shape[0], LANES), lambda g, m: (0, g)),
            weight,
            rows,
            rows,
            rows,
            rows,
            pl.BlockSpec((1, tokens, columns_x), lambda g, m: (m, 0, 0)),
        ],
        out_specs=[rows, ends, weight, pl.BlockSpec((8, LANES), lambda g, m: (0, g))],
        out_shape=[
            jax.ShapeDtypeStruct((micros, tokens, inner), F32),
            jax.ShapeDtypeStruct((micros, CONV - 1, inner), F32),
            jax.ShapeDtypeStruct((inner, columns_x), F32),
            jax.ShapeDtypeStruct((8, inner), F32),
        ],
        scratch_shapes=[pltpu.VMEM((PAD + tokens, LANES), F32)] * 2,
        compiler_params=kernel_params(),
        name="mixer_conv_back",
    )(lengths, place, xz, edge, channel, w_x, conv, act, act_grad, y_grad, projected_grad)


def scan_end(keep, projected, w_step, channel, act, inject):
    micros, tokens, inner = act.shape
    rows = pl.BlockSpec((1, tokens, LANES), lambda g, m: (m, 0, g))
    columns_x = projected.shape[2]
    shape = jax.ShapeDtypeStruct((micros, tokens, inner), F32)
    return pl.pallas_call(
        end_kernel,
        grid=(inner // LANES, micros),
        in_specs=[
            pl.BlockSpec(memory_space=pltpu.SMEM),
            pl.BlockSpec((1, tokens, columns_x), lambda g, m: (m, 0, 0)),
            pl.BlockSpec((RANK, LANES), lambda g, m: (0, g)),
            pl.BlockSpec((channel.shape[0], LANES), lambda g, m: (0, g)),
            rows,
            pl.BlockSpec((1, tokens, STATES, 128), lambda g, m: (m, 0, 0, 0)),
        ],
        out_specs=[
            rows,
            rows,
            pl.BlockSpec((STATES, LANES), lambda g, m: (m, g)),
            pl.BlockSpec((TOTAL_ROWS, LANES), lambda g, m: (0, g)),
        ],
        out_shape=[
            shape,
            shape,
            jax.ShapeDtypeStruct((micros * STATES, inner), BF16),
            jax.ShapeDtypeStruct((TOTAL_ROWS, inner), F32),
        ],
        compiler_params=kernel_params(),
        name="scan_end",
    )(keep, projected, w_step, channel, act, inject)


def scan_forward(place, keep, dt, act, inject, readout, rate, ends_all, totals_all):
    micros, tokens, inner = dt.shape
    rows, wide, rated, state, _, edges, totals, every, scalars = specs(tokens, ends_all.shape[0])
    return pl.pallas_call(
        forward_kernel,
        grid=(micros, inner // LANES),
        in_specs=[scalars, scalars, rows, rows, wide, wide, rated, edges, totals],
        out_specs=[rows, every, state],
        out_shape=[
            jax.ShapeDtypeStruct((micros, tokens, inner), F32),
            jax.ShapeDtypeStruct((micros, tokens, STATES, inner), F32),
            jax.ShapeDtypeStruct((micros, STATES, inner), F32),
        ],
        compiler_params=kernel_params(),
        name="scan_forward",
    )(place, keep, dt, act, inject, readout, rate, ends_all, totals_all)


def scan_start(keep, dt, dy, readout, rate, ahead):
    micros, tokens, inner = dt.shape
    rows, wide, rated, _, edge, _, _, _, scalars = specs(tokens, 1)
    unread = pl.BlockSpec(memory_space=pl.ANY)

    def body(keep, dt, dy, readout, rate, *rest):
        start_kernel(keep, dt, dy, readout, rate, rest[-1])

    return pl.pallas_call(
        body,
        grid=(micros, inner // LANES),
        in_specs=[scalars, rows, rows, wide, rated] + [unread] * len(ahead),
        out_specs=edge,
        out_shape=jax.ShapeDtypeStruct((micros * STATES, inner), BF16),
        compiler_params=kernel_params(),
        name="scan_start",
    )(keep, dt, dy, readout, rate, *ahead)


def scan_backward(
    place, keep, dt, act, dy, inject, readout, rate, totals_all, starts_all, start, hs, ahead
):
    micros, tokens, inner = dt.shape
    rows, wide, rated, state, _, edges, totals, every, scalars = specs(tokens, totals_all.shape[0])
    unread = pl.BlockSpec(memory_space=pl.ANY)

    def body(*refs):
        backward_kernel(*refs[:12], *refs[12 + len(ahead) :])

    return pl.pallas_call(
        body,
        grid=(micros, inner // LANES),
        in_specs=[
            scalars, scalars, rows, rows, rows, wide, wide, rated, totals, edges, state, every,
        ]
        + [unread] * len(ahead),
        out_specs=[rows, rows, wide, wide, state],
        out_shape=[
            jax.ShapeDtypeStruct((micros, tokens, inner), F32),
            jax.ShapeDtypeStruct((micros, tokens, inner), F32),
            jax.ShapeDtypeStruct((micros, tokens, STATES, 128), F32),
            jax.ShapeDtypeStruct((micros, tokens, STATES, 128), F32),
            jax.ShapeDtypeStruct((micros, STATES, inner), F32),
        ],
        compiler_params=kernel_params(),
        name="scan_backward",
    )(place, keep, dt, act, dy, inject, readout, rate, totals_all, starts_all, start, hs, *ahead)


def expert_kernel(taken, w_up, w_down, hidden_out, slope_out, out, total):
    step = pl.program_id(1)
    values = dot(taken[0], w_up[0], 1, 0)
    below = 0.5 + 0.5 * lax.erf(values * math.sqrt(0.5))
    hidden = (values * below).astype(BF16)
    density = jnp.exp(-0.5 * values * values) * (1.0 / math.sqrt(2.0 * math.pi))
    hidden_out[0] = hidden
    slope_out[0] = below + values * density

    @pl.when(step == 0)
    def _():
        total[...] = jnp.zeros_like(total)

    total[...] += dot(hidden, w_down[0], 1, 0)

    @pl.when(step == pl.num_programs(1) - 1)
    def _():
        out[0] = total[...].astype(BF16)


def expert_back_kernel(
    taken, grad, w_up, w_down, hidden, slope, up_out, down_out, taken_out, total
):
    step = pl.program_id(1)
    pre_grad = (dot(grad[0], w_down[0], 1, 1) * slope[0]).astype(BF16)
    down_out[0] = dot(hidden[0], grad[0], 0, 0).astype(BF16)
    up_out[0] = dot(taken[0], pre_grad, 0, 0).astype(BF16)

    @pl.when(step == 0)
    def _():
        total[...] = jnp.zeros_like(total)

    total[...] += dot(pre_grad, w_up[0], 1, 1)

    @pl.when(step == pl.num_programs(1) - 1)
    def _():
        taken_out[0] = total[...].astype(BF16)


def expert_specs(rows, width):
    whole = pl.BlockSpec((1, rows, width), lambda e, j: (e, 0, 0))
    up = pl.BlockSpec((1, width, HIDDEN), lambda e, j: (e, 0, j))
    down = pl.BlockSpec((1, HIDDEN, width), lambda e, j: (e, j, 0))
    units = pl.BlockSpec((1, rows, HIDDEN), lambda e, j: (e, 0, j))
    return whole, up, down, units


def run_experts(taken, w_up, w_down):
    experts, rows, width = taken.shape
    hidden = w_up.shape[2]
    whole, up, down, units = expert_specs(rows, width)
    return pl.pallas_call(
        expert_kernel,
        grid=(experts, hidden // HIDDEN),
        in_specs=[whole, up, down],
        out_specs=[units, units, whole],
        out_shape=[
            jax.ShapeDtypeStruct((experts, rows, hidden), BF16),
            jax.ShapeDtypeStruct((experts, rows, hidden), F32),
            jax.ShapeDtypeStruct(taken.shape, BF16),
        ],
        scratch_shapes=[pltpu.VMEM((rows, width), F32)],
        compiler_params=kernel_params(),
        name="experts",
    )(taken, w_up, w_down)


def run_experts_back(taken, grad, w_up, w_down, hidden, slope):
    experts, rows, width = taken.shape
    whole, up, down, units = expert_specs(rows, width)
    return pl.pallas_call(
        expert_back_kernel,
        grid=(experts, hidden.shape[2] // HIDDEN),
        in_specs=[whole, whole, up, down, units, units],
        out_specs=[up, down, whole],
        out_shape=[
            jax.ShapeDtypeStruct(w_up.shape, BF16),
            jax.ShapeDtypeStruct(w_down.shape, BF16),
            jax.ShapeDtypeStruct(taken.shape, BF16),
        ],
        scratch_shapes=[pltpu.VMEM((rows, width), F32)],
        compiler_params=kernel_params(),
        name="experts_back",
    )(taken, grad, w_up, w_down, hidden, slope)


def head_columns(width):
    return lax.broadcasted_iota(jnp.int32, (1, width), 1) + pl.program_id(0) * width


def head_kernel(limits, rows, table, targets, logits_out, stats, largest, summed, wanted):
    step = pl.program_id(0)
    tile = table.shape[1]
    column = head_columns(tile)
    logits = dot(rows[...], table[...], 1, 0)
    logits = jnp.where(column < limits[1], logits, -1e30)
    logits_out[...] = logits
    named = targets[...] - limits[0]
    named = jnp.where(named < limits[1], named, -1)

    @pl.when(step == 0)
    def _():
        largest[...] = jnp.full_like(largest, -1e30)
        summed[...] = jnp.zeros_like(summed)
        wanted[...] = jnp.zeros_like(wanted)

    parts = [logits[:, first : first + 128] for first in range(0, tile, 128)]
    before = largest[...]
    top = functools.reduce(jnp.maximum, parts, before)
    total = summed[...] * jnp.exp(before - top)
    found = wanted[...]
    for index, part in enumerate(parts):
        total = total + jnp.exp(part - top)
        spot = column[:, index * 128 : (index + 1) * 128]
        found = found + jnp.where(spot == named, part, 0.0)
    largest[...], summed[...], wanted[...] = top, total, found

    @pl.when(step == pl.num_programs(0) - 1)
    def _():
        most = jnp.max(top, axis=1, keepdims=True)
        stats[...] = jnp.zeros_like(stats)
        stats[:, 0:1] = most
        stats[:, 1:2] = jnp.sum(total * jnp.exp(top - most), axis=1, keepdims=True)
        stats[:, 2:3] = jnp.sum(found, axis=1, keepdims=True)


def head_back_kernel(
    limits, rows, table, targets, scalars, logits, table_out, rows_out, total
):
    step = pl.program_id(0)
    column = head_columns(table.shape[1])
    inside = column < limits[1]
    probability = jnp.exp(logits[...] - scalars[:, 0:1])
    hit = jnp.where(column == targets[...] - limits[0], 1.0, 0.0)
    grad = scalars[:, 1:2] * (probability - hit)
    grad = jnp.where(inside, grad, 0.0).astype(BF16)

    @pl.when(step == 0)
    def _():
        total[...] = jnp.zeros_like(total)

    table_out[...] = dot(rows[...], grad, 1, 0).astype(BF16)

    @pl.when(step < pl.num_programs(0) - 1)
    def _():
        total[...] += dot(grad, table[...], 1, 1)

    @pl.when(step == pl.num_programs(0) - 1)
    def _():
        weight = jnp.where(inside, table[...].astype(F32), 0.0).astype(BF16)
        rows_out[...] = (total[...] + dot(grad, weight, 1, 1)).astype(BF16)


def head_specs(rows, table):
    count, width = rows.shape
    tile = 1280 if count <= 512 else 640
    whole = pl.BlockSpec((count, width), lambda j: (0, 0))
    part = pl.BlockSpec((width, tile), lambda j: (0, j))
    column = pl.BlockSpec((count, 1), lambda j: (0, 0))
    few = pl.BlockSpec((count, 8), lambda j: (0, 0))
    logits = pl.BlockSpec((count, tile), lambda j: (0, j))
    return whole, part, column, few, logits, (-(-table.shape[1] // tile),)


def head(limits, rows, table, targets):
    whole, part, column, few, logits, grid = head_specs(rows, table)
    return pl.pallas_call(
        head_kernel,
        grid=grid,
        in_specs=[pl.BlockSpec(memory_space=pltpu.SMEM), whole, part, column],
        out_specs=[logits, few],
        out_shape=[
            jax.ShapeDtypeStruct((rows.shape[0], table.shape[1]), F32),
            jax.ShapeDtypeStruct((rows.shape[0], 8), F32),
        ],
        scratch_shapes=[pltpu.VMEM((rows.shape[0], 128), F32)] * 3,
        compiler_params=kernel_params(),
        name="head",
    )(limits, rows, table, targets)


def head_back(limits, rows, table, targets, scalars, logits):
    whole, part, column, few, logit, grid = head_specs(rows, table)
    turned = pl.BlockSpec((rows.shape[1], rows.shape[0]), lambda j: (0, 0))
    return pl.pallas_call(
        head_back_kernel,
        grid=grid,
        in_specs=[
            pl.BlockSpec(memory_space=pltpu.SMEM), turned, part, column, few, logit,
        ],
        out_specs=[part, whole],
        out_shape=[
            jax.ShapeDtypeStruct(table.shape, BF16),
            jax.ShapeDtypeStruct(rows.shape, BF16),
        ],
        scratch_shapes=[pltpu.VMEM(rows.shape, F32)],
        compiler_params=kernel_params(),
        name="head_back",
    )(limits, rows.T, table, targets, scalars, logits)


def exchange_kernel(groups, gathers, ahead, *refs):
    arrays = len(groups)
    inputs, outputs = refs[:arrays], refs[arrays + ahead : 2 * arrays + ahead]
    sends, receives, own_sem = refs[2 * arrays + ahead :]

    def place_of(axes):
        if len(axes) == 1:
            return lax.axis_size(axes[0]), lax.axis_index(axes[0]), lambda peer: {axes[0]: peer}
        width = lax.axis_size(axes[1])
        return (
            lax.axis_size(axes[0]) * width,
            lax.axis_index(axes[0]) * width + lax.axis_index(axes[1]),
            lambda peer: {axes[0]: peer // width, axes[1]: peer % width},
        )

    def source(index, peer):
        return inputs[index] if gathers[index] else inputs[index].at[peer]

    def copy(index, device, peer, block):
        return pltpu.make_async_remote_copy(
            src_ref=source(index, peer),
            dst_ref=outputs[index].at[block],
            send_sem=sends.at[index, peer],
            recv_sem=receives.at[index, block],
            device_id=device(peer),
            device_id_type=MESH,
        )

    barrier = pltpu.get_barrier_semaphore()
    total = 0
    for axes in sorted(set(groups)):
        peers, me, device = place_of(axes)

        def greet(lap, _):
            pl.semaphore_signal(
                barrier, inc=1, device_id=device((me + lap) % peers), device_id_type=MESH
            )
            return _

        lax.fori_loop(1, peers, greet, 0)
        total += peers - 1
    own = []
    for index, axes in enumerate(groups):
        me = place_of(axes)[1]
        own.append(
            pltpu.make_async_copy(source(index, me), outputs[index].at[me], own_sem.at[index])
        )
        own[-1].start()
    pl.semaphore_wait(barrier, total)
    for index, axes in enumerate(groups):
        peers, me, device = place_of(axes)

        def begin(lap, _):
            copy(index, device, (me + lap) % peers, me).start()
            return _

        lax.fori_loop(1, peers, begin, 0)
    for index, axes in enumerate(groups):
        peers, me, device = place_of(axes)
        own[index].wait()

        def end(lap, _):
            before = (me + peers - lap) % peers
            copy(index, device, before, before).wait_recv()
            copy(index, device, (me + lap) % peers, me).wait_send()
            return _

        lax.fori_loop(1, peers, end, 0)


def exchange(values, gathers, identity, axes=("seq",), space=pltpu.VMEM, ahead=()):
    groups = [axes] * len(values)
    peers = [math.prod(lax.axis_size(axis) for axis in group) for group in groups]
    place = pl.BlockSpec(memory_space=space)
    unread = pl.BlockSpec(memory_space=pl.ANY)
    shapes = [
        jax.ShapeDtypeStruct(((count,) if gather else ()) + value.shape, value.dtype)
        for value, gather, count in zip(values, gathers, peers)
    ]
    arrays = len(values)
    return pl.pallas_call(
        functools.partial(exchange_kernel, tuple(groups), tuple(gathers), len(ahead)),
        out_shape=shapes,
        in_specs=[place] * arrays + [unread] * len(ahead),
        out_specs=[place] * arrays,
        scratch_shapes=[
            pltpu.SemaphoreType.DMA((arrays, max(peers))),
            pltpu.SemaphoreType.DMA((arrays, max(peers))),
            pltpu.SemaphoreType.DMA((arrays,)),
        ],
        compiler_params=pltpu.CompilerParams(collective_id=identity, has_side_effects=True),
        name="exchange",
    )(*values, *ahead)


def hold(values, ahead):
    unread = pl.BlockSpec(memory_space=pl.ANY)
    return pl.pallas_call(
        lambda *refs: None,
        out_shape=[jax.ShapeDtypeStruct(value.shape, value.dtype) for value in values],
        in_specs=[unread] * (len(values) + len(ahead)),
        out_specs=[unread] * len(values),
        input_output_aliases={index: index for index in range(len(values))},
        name="hold",
    )(*values, *ahead)


class Line:
    SEMAPHORES = 6

    def __init__(self, inputs, outputs, semaphores):
        self.inputs, self.outputs = inputs, outputs
        self.sends, self.receives = semaphores[0::2], semaphores[1::2]
        self.outers = lax.axis_size("seq") // 2
        me = lax.axis_index("seq")
        self.outer, self.inner = me // 2, me % 2
        self.later = self.outer + 1 < self.outers
        self.earlier = self.outer > 0

    def block(self, outer):
        return outer * 2 + self.inner

    def across(self, outer):
        return outer * 2 + 1 - self.inner

    def target(self, way):
        step = (2, -2, 1 - 2 * self.inner)[way]
        return {"seq": self.outer * 2 + self.inner + step}

    def pieces(self):
        for index, source in enumerate(self.inputs):
            for piece in range(source.shape[0]):
                yield index, piece

    def copy(self, way, index, outer, piece, place, first=False):
        source = self.outputs[index].at[place, piece]
        return pltpu.make_async_remote_copy(
            src_ref=self.inputs[index].at[piece] if first else source,
            dst_ref=self.outputs[index].at[place, piece],
            send_sem=self.sends[way].at[index, outer, piece],
            recv_sem=self.receives[way].at[index, outer, piece],
            device_id=self.target(way),
            device_id_type=MESH,
        )

    def ways(self):
        return ((0, self.later), (1, self.earlier))

    def greet(self, barrier):
        for way, exists in self.ways():

            @pl.when(exists)
            def _():
                pl.semaphore_signal(
                    barrier, inc=1, device_id=self.target(way), device_id_type=MESH
                )

        pl.semaphore_signal(barrier, inc=1, device_id=self.target(2), device_id_type=MESH)
        return 1 + self.later.astype(jnp.int32) + self.earlier.astype(jnp.int32)

    def begin(self):
        mine = self.block(self.outer)
        for index, piece in self.pieces():
            for way, exists in self.ways():

                @pl.when(exists)
                def _():
                    self.copy(way, index, self.outer, piece, mine, True).start()

            self.copy(2, index, self.outer, piece, mine, True).start()

    def forward(self, lap):
        for index, piece in self.pieces():
            for way, exists in self.ways():
                outer = self.outer + (-lap, lap)[way]
                place = self.block(outer)

                @pl.when(jnp.logical_and(outer >= 0, outer < self.outers))
                def _():
                    self.copy(way, index, outer, piece, place).wait_recv()

                    @pl.when(exists)
                    def _():
                        self.copy(way, index, outer, piece, place).start()

                    self.copy(2, index, outer, piece, place).start()

    def take(self, outer):
        for index, piece in self.pieces():
            self.copy(2, index, outer, piece, self.across(outer)).wait_recv()

    def each(self, lap, use, partners=None):
        for way in range(2):
            outer = self.outer + (-lap, lap)[way]

            @pl.when(jnp.logical_and(outer >= 0, outer < self.outers))
            def _():
                if partners is not True:
                    use(self.block(outer))
                if partners is not False:
                    self.take(outer)
                    use(self.across(outer))

    def end(self):
        def one(outer, _):
            for index, piece in self.pieces():
                place = self.block(outer)

                @pl.when(jnp.logical_and(self.later, outer <= self.outer))
                def _():
                    self.copy(0, index, outer, piece, place).wait_send()

                @pl.when(jnp.logical_and(self.earlier, outer >= self.outer))
                def _():
                    self.copy(1, index, outer, piece, place).wait_send()

                self.copy(2, index, outer, piece, place).wait_send()
            return 0

        lax.fori_loop(0, self.outers, one, 0)


def line_semaphores(values):
    shape = (len(values), lax.axis_size("seq") // 2, max(value.shape[0] for value in values))
    return [pltpu.SemaphoreType.DMA(shape)] * Line.SEMAPHORES


def gather_kernel(arrays, ahead, relays, everyone, *refs):
    if everyone:
        tally, tallies = refs[arrays], refs[2 * arrays + 1 + ahead]
        refs = list(refs)
        del refs[2 * arrays + 1 + ahead], refs[arrays]
    inputs = refs[:arrays]
    outputs = refs[arrays + ahead : 2 * arrays + ahead]
    wholes = refs[2 * arrays + ahead : 2 * arrays + ahead + len(relays)]
    rest = refs[2 * arrays + ahead + len(relays) :]
    line = Line(inputs, outputs, rest[: Line.SEMAPHORES])
    own_sem, relay_sends, relay_receives, relay_own = rest[Line.SEMAPHORES :][:4]
    all_sends, all_receives, all_own = rest[Line.SEMAPHORES + 4 :]
    mats, here = lax.axis_size("mat"), lax.axis_index("mat")
    me = lax.axis_index("seq")
    devices = lax.axis_size("seq") * mats
    number = me * mats + here

    def device(other):
        return {"seq": other // mats, "mat": other % mats}

    def report(other, origin):
        return pltpu.make_async_remote_copy(
            src_ref=tally,
            dst_ref=tallies.at[origin],
            send_sem=all_sends.at[other],
            recv_sem=all_receives.at[origin],
            device_id=device(other),
            device_id_type=MESH,
        )

    def relayed(relay, block, origin):
        index, place = relays[relay]
        return pltpu.make_async_remote_copy(
            src_ref=outputs[index].at[block],
            dst_ref=wholes[relay].at[origin, block],
            send_sem=relay_sends.at[relay, block],
            recv_sem=relay_receives.at[relay, origin, block],
            device_id={"mat": place},
            device_id_type=MESH,
        )

    def kept(relay, block):
        index, place = relays[relay]
        return pltpu.make_async_copy(
            outputs[index].at[block], wholes[relay].at[place, block], relay_own.at[relay, block]
        )

    def relay_all(block):
        for relay, (_, place) in enumerate(relays):

            @pl.when(here != place)
            def _():
                relayed(relay, block, here).start()

            @pl.when(here == place)
            def _():
                kept(relay, block).start()

    def relay_end(block, _):
        for relay, (_, place) in enumerate(relays):

            @pl.when(here != place)
            def _():
                relayed(relay, block, here).wait_send()

            @pl.when(here == place)
            def _():
                kept(relay, block).wait()
                for origin in range(mats):
                    if origin != place:
                        relayed(relay, block, origin).wait_recv()

        return 0

    barrier = pltpu.get_barrier_semaphore()
    if everyone:

        def greet_all(lap, _):
            pl.semaphore_signal(
                barrier, inc=1, device_id=device((number + lap) % devices), device_id_type=MESH
            )
            return 0

        lax.fori_loop(1, devices, greet_all, 0)
        greeted = devices - 1
    else:
        greeted = line.greet(barrier)
    if relays and not everyone:

        def greet_mat(lap, _):
            pl.semaphore_signal(
                barrier, inc=1, device_id={"mat": (here + lap) % mats}, device_id_type=MESH
            )
            return 0

        lax.fori_loop(1, mats, greet_mat, 0)
        greeted = greeted + mats - 1
    own = [
        pltpu.make_async_copy(inputs[index], outputs[index].at[me], own_sem.at[index])
        for index in range(arrays)
    ]
    for copy in own:
        copy.start()
    pl.semaphore_wait(barrier, greeted)
    if everyone:

        def report_all(lap, _):
            report((number + lap) % devices, number).start()
            return 0

        lax.fori_loop(1, devices, report_all, 0)
        own_tally = pltpu.make_async_copy(tally, tallies.at[number], all_own)
        own_tally.start()
    line.begin()
    for copy in own:
        copy.wait()
    relay_all(me)

    def step(lap, _):
        line.forward(lap)

        @pl.when(lap > 1)
        def _():
            line.each(lap - 1, relay_all)

        return 0

    lax.fori_loop(1, line.outers, step, 0)
    line.take(line.outer)
    relay_all(line.across(line.outer))
    line.each(line.outers - 1, relay_all)
    line.end()
    if relays:
        lax.fori_loop(0, lax.axis_size("seq"), relay_end, 0)
    if everyone:

        def report_end(lap, _):
            before = (number + devices - lap) % devices
            report(before, before).wait_recv()
            report((number + lap) % devices, number).wait_send()
            return 0

        lax.fori_loop(1, devices, report_end, 0)
        own_tally.wait()


def gather_seq(values, identity, space=pltpu.VMEM, ahead=(), relays=(), everyone=()):
    peers = lax.axis_size("seq")
    mats = lax.axis_size("mat")
    plain = [value.shape for value in values]
    values = [
        value.reshape((2, -1) + value.shape[1:]) if value.shape[0] % 32 == 0 else value[None]
        for value in values
    ]
    shapes = [jax.ShapeDtypeStruct((peers,) + value.shape, value.dtype) for value in values]
    shapes += [
        jax.ShapeDtypeStruct((mats, peers) + values[index].shape, values[index].dtype)
        for index, _ in relays
    ]
    place = pl.BlockSpec(memory_space=space)
    unread = pl.BlockSpec(memory_space=pl.ANY)
    arrays, more = len(values), len(everyone)
    shapes[arrays:arrays] = [
        jax.ShapeDtypeStruct((peers * mats,) + value.shape, value.dtype) for value in everyone
    ]
    results = pl.pallas_call(
        functools.partial(gather_kernel, arrays, len(ahead), tuple(relays), bool(more)),
        out_shape=shapes,
        in_specs=[place] * (arrays + more) + [unread] * len(ahead),
        out_specs=[place] * (arrays + more) + [unread] * len(relays),
        scratch_shapes=line_semaphores(values)
        + [
            pltpu.SemaphoreType.DMA((arrays,)),
            pltpu.SemaphoreType.DMA((max(1, len(relays)), peers)),
            pltpu.SemaphoreType.DMA((max(1, len(relays)), mats, peers)),
            pltpu.SemaphoreType.DMA((max(1, len(relays)), peers)),
            pltpu.SemaphoreType.DMA((peers * mats,)),
            pltpu.SemaphoreType.DMA((peers * mats,)),
            pltpu.SemaphoreType.DMA,
        ],
        compiler_params=pltpu.CompilerParams(collective_id=identity, has_side_effects=True),
        name="gather_seq",
    )(*values, *everyone, *ahead)
    results = list(results)
    reported = results[arrays : arrays + more]
    del results[arrays : arrays + more]
    gathered = [result.reshape((peers,) + shape) for result, shape in zip(results, plain)]
    relayed = [
        result.reshape((mats, peers) + plain[index])
        for result, (index, _) in zip(results[arrays:], relays)
    ]
    return gathered + relayed + reported


def reduce_kernel(arrays, riders, *refs):
    rides = [refs[index : index + 5] for index in range(0, 5 * riders, 5)]
    refs = refs[5 * riders :]
    mats, here = lax.axis_size("mat"), lax.axis_index("mat")

    def ride(refs, place, origin):
        source, target, ride_sends, ride_receives, _ = refs
        return pltpu.make_async_remote_copy(
            src_ref=source.at[place],
            dst_ref=target.at[origin],
            send_sem=ride_sends.at[place],
            recv_sem=ride_receives.at[origin],
            device_id={"mat": place},
            device_id_type=MESH,
        )

    def stay(refs):
        source, target, _, _, ride_own = refs
        return pltpu.make_async_copy(source.at[here], target.at[here], ride_own)

    inputs, outputs = refs[:arrays], refs[arrays : 2 * arrays]
    got, keep = refs[2 * arrays : 3 * arrays], refs[3 * arrays : 4 * arrays]
    passes, arrivals, sends, receives = refs[4 * arrays :]
    outers = lax.axis_size("seq") // 2
    me = lax.axis_index("seq")
    outer, inner = me // 2, me % 2
    partner = {"seq": outer * 2 + 1 - inner}

    def hand(index, place):
        return pltpu.make_async_remote_copy(
            src_ref=inputs[index].at[place * 2 + 1 - inner],
            dst_ref=got[index].at[place],
            send_sem=passes.at[index, place],
            recv_sem=arrivals.at[index, place],
            device_id=partner,
            device_id_type=MESH,
        )

    def send(index, place, origin):
        return pltpu.make_async_remote_copy(
            src_ref=keep[index].at[place],
            dst_ref=outputs[index].at[origin],
            send_sem=sends.at[index, place],
            recv_sem=receives.at[index, origin],
            device_id={"seq": place * 2 + inner},
            device_id_type=MESH,
        )

    barrier = pltpu.get_barrier_semaphore()

    def greet(lap, _):
        pl.semaphore_signal(
            barrier,
            inc=1,
            device_id={"seq": ((outer + lap) % outers) * 2 + inner},
            device_id_type=MESH,
        )
        return 0

    pl.semaphore_signal(barrier, inc=1, device_id=partner, device_id_type=MESH)
    lax.fori_loop(1, outers, greet, 0)
    def greet_mat(lap, _):
        pl.semaphore_signal(
            barrier, inc=1, device_id={"mat": (here + lap) % mats}, device_id_type=MESH
        )
        return 0

    if riders:
        lax.fori_loop(1, mats, greet_mat, 0)
    pl.semaphore_wait(barrier, outers + (mats - 1 if riders else 0))
    for one in rides:
        stay(one).start()

        def set_off(lap, _):
            ride(one, (here + lap) % mats, here).start()
            return 0

        lax.fori_loop(1, mats, set_off, 0)

    def begin(lap, _):
        for index in range(arrays):
            hand(index, (outer + 1 + lap) % outers).start()
        return 0

    lax.fori_loop(0, outers, begin, 0)

    def add(lap, _):
        place = (outer + 1 + lap) % outers
        for index in range(arrays):
            hand(index, place).wait_recv()
            total = inputs[index][place * 2 + inner].astype(F32) + got[index][place].astype(F32)
            keep[index][place] = total.astype(BF16)

            @pl.when(place != outer)
            def _():
                send(index, place, outer).start()

            @pl.when(place == outer)
            def _():
                outputs[index][outer] = total.astype(BF16)

        return 0

    lax.fori_loop(0, outers, add, 0)

    def end(lap, _):
        place = (outer + lap) % outers
        for index in range(arrays):
            hand(index, place).wait_send()

            @pl.when(place != outer)
            def _():
                send(index, place, place).wait_recv()
                send(index, place, outer).wait_send()

        return 0

    lax.fori_loop(0, outers, end, 0)
    for one in rides:
        stay(one).wait()

        def arrive(lap, _):
            before = (here + mats - lap) % mats
            ride(one, before, before).wait_recv()
            ride(one, (here + lap) % mats, here).wait_send()
            return 0

        lax.fori_loop(1, mats, arrive, 0)


def reduce_seq(values, identity, ahead=(), riders=()):
    outers = lax.axis_size("seq") // 2
    arrays = len(values)
    shapes = [(outers,) + value.shape[1:] for value in values]
    place = pl.BlockSpec(memory_space=pltpu.VMEM)
    unread = pl.BlockSpec(memory_space=pl.ANY)

    count, mats = len(riders), lax.axis_size("mat")
    first = arrays + count + len(ahead)

    def body(*refs):
        sources = refs[arrays : arrays + count]
        targets = refs[first + arrays : first + arrays + count]
        rest = refs[first + arrays + count :]
        rides = []
        for index in range(count):
            rides += [sources[index], targets[index], *rest[3 * index : 3 * index + 3]]
        reduce_kernel(
            arrays,
            count,
            *rides,
            *refs[:arrays],
            *refs[first : first + arrays],
            *rest[3 * count :],
        )

    results = pl.pallas_call(
        body,
        out_shape=[jax.ShapeDtypeStruct(shape, BF16) for shape in shapes]
        + [jax.ShapeDtypeStruct(rider.shape, rider.dtype) for rider in riders],
        in_specs=[place] * arrays + [unread] * (count + len(ahead)),
        out_specs=[place] * arrays + [unread] * count,
        scratch_shapes=[
            pltpu.SemaphoreType.DMA((mats,)),
            pltpu.SemaphoreType.DMA((mats,)),
            pltpu.SemaphoreType.DMA,
        ]
        * count
        + [pltpu.VMEM(shape, BF16) for shape in shapes * 2]
        + [pltpu.SemaphoreType.DMA((arrays, outers))] * 4,
        compiler_params=pltpu.CompilerParams(
            collective_id=identity, has_side_effects=True, vmem_limit_bytes=48 * 1024 * 1024
        ),
        name="reduce_seq",
    )(*values, *riders, *ahead)
    sums = [jnp.sum(result.astype(F32), axis=0) for result in results[:arrays]]
    return sums + list(results[arrays:])


def lookup_kernel(
    ids, turned, small, up_mom, in_mom, down_mom, out_mom, up, down, outward,
    out, smalls, moments, up_low, down_low, out_low, table, found, give, got, keep, taken, passes, arrivals, sends,
    receives, small_sends, small_receives, small_own, near, low, loads, stores,
):
    outers, mats = taken.shape[0], taken.shape[1]
    me = lax.axis_index("seq")
    here = lax.axis_index("mat")
    outer, inner = me // 2, me % 2
    partner = {"seq": outer * 2 + 1 - inner}
    tokens = 256
    lanes = lax.broadcasted_iota(jnp.int32, (128, 128), 1)

    def device(to_outer, to_mat):
        return {"seq": to_outer * 2 + inner, "mat": to_mat}

    def hand(lap, place):
        return pltpu.make_async_remote_copy(
            src_ref=give.at[lap, place],
            dst_ref=got.at[lap, place],
            send_sem=passes.at[lap, place],
            recv_sem=arrivals.at[lap, place],
            device_id=partner,
            device_id_type=MESH,
        )

    def send(to_outer, to_mat, from_outer, from_mat):
        return pltpu.make_async_remote_copy(
            src_ref=keep.at[to_outer, to_mat],
            dst_ref=taken.at[from_outer, from_mat],
            send_sem=sends.at[to_outer, to_mat],
            recv_sem=receives.at[from_outer, from_mat],
            device_id=device(to_outer, to_mat),
            device_id_type=MESH,
        )

    def share(to_mat, from_mat):
        return pltpu.make_async_remote_copy(
            src_ref=small,
            dst_ref=smalls.at[from_mat],
            send_sem=small_sends.at[to_mat],
            recv_sem=small_receives.at[from_mat],
            device_id={"mat": to_mat},
            device_id_type=MESH,
        )

    own_small = pltpu.make_async_copy(small, smalls.at[here], small_own)
    own_small.start()
    barrier = pltpu.get_barrier_semaphore()

    def greet(lap, _):
        pl.semaphore_signal(
            barrier,
            inc=1,
            device_id=device((outer + lap // mats) % outers, (here + lap % mats) % mats),
            device_id_type=MESH,
        )
        return _

    pl.semaphore_signal(barrier, inc=1, device_id=partner, device_id_type=MESH)
    lax.fori_loop(1, outers * mats, greet, 0)
    pl.semaphore_wait(barrier, outers * mats)

    def share_start(lap, _):
        share((here + lap) % mats, here).start()
        return 0

    lax.fori_loop(1, mats, share_start, 0)
    for first in range(0, table.shape[0], VOCAB_TILE):
        table[first : first + VOCAB_TILE, :] = turned[:, first : first + VOCAB_TILE].T

    def find(block):
        def rows(index, _):
            for step in range(8):
                row = index * 8 + step
                entry = ids[block * mats * tokens + row]
                found[pl.ds(row, 1), :] = table[pl.ds(entry, 1), :]
            return 0

        lax.fori_loop(0, mats * tokens // 8, rows, 0)

    def store(target):
        for place in range(mats):
            base = place * tokens
            target[place, 0:tokens, :] = found[base : base + tokens, 0:128].astype(BF16)
            low = found[base : base + 128, 128:256]
            high = pltpu.roll(found[base + 128 : base + tokens, 128:256], 64, 1)
            target[place, tokens : tokens + 128, :] = jnp.where(lanes < 64, low, high).astype(BF16)

    def outer_of(lap):
        return (outer + 1 + lap) % outers

    def hand_over(lap):
        find(outer_of(lap) * 2 + 1 - inner)
        store(give.at[lap])
        for place in range(mats):
            hand(lap, place).start()

    def compute(lap, _):
        to_outer = outer_of(lap)

        @pl.when(lap + 1 < outers)
        def _():
            hand_over(lap + 1)

        find(to_outer * 2 + inner)
        store(keep.at[to_outer])
        for place in range(mats):
            hand(lap, place).wait_recv()
            keep[to_outer, place] = keep[to_outer, place] + got[lap, place]
            own = jnp.logical_and(to_outer == outer, place == here)

            @pl.when(jnp.logical_not(own))
            def _():
                send(to_outer, place, outer, here).start()

            @pl.when(own)
            def _():
                taken[outer, here] = keep[to_outer, place]

        return 0

    hand_over(0)
    lax.fori_loop(0, outers, compute, 0)

    tasks = (
        (up, up_low),
        (down, down_low),
        (outward, out_low),
        (up_mom, moments.at[UP_PLACE]),
        (in_mom, moments.at[IN_PLACE]),
        (down_mom, moments.at[DOWN_PLACE]),
        (out_mom, moments.at[OUT_PLACE]),
    )

    def load(task):
        source, slot = tasks[task][0], task % 2
        rows = pl.ds(0, source.shape[0])
        return pltpu.make_async_copy(source, near.at[slot, rows], loads.at[slot])

    def keep_low(task):
        target, slot = tasks[task][1], task % 2
        rows = pl.ds(0, target.shape[0])
        return pltpu.make_async_copy(low.at[slot, rows], target, stores.at[slot])

    load(0).start()
    for task, (source, target) in enumerate(tasks):
        slot = task % 2
        if task + 1 < len(tasks):
            load(task + 1).start()
        load(task).wait()
        if task > 1:
            keep_low(task - 2).wait()

        def round_rows(index, _):
            cut = pl.ds(pl.multiple_of(index * 64, 64), 64)
            low[slot, cut, :] = near[slot, cut, :].astype(BF16)
            return 0

        lax.fori_loop(0, source.shape[0] // 64, round_rows, 0)
        if source.shape[0] < target.shape[0]:
            missing = target.shape[0] - source.shape[0]
            low[slot, source.shape[0] :, :] = jnp.zeros((missing, low.shape[2]), BF16)
        keep_low(task).start()
    keep_low(len(tasks) - 2).wait()
    keep_low(len(tasks) - 1).wait()

    def finish(lap, _):
        to_outer, to_mat = (outer + lap // mats) % outers, (here + lap % mats) % mats
        send(to_outer, to_mat, to_outer, to_mat).wait_recv()
        send(to_outer, to_mat, outer, here).wait_send()
        return _

    lax.fori_loop(1, outers * mats, finish, 0)

    def end(lap, _):
        for place in range(mats):
            hand(lap, place).wait_send()
        return 0

    lax.fori_loop(0, outers, end, 0)

    def share_end(lap, _):
        before = (here + mats - lap) % mats
        share(before, before).wait_recv()
        share((here + lap) % mats, here).wait_send()
        return 0

    lax.fori_loop(1, mats, share_end, 0)
    own_small.wait()
    for place in range(mats):

        def gather(source, total):
            return total + taken[source, place].astype(F32)

        out[place] = lax.fori_loop(0, outers, gather, jnp.zeros((384, 128), F32)).astype(BF16)


def lookup(ids, table, small, wide, identity):
    outers, mats = lax.axis_size("seq") // 2, lax.axis_size("mat")
    part, entries = table.shape
    padded = (entries // VOCAB_TILE + 1) * VOCAB_TILE
    table = jnp.pad(table, ((0, 256 - part), (0, padded - entries)))
    table = table.astype(BF16).astype(F32)
    ids = jnp.where((ids >= 0) & (ids < entries), ids, entries)
    unread = pl.BlockSpec(memory_space=pl.ANY)
    vmem = pl.BlockSpec(memory_space=pltpu.VMEM)
    blocks = pltpu.VMEM((outers, mats, 384, 128), BF16)
    return pl.pallas_call(
        lookup_kernel,
        out_shape=[
            jax.ShapeDtypeStruct((mats, 384, 128), BF16),
            jax.ShapeDtypeStruct((mats,) + small.shape, BF16),
            jax.ShapeDtypeStruct((mats,) + wide[0].shape, BF16),
            *[jax.ShapeDtypeStruct(value.shape, BF16) for value in wide[4:]],
        ],
        in_specs=[pl.BlockSpec(memory_space=pltpu.SMEM), vmem, vmem] + [unread] * len(wide),
        out_specs=[vmem, vmem] + [unread] * 4,
        scratch_shapes=[
            pltpu.VMEM((padded, 256), F32),
            pltpu.VMEM((mats * 256, 256), F32),
            blocks,
            blocks,
            blocks,
            blocks,
            *[pltpu.SemaphoreType.DMA((outers, mats))] * 4,
            pltpu.SemaphoreType.DMA((mats,)),
            pltpu.SemaphoreType.DMA((mats,)),
            pltpu.SemaphoreType.DMA,
            pltpu.VMEM((2,) + wide[0].shape, F32),
            pltpu.VMEM((2,) + wide[0].shape, BF16),
            pltpu.SemaphoreType.DMA((2,)),
            pltpu.SemaphoreType.DMA((2,)),
        ],
        compiler_params=pltpu.CompilerParams(
            collective_id=identity, has_side_effects=True, vmem_limit_bytes=56 * 1024 * 1024
        ),
        name="lookup",
    )(ids, table, small, *wide)


def scatter_rows_kernel(
    entries, ids, rows, others, first_rider, second_rider, out, squares, whole, buffer, near, *rest
):
    line = Line([rows], [buffer], rest[: Line.SEMAPHORES])
    rider_sends, rider_receives, rider_own, near_own = rest[Line.SEMAPHORES :]
    places = lax.axis_size("mat")
    here = lax.axis_index("mat")
    riders = ((first_rider, UP_PLACE), (second_rider, DOWN_PLACE))

    def ride(rider, origin):
        source, place = riders[rider]
        return pltpu.make_async_remote_copy(
            src_ref=source,
            dst_ref=whole.at[origin],
            send_sem=rider_sends.at[rider],
            recv_sem=rider_receives.at[origin],
            device_id={"mat": place},
            device_id_type=MESH,
        )

    def stay(rider):
        source, place = riders[rider]
        return pltpu.make_async_copy(source, whole.at[place], rider_own)

    mats = rows.shape[0]
    lanes = lax.broadcasted_iota(jnp.int32, (128, 128), 1)
    nears = [
        pltpu.make_async_copy(source, near.at[rider], near_own.at[rider])
        for rider, (source, _) in enumerate(riders)
    ]
    for copy in nears:
        copy.start()

    def add(block, source):
        parts = []
        for place in range(mats):
            tail = source[place, 256:384, :].astype(F32)
            low = jnp.where(lanes < 64, tail, 0.0)
            high = jnp.where(lanes < 64, pltpu.roll(tail, 64, 1), 0.0)
            tails = jnp.concatenate([low, high], axis=0).astype(BF16)
            parts.append(jnp.concatenate([source[place, 0:256, :], tails], axis=1))
        values = jnp.concatenate(parts, axis=0)
        names = jnp.concatenate(
            [ids[pl.ds(block * 2 * mats + half, 1), :] for half in range(2 * mats)], axis=1
        )
        group = lax.shift_right_arithmetic(names, 7)
        spot = lax.broadcasted_iota(jnp.int32, (128, names.shape[1]), 0)
        hits = jnp.where(spot == jnp.bitwise_and(names, 127), 1.0, 0.0).astype(BF16)

        def piece(index, _):
            first = pl.multiple_of(index * VOCAB_TILE, VOCAB_TILE)
            masked = []
            for step in range(VOCAB_TILE // 128):
                chosen = jnp.where(group == index * (VOCAB_TILE // 128) + step, 1.0, 0.0)
                masked.append(hits * chosen.astype(BF16))
            out[pl.ds(first, VOCAB_TILE), :] += dot(
                jnp.concatenate(masked, axis=0), values, 1, 0
            )
            return 0

        lax.fori_loop(0, out.shape[0] // VOCAB_TILE, piece, 0)

    barrier = pltpu.get_barrier_semaphore()
    greeted = line.greet(barrier)

    def greet_mat(lap, _):
        pl.semaphore_signal(
            barrier, inc=1, device_id={"mat": (here + lap) % places}, device_id_type=MESH
        )
        return _

    lax.fori_loop(1, places, greet_mat, 0)
    pl.semaphore_wait(barrier, greeted + places - 1)
    line.begin()
    for rider, (_, place) in enumerate(riders):

        @pl.when(here != place)
        def _():
            ride(rider, here).start()

        @pl.when(here == place)
        def _():
            stay(rider).start()

    def use(block):
        add(block, buffer.at[block])

    part = others.shape[0]

    def fill(index, _):
        cut = pl.ds(pl.multiple_of(index * VOCAB_TILE, VOCAB_TILE), VOCAB_TILE)
        more = others[:, cut].astype(F32).T
        out[cut, :] = jnp.concatenate(
            [more, jnp.zeros((VOCAB_TILE, 256 - part), F32)], axis=1
        )
        return 0

    lax.fori_loop(0, out.shape[0] // VOCAB_TILE, fill, 0)
    add(line.block(line.outer), rows)

    def square(index, total):
        cut = pl.ds(pl.multiple_of(index * 64, 64), 64)
        for rider in range(len(riders)):
            values = near[rider, cut, :].astype(F32)
            values = jnp.sum(values * values, axis=0, keepdims=True)
            for lane in range(0, values.shape[1], 256):
                total = total + values[:, lane : lane + 256]
        return total

    for copy in nears:
        copy.wait()
    total = lax.fori_loop(0, near.shape[1] // 64, square, jnp.zeros((1, 256), F32))

    def step(lap, _):
        line.forward(lap)

        @pl.when(lap == 1)
        def _():
            line.take(line.outer)
            use(line.across(line.outer))

        @pl.when(lap > 1)
        def _():
            line.each(lap - 1, use)

        return 0

    lax.fori_loop(1, line.outers, step, 0)
    line.each(line.outers - 1, use)
    line.end()
    for rider, (_, place) in enumerate(riders):

        @pl.when(here != place)
        def _():
            ride(rider, here).wait_send()

        @pl.when(here == place)
        def _():
            stay(rider).wait()
            for origin in range(places):
                if origin != place:
                    ride(rider, origin).wait_recv()

    def finish(index, total):
        cut = pl.ds(pl.multiple_of(index * VOCAB_TILE, VOCAB_TILE), VOCAB_TILE)
        values = out[cut, :]
        entry = lax.broadcasted_iota(jnp.int32, values.shape, 0) + index * VOCAB_TILE
        values = jnp.where(entry < entries, values, 0.0)
        return total + jnp.sum(values * values, axis=0, keepdims=True)

    total = lax.fori_loop(0, out.shape[0] // VOCAB_TILE, finish, total)
    squares[...] = jnp.broadcast_to(total, (8, 256))


def scatter_rows(ids, rows, others, entries, identity, riders):
    peers = lax.axis_size("seq")
    mats = lax.axis_size("mat")
    padded = -(-entries // VOCAB_TILE) * VOCAB_TILE
    unread = pl.BlockSpec(memory_space=pl.ANY)
    place = pl.BlockSpec(memory_space=pltpu.VMEM)
    return pl.pallas_call(
        functools.partial(scatter_rows_kernel, entries),
        out_shape=[
            jax.ShapeDtypeStruct((padded, 256), F32),
            jax.ShapeDtypeStruct((8, 256), F32),
            jax.ShapeDtypeStruct((mats,) + riders[0].shape, BF16),
        ],
        in_specs=[place, place, place, unread, unread],
        out_specs=[place, place, unread],
        scratch_shapes=[
            pltpu.VMEM((peers,) + rows.shape, BF16),
            pltpu.VMEM((2,) + riders[0].shape, BF16),
            *line_semaphores([rows]),
            pltpu.SemaphoreType.DMA((2,)),
            pltpu.SemaphoreType.DMA((mats,)),
            pltpu.SemaphoreType.DMA,
            pltpu.SemaphoreType.DMA((2,)),
        ],
        compiler_params=pltpu.CompilerParams(
            collective_id=identity, has_side_effects=True, vmem_limit_bytes=48 * 1024 * 1024
        ),
        name="scatter_rows",
    )(ids, rows, jnp.pad(others, ((0, 0), (0, padded - entries))), *riders)


def swap_seq(value, identity, ahead=()):
    return exchange([value], [False], identity, ahead=ahead)[0]


def move_rows(value, steps):
    count = lax.axis_size("seq")
    leading, last = (max(0, -steps), min(count, count - steps))
    return lax.ppermute(value, "seq", [(source, source + steps) for source in range(leading, last)])


def normalize(values, gain):
    scale = lax.rsqrt(jnp.mean(values * values, axis=-1, keepdims=True) + 1e-05)
    hat = values * scale
    return hat * gain, hat, scale


def normalize_back(hat, scale, gain, grad):
    gain_grad = jnp.sum(grad * hat, axis=0)
    hat_grad = grad * gain
    return gain_grad, scale * (hat_grad - hat * jnp.mean(hat_grad * hat, axis=-1, keepdims=True))


def silu_back(values):
    sig = jax.nn.sigmoid(values)
    return sig * (1.0 + values * (1.0 - sig))


def padded_rows(flat):
    size = flat.shape[-1]
    room = -(-size // 16384) * 16384 - size
    flat = jnp.pad(flat, [(0, 0)] * (flat.ndim - 1) + [(0, room)])
    return flat.reshape(flat.shape[:-1] + (-1, 1024))


def pack_small(parts):
    return padded_rows(jnp.concatenate([part.astype(BF16).reshape(-1) for part in parts]))


def unpack_small(every, parts):
    every = every.reshape(every.shape[0], -1)
    result, offset = [], 0
    for part in parts:
        size = part.size
        result.append(every[:, offset : offset + size].reshape((-1,) + part.shape))
        offset += size
    return result


def columns(stacked):
    count, rows, width = stacked.shape
    return stacked.transpose(1, 0, 2).reshape(rows, count * width)


def step_grads(weights, embedded, route, lengths, slots, weight_mask, targets, loss_all):
    table, w_in, w_out, w_up, w_down, w_x, w_step, w_route, chan_low, gains_low = weights
    channel = chan_low.astype(F32)
    gains = gains_low.astype(F32)
    me = lax.axis_index("seq")
    count = lax.axis_size("seq")
    micros, tokens = route.shape
    inner = w_in.shape[1] // 2
    vocab_part = table.shape[1]
    first_pos = me * tokens
    vocab_start = me * vocab_part
    bounds = jnp.cumsum(lengths, axis=1)
    position = first_pos + jnp.arange(tokens, dtype=jnp.int32)
    opening = position[None, :, None] == bounds[:, None, :-1]
    keeping = 1.0 - jnp.logical_or(
        jnp.any(opening, axis=2), position[None] == 0
    ).astype(F32)
    place = me.astype(jnp.int32).reshape(1)

    x0 = embedded.astype(F32)

    u, hat0, scale0 = normalize(x0, gains[0])
    u_low = u.astype(BF16)
    xz = dot(u_low, w_in, 1, 0).reshape(micros, tokens, 2 * inner)
    z = xz[:, :, inner:]
    edge = move_rows(xz[:, tokens - (CONV - 1) :, :inner], 1)
    conv, act, projected = convolve(lengths, place, xz, edge, channel, w_x)
    rank_low = projected[:, :, :RANK].reshape(-1, RANK).astype(BF16)
    rate = -jnp.exp(channel[CONV + 3 :])
    wide = projected[:, :, :, None]
    wide_shape = (micros, tokens, STATES, 128)
    inject = jnp.broadcast_to(wide[:, :, RANK : RANK + STATES], wide_shape)
    readout = jnp.broadcast_to(wide[:, :, RANK + STATES :], wide_shape)
    pre, dt, ends, totals = scan_end(keeping, projected, w_step, channel, act, inject)
    ends_all, totals_all = gather_seq([ends, totals], 1)
    y, hs, start = scan_forward(
        place, keeping, dt, act, inject, readout, rate, ends_all, totals_all
    )
    skip = channel[CONV + 2]
    z_silu = jax.nn.silu(z)
    core = y + skip * act
    mixed_low = (core * z_silu).reshape(-1, inner).astype(BF16)
    x1 = x0 + dot(mixed_low, w_out, 1, 0)

    experts = w_route.shape[1]
    capacity = max(2, 2 * tokens // experts)
    local_experts = w_up.shape[0]
    s, hat1, scale1 = normalize(x1, gains[1])
    s_low = s.astype(BF16)
    scores = dot(s_low, w_route, 1, 0)
    chosen = route.reshape(-1)[:, None] == jnp.arange(experts, dtype=jnp.int32)[None, :]
    gate = jax.nn.sigmoid(jnp.sum(jnp.where(chosen, scores, 0.0), axis=1))
    onehot = chosen.astype(jnp.int32).reshape(micros, tokens, experts)
    ranking = jnp.sum(jnp.cumsum(onehot, axis=1) * onehot, axis=2) - 1
    placed = route * capacity + ranking
    all_slots = experts * capacity
    sender = (
        placed[:, None, :] == jnp.arange(all_slots, dtype=jnp.int32)[None, :, None]
    ).astype(BF16)

    def to_experts(rows, identity, ahead=()):
        sent = jnp.einsum(
            "mst,mtd->msd", sender, rows.reshape(micros, tokens, D), preferred_element_type=F32
        ).astype(BF16)
        sent = sent.reshape(micros, count, -1, D).transpose(1, 0, 2, 3).reshape(count, -1, D)
        arrived = swap_seq(sent, identity, ahead).reshape(count, micros, local_experts, capacity, D)
        return arrived.transpose(2, 0, 1, 3, 4).reshape(local_experts, -1, D)

    def from_experts(rows, identity, ahead=()):
        rows = rows.reshape(local_experts, count, micros, capacity, D).transpose(1, 2, 0, 3, 4)
        back = swap_seq(rows.reshape(count, -1, D), identity, ahead)
        back = back.reshape(count, micros, -1, D)
        back = back.transpose(1, 0, 2, 3).reshape(micros, all_slots, D)
        return jnp.einsum("mst,msd->mtd", sender, back, preferred_element_type=F32).reshape(-1, D)

    taken = to_experts(s_low, 2)
    hidden, slope, result = run_experts(taken, w_up, w_down)
    combined = from_experts(result, 3)
    x2 = x1 + gate[:, None] * combined

    final, hat2, scale2 = normalize(x2, gains[2])
    own_count = slots.shape[1]
    local_rows = slots - first_pos
    select = (
        local_rows[:, :, None] == jnp.arange(tokens, dtype=jnp.int32)[None, None, :]
    ).astype(BF16)
    picked_rows = jnp.einsum(
        "mst,mtd->msd",
        select,
        final.astype(BF16).reshape(micros, tokens, D),
        preferred_element_type=F32,
    ).astype(BF16)
    rows = gather_seq([picked_rows.reshape(-1, D)], 4)[0].reshape(count * micros * own_count, D)

    def by_device(values):
        return values.reshape(micros, count, own_count).transpose(1, 0, 2).reshape(-1)

    targets = by_device(targets)
    counted = by_device(weight_mask).astype(F32)
    limits = jnp.stack(
        [vocab_start, jnp.minimum(VOCAB_REAL - vocab_start, vocab_part), vocab_part]
    ).astype(jnp.int32)
    logits, stats = head(limits, rows, table, targets[:, None])
    stats = exchange([stats.T], [True], 5)[0]
    top = jnp.max(stats[:, 0], axis=0)
    lse = top + jnp.log(jnp.sum(stats[:, 1] * jnp.exp(stats[:, 0] - top[None]), axis=0))
    unweighted = lse - jnp.sum(stats[:, 2], axis=0)

    def own(values):
        return lax.dynamic_index_in_dim(
            values.reshape(count, micros, own_count), me, 0, keepdims=False
        )

    rows_here = own(unweighted)
    counted_here = own(counted)
    loss_here = jnp.sum(rows_here * counted_here)
    count_here = jnp.sum(counted_here)
    scalars = jnp.pad(jnp.stack([lse, counted / loss_all], axis=1), ((0, 0), (0, 6)))
    table_grad, rows_grad = head_back(limits, rows, table, targets[:, None], scalars, logits)
    rows_grad = rows_grad.reshape(count, -1, D)
    rows_grad = reduce_seq([rows_grad], 6)[0].reshape(micros, own_count, D)
    final_grad = jnp.einsum(
        "mst,msd->mtd",
        select.astype(F32),
        rows_grad,
        precision=lax.Precision.HIGHEST,
        preferred_element_type=F32,
    ).reshape(-1, D)
    gain_two, x2_grad = normalize_back(hat2, scale2, gains[2], final_grad)

    gate_grad = jnp.sum(x2_grad * combined, axis=1)
    out_grad = to_experts((gate[:, None] * x2_grad).astype(BF16), 7, [table_grad])
    up_grad, down_grad, taken_grad = run_experts_back(
        taken, out_grad, w_up, w_down, hidden, slope
    )
    s_table = scatter_mat(table_grad, 0)
    s_grad = from_experts(taken_grad, 8, [table_grad])
    score_grad = jnp.where(chosen, (gate_grad * gate * (1.0 - gate))[:, None], 0.0).astype(BF16)
    route_grad = dot(s_low, score_grad, 0, 0)
    s_grad = s_grad + dot(score_grad, w_route, 1, 1)
    gain_one, more = normalize_back(hat1, scale1, gains[1], s_grad)
    x1_grad = x2_grad + more

    x1_grad_low = x1_grad.astype(BF16)
    mixed_grad = dot(x1_grad_low, w_out, 1, 1).reshape(micros, tokens, inner)
    out_weight_grad = dot(mixed_low, x1_grad_low, 0, 0)
    y_grad = mixed_grad * z_silu
    z_grad = mixed_grad * core * silu_back(z)
    out_weight_grad = out_weight_grad.astype(BF16)
    up_grad, down_grad = hold([up_grad, down_grad], [s_table, out_weight_grad])
    s_up = scatter_mat(up_grad, 2)
    s_down = scatter_mat(down_grad, 1)
    s_out = scatter_mat(out_weight_grad, 0)
    starts_all = gather_seq(
        [scan_start(keeping, dt, y_grad, readout, rate, [out_weight_grad, up_grad, down_grad])], 9
    )[0]
    dt_grad, act_grad, inject_grad, readout_grad, rate_grad = scan_backward(
        place, keeping, dt, act, y_grad, inject, readout, rate, totals_all, starts_all, start, hs,
        [],
    )
    skip_grad = jnp.sum(y_grad * act, axis=(0, 1))
    pre_dt = dt_grad * jax.nn.sigmoid(pre)
    pre_dt_low = pre_dt.reshape(-1, inner).astype(BF16)
    step_weight_grad = dot(rank_low, pre_dt_low, 0, 0)
    projected_grad = jnp.concatenate(
        [
            dot(pre_dt_low, w_step, 1, 1),
            jnp.sum(inject_grad, axis=3).reshape(-1, STATES),
            jnp.sum(readout_grad, axis=3).reshape(-1, STATES),
        ],
        axis=1,
    ).astype(BF16)
    raw_grad, head_grad, x_weight_grad, conv_rows = convolve_back(
        lengths, place, xz, edge, channel, w_x, conv, act, act_grad, y_grad,
        projected_grad.reshape(micros, tokens, -1),
    )
    chan_grad = jnp.concatenate(
        [
            conv_rows[: CONV + 1],
            jnp.sum(pre_dt, axis=(0, 1))[None],
            skip_grad[None],
            jnp.sum(rate_grad, axis=0) * rate,
        ],
        axis=0,
    )
    edge_grad = move_rows(head_grad, -1)
    raw_grad = raw_grad + jnp.pad(
        edge_grad, ((0, 0), (tokens - (CONV - 1), 0), (0, 0))
    )
    xz_grad = jnp.concatenate([raw_grad, z_grad], axis=2).reshape(-1, 2 * inner).astype(BF16)
    in_grad = dot(u_low, xz_grad, 0, 0)
    gain_zero, more = normalize_back(hat0, scale0, gains[0], dot(xz_grad, w_in, 1, 1))
    x0_grad = (x1_grad + more).astype(BF16)
    grads = (
        s_table,
        scatter_mat(in_grad, 1),
        s_out,
        s_up,
        s_down,
        x_weight_grad,
        step_weight_grad,
        route_grad,
        chan_grad,
        jnp.stack([gain_zero, gain_one, gain_two]),
    )
    return grads, x0_grad, loss_here, count_here, rows_here


def scatter_mat(grad, dim):
    return lax.psum_scatter(grad.astype(BF16), "mat", scatter_dimension=dim, tiled=True)


def ortho_kernel(
    place, scale, moments, later, experts, inward, outward, out,
    moment, grads, current, rounded, gram, low, poly, slope, trace, semaphores,
):
    blocks, size, _ = experts.shape
    tile = TILE
    tiles = size // tile
    eye = lax.broadcasted_iota(jnp.int32, (tile, tile), 0) == lax.broadcasted_iota(
        jnp.int32, (tile, tile), 1
    )
    turned = jnp.logical_or(place[0] == DOWN_PLACE, place[0] == OUT_PLACE)

    def band(index):
        return pl.ds(index * tile, tile)

    half = moments.shape[1]
    fetches = [
        pltpu.make_async_copy(moments, moment.at[:, pl.ds(0, half)], semaphores.at[0]),
        pltpu.make_async_copy(later, moment.at[:, pl.ds(half, half)], semaphores.at[1 + blocks]),
    ]
    for fetch in fetches:
        fetch.start()

    @pl.when(jnp.logical_or(place[0] == UP_PLACE, place[0] == DOWN_PLACE))
    def _():
        copy = pltpu.make_async_copy(experts, grads, semaphores.at[1])
        copy.start()
        copy.wait()

    @pl.when(place[0] == IN_PLACE)
    def _():
        copy = pltpu.make_async_copy(inward, grads, semaphores.at[1])
        copy.start()
        copy.wait()

    @pl.when(place[0] == OUT_PLACE)
    def _():
        rows = outward.shape[1]
        grads[:, rows:, :] = jnp.zeros((blocks, size - rows, size), BF16)
        copies = [
            pltpu.make_async_copy(
                outward.at[block], grads.at[block, pl.ds(0, rows)], semaphores.at[1 + block]
            )
            for block in range(blocks)
        ]
        for copy in copies:
            copy.start()
        for copy in copies:
            copy.wait()

    for fetch in fetches:
        fetch.wait()
    trace[...] = jnp.zeros_like(trace)

    def load(lap, _):
        block, index = lap // tiles, lap % tiles
        rows = pl.ds(pl.multiple_of(index * tile, tile), tile)
        values = MOMENTUM * moment[block, rows, :].astype(F32)
        values = values + scale[0] * grads[block, rows, :].astype(F32)
        values = values.astype(BF16).astype(F32)
        trace[...] += jnp.sum(values * values, axis=0, keepdims=True)

        @pl.when(turned)
        def _():
            flipped = values.T
            current[block, :, rows] = flipped
            rounded[0, block, :, rows] = flipped.astype(BF16)

        @pl.when(jnp.logical_not(turned))
        def _():
            current[block, rows, :] = values
            rounded[0, block, rows, :] = values.astype(BF16)

        return 0

    lax.fori_loop(0, blocks * tiles, load, 0)
    total = jnp.sum(trace[...])
    factor = 1.0 / (jnp.sqrt(total + jnp.zeros((8, 128), F32)) + 1e-07)[0:1, 0:1]

    def sweep(step, gain):
        now = step % 2

        diagonal = []
        for index in range(tiles):
            total = jnp.zeros((tile, size - index * tile), F32)
            for block in range(blocks):
                total = total + dot(
                    rounded[now, block, band(index), :],
                    rounded[now, block, index * tile :, :],
                    1,
                    1,
                )
            total = total * gain
            corner = total[:, :tile]
            own = jnp.where(eye, corner, 0.0)
            diagonal.append(jnp.sum(own, axis=0, keepdims=True))
            slope[band(index), :] = jnp.broadcast_to(
                jnp.sum(own, axis=1, keepdims=True), (tile, 128)
            )
            gram[band(index), index * tile :] = total
            low[band(index), band(index)] = (corner - own).astype(BF16)
            for other in range(index + 1, tiles):
                part = total[:, (other - index) * tile : (other - index + 1) * tile]
                flipped = part.T
                low[band(index), band(other)] = part.astype(BF16)
                gram[band(other), band(index)] = flipped
                low[band(other), band(index)] = flipped.astype(BF16)

        for index in range(tiles):
            product = dot(low[band(index), :], low[...], 1, 0)
            own = spread(slope[band(index), :], tile)
            for other in range(tiles):
                values = gram[band(index), band(other)]
                sums = own + diagonal[other]
                total = (COEF_B + COEF_C * sums) * values
                total = total + COEF_C * product[:, other * tile : (other + 1) * tile]
                if other == index:
                    total = jnp.where(eye, total - COEF_C * values * values, total)
                    part = jnp.sum(jnp.where(eye, total, 0.0), axis=1, keepdims=True)
                    total = jnp.where(eye, 0.0, total)
                poly[band(index), band(other)] = total.astype(BF16)
            slope[band(index), :] = jnp.broadcast_to(part + COEF_A, (tile, 128))

        def advance(lap, _):
            block, index = lap // tiles, lap % tiles
            rows = pl.ds(pl.multiple_of(index * tile, tile), tile)
            scaled = spread(slope[rows, :], size) * current[block, rows, :]
            values = scaled + dot(poly[rows, :], rounded[now, block], 1, 0)
            current[block, rows, :] = values
            rounded[1 - now, block, rows, :] = values.astype(BF16)
            return 0

        def advance_first(lap, _):
            block, index = lap // tiles, lap % tiles
            rows = pl.ds(pl.multiple_of(index * tile, tile), tile)
            scaled = spread(slope[rows, :], size) * current[block, rows, :]
            values = (scaled + dot(poly[rows, :], rounded[now, block], 1, 0)) * factor
            current[block, rows, :] = values
            rounded[1 - now, block, rows, :] = values.astype(BF16)
            return 0

        @pl.when(step == 0)
        def _():
            lax.fori_loop(0, blocks * tiles, advance_first, 0)

        @pl.when(step > 0)
        def _():
            lax.fori_loop(0, blocks * tiles, advance, 0)

        return jnp.ones_like(gain)

    lax.fori_loop(0, ORTHO_STEPS, sweep, factor * factor)

    def store(lap, _):
        block, index = lap // tiles, lap % tiles
        rows = pl.ds(pl.multiple_of(index * tile, tile), tile)

        @pl.when(turned)
        def _():
            out[block, :, rows] = current[block, rows, :].T.astype(BF16)

        @pl.when(jnp.logical_not(turned))
        def _():
            out[block, rows, :] = current[block, rows, :].astype(BF16)

        return 0

    lax.fori_loop(0, blocks * tiles, store, 0)


def orthogonalize(scale, moments, later, experts, inward, outward):
    blocks, size, width = experts.shape
    vmem = pl.BlockSpec(memory_space=pltpu.VMEM)
    smem = pl.BlockSpec(memory_space=pltpu.SMEM)
    unread = pl.BlockSpec(memory_space=pl.ANY)
    place = lax.axis_index("mat").astype(jnp.int32).reshape(1)
    return pl.pallas_call(
        ortho_kernel,
        out_shape=jax.ShapeDtypeStruct(experts.shape, BF16),
        in_specs=[smem, smem] + [unread] * 5,
        out_specs=vmem,
        scratch_shapes=[
            pltpu.VMEM((blocks, size, width), BF16),
            pltpu.VMEM((blocks, size, width), BF16),
            pltpu.VMEM((blocks, size, width), F32),
            pltpu.VMEM((2, blocks, size, width), BF16),
            pltpu.VMEM((size, size), F32),
            pltpu.VMEM((size, size), BF16),
            pltpu.VMEM((size, size), BF16),
            pltpu.VMEM((size, 128), F32),
            pltpu.VMEM((1, size), F32),
            pltpu.SemaphoreType.DMA((2 + blocks,)),
        ],
        compiler_params=pltpu.CompilerParams(vmem_limit_bytes=56 * 1024 * 1024),
        name="orthogonalize",
    )(place, scale.reshape(1), moments, later, experts, inward, outward)


def adamw_update(weight, mean, square, grad, rate, decay):
    mean = BETA_ONE * mean + (1.0 - BETA_ONE) * grad
    square = BETA_TWO * square + (1.0 - BETA_TWO) * grad * grad
    ratio = (
        mean
        / (1.0 - BETA_ONE**STEP_COUNT)
        / (jnp.sqrt(square / (1.0 - BETA_TWO**STEP_COUNT)) + ADAM_EPS)
    )
    return (weight * (1.0 - rate * decay) - rate * ratio, mean, square)


def table_kernel(scale, grad, weight, mean, square, _ahead, new_weight, new_mean, new_square):
    part = weight.shape[0]
    turned = grad[...].T[:part] * scale[0]
    results = adamw_update(weight[...], mean[...], square[...], turned, 0.05, 0.1)
    new_weight[...], new_mean[...], new_square[...] = results


def update_table(scale, grad, weight, mean, square, ahead):
    part, entries = weight.shape
    flat = pl.BlockSpec((part, VOCAB_TILE), lambda i: (0, i))
    return pl.pallas_call(
        table_kernel,
        grid=(-(-entries // VOCAB_TILE),),
        in_specs=[
            pl.BlockSpec(memory_space=pltpu.SMEM),
            pl.BlockSpec((VOCAB_TILE, 256), lambda i: (i, 0)),
            flat,
            flat,
            flat,
            pl.BlockSpec(memory_space=pl.ANY),
        ],
        out_specs=[flat] * 3,
        out_shape=[jax.ShapeDtypeStruct(weight.shape, F32)] * 3,
        compiler_params=kernel_params(),
        cost_estimate=pl.CostEstimate(
            flops=20 * entries * 256,
            bytes_accessed=7 * entries * 256 * 4,
            transcendentals=2 * entries * 256,
        ),
        name="update_table",
    )(scale.reshape(1), grad, weight, mean, square, ahead)


def local(
    token_ids,
    expert_route,
    doc_lengths,
    loss_slots,
    loss_weight,
    target_ids,
    embedding,
    embedding_mom,
    embedding_sq,
    in_project,
    in_project_mom,
    out_project,
    out_project_mom,
    expert_up,
    expert_up_mom,
    expert_down,
    expert_down_mom,
    x_project,
    x_project_mom,
    x_project_sq,
    step_project,
    step_project_mom,
    step_project_sq,
    router_weight,
    router_mom,
    router_sq,
    channel_param,
    channel_mom,
    channel_sq,
    norm_gains,
    gains_mom,
    gains_sq,
):
    micros = token_ids.shape[0]
    mats = lax.axis_size("mat")
    seq_count = lax.axis_size("seq")
    tokens = expert_route.shape[2]
    vocab_part, part = embedding.shape
    ids = exchange([token_ids.reshape(-1, 128)], [True], 12, ("mat",))[0]
    ids = ids.reshape(mats, micros, seq_count, tokens)
    ids = ids.transpose(2, 0, 1, 3).reshape(-1) - lax.axis_index("seq") * vocab_part
    parts = [x_project, step_project, router_weight, channel_param, norm_gains]
    wide = [expert_up_mom[0], in_project_mom, expert_down_mom[0], out_project_mom]
    wide += [expert_up[0], expert_down[0], out_project]
    found, small, moments, w_up, w_down, w_out = lookup(
        ids, embedding.T, pack_small(parts), wide, 10
    )
    found, w_table = lax.optimization_barrier((found, embedding.T.astype(BF16)))
    small = unpack_small(small, parts)
    weights = (
        lax.all_gather(w_table, "mat", axis=0, tiled=True),
        lax.all_gather(in_project.astype(BF16), "mat", axis=1, tiled=True),
        lax.all_gather(w_out, "mat", axis=0, tiled=True),
        lax.all_gather(w_up[None], "mat", axis=2, tiled=True),
        lax.all_gather(w_down[None], "mat", axis=1, tiled=True),
        small[0].reshape(-1, small[0].shape[2]),
        columns(small[1]),
        small[2].reshape(-1, small[2].shape[2]),
        columns(small[3]),
        columns(small[4]),
    )
    half = micros * tokens // 2
    tails = found[:, 2 * half :].reshape(mats, half, 2, part - 128).transpose(0, 2, 1, 3)
    heads = found[:, : 2 * half].reshape(mats, 2, half, 128)
    embedded = jnp.concatenate([heads, tails], axis=3).transpose(1, 2, 0, 3)
    embedded = embedded.reshape(micros * tokens, mats * part)
    loss_all = micros * lax.axis_size("mat") * loss_weight.shape[2]
    moments, later = jnp.split(moments, 2, axis=1)
    moments = lax.all_to_all(moments, "mat", split_axis=0, concat_axis=0, tiled=True)
    grads, x0_grad, loss_part, count_part, rows_here = step_grads(
        weights,
        embedded,
        expert_route[:, 0, :, 0],
        doc_lengths[:, 0],
        loss_slots[:, 0],
        loss_weight[:, 0],
        target_ids[:, 0],
        loss_all,
    )
    row_loss = rows_here[:, None, :]
    s_table, s_in, s_out, s_up, s_down, g_x, g_step, g_route, g_chan, g_gain = grads
    pieces = (
        g_x.reshape(mats, -1),
        g_step.reshape(g_step.shape[0], mats, -1).transpose(1, 0, 2).reshape(mats, -1),
        g_route.reshape(mats, -1),
        g_chan.reshape(g_chan.shape[0], mats, -1).transpose(1, 0, 2).reshape(mats, -1),
        g_gain.reshape(g_gain.shape[0], mats, -1).transpose(1, 0, 2).reshape(mats, -1),
    )
    packed = jnp.concatenate(pieces, axis=1)
    unit = seq_count * 2048
    packed = jnp.pad(packed, ((0, 0), (0, -packed.shape[1] % unit)))
    packed = packed.astype(BF16).reshape(mats, -1, 128)
    x0_parts = x0_grad.reshape(2, -1, mats, part).transpose(2, 0, 1, 3)
    x0_heads = x0_parts[..., :128].reshape(mats, -1, 128)
    x0_tails = jnp.concatenate([x0_parts[:, 0, :, 128:], x0_parts[:, 1, :, 128:]], axis=2)
    x0_heads, moments = lax.optimization_barrier((x0_heads, moments))
    x0_rows = 3 * micros * tokens // 2
    mixed = lax.all_to_all(
        jnp.concatenate([x0_heads, x0_tails, packed], axis=1),
        "mat",
        split_axis=0,
        concat_axis=0,
        tiled=True,
    )
    packed = jnp.sum(mixed[:, x0_rows:].astype(F32), axis=0).astype(BF16)
    g_table, table_squares, whole_experts = scatter_rows(
        ids.reshape(-1, 128),
        mixed[:, :x0_rows],
        s_table,
        vocab_part,
        13,
        [s_up[0], s_down[0]],
    )
    s_in, s_out, packed, later = reduce_seq(
        [
            s_in.reshape(seq_count, -1, D),
            s_out.reshape(seq_count, -1, D),
            packed.reshape(seq_count, -1, 128),
        ],
        14,
        [g_table],
        [later],
    )
    s_up = s_up.astype(F32)
    s_down = s_down.astype(F32)
    squares = sum(jnp.sum(g * g) for g in (s_in, s_out, packed))
    squares = squares + jnp.sum(table_squares[0])
    tallies = jnp.stack([squares, loss_part, count_part])
    tallies = jnp.broadcast_to(jnp.pad(tallies, (0, 5))[:, None], (8, 128))
    g_in, g_out, packed, whole_in, whole_out, totals = gather_seq(
        [s_in.astype(BF16), s_out.astype(BF16), packed.astype(BF16)],
        15,
        relays=[(0, IN_PLACE), (1, OUT_PLACE)],
        everyone=[tallies],
    )
    g_in = g_in.reshape(-1, D).astype(F32)
    g_out = g_out.reshape(-1, D).astype(F32)
    totals = jnp.sum(totals[:, :, 0], axis=0)
    squares, loss_total, loss_count = totals[0], totals[1], totals[2]
    grad_norm = jnp.sqrt(squares)
    scale = jnp.minimum(1.0, CLIP_NORM / (grad_norm + 1e-06))
    mom_in = MOMENTUM * in_project_mom + g_in * scale
    mom_out = MOMENTUM * out_project_mom + g_out * scale
    mom_up = MOMENTUM * expert_up_mom + s_up * scale
    mom_down = MOMENTUM * expert_down_mom + s_down * scale
    ortho = orthogonalize(
        scale,
        moments,
        later,
        whole_experts,
        whole_in.reshape(mats, D, -1),
        whole_out.reshape(mats, -1, D),
    )
    packed, ortho = lax.optimization_barrier((packed, ortho))
    packed = packed.reshape(-1)
    shards, offset = [], 0
    for piece, like in zip(
        pieces, (x_project, step_project, router_weight, channel_param, norm_gains)
    ):
        shards.append(packed[offset : offset + piece.shape[1]].reshape(like.shape).astype(F32))
        offset += piece.shape[1]
    table_new = update_table(
        scale, g_table, embedding.T, embedding_mom.T, embedding_sq.T, ortho
    )
    table_new = [values.T for values in table_new]
    ortho = lax.all_to_all(ortho, "mat", split_axis=0, concat_axis=0, tiled=True)
    shrink = 1.0 - LR_MUON * DECAY_MUON
    new_up = expert_up * shrink - LR_MUON * 0.2 * math.sqrt(max(D, FF)) * ortho[UP_PLACE][None].astype(F32)
    new_in = in_project * shrink - LR_MUON * 0.2 * math.sqrt(max(D, 2 * DI)) * ortho[IN_PLACE].astype(F32)
    new_down = (
        expert_down * shrink - LR_MUON * 0.2 * math.sqrt(max(D, FF)) * ortho[DOWN_PLACE][None].astype(F32)
    )
    new_out = (
        out_project * shrink
        - LR_MUON * 0.2 * math.sqrt(max(D, DI)) * ortho[OUT_PLACE, : out_project.shape[0]].astype(F32)
    )
    x_new = adamw_update(x_project, x_project_mom, x_project_sq, shards[0] * scale, 0.06, 0.1)
    step_new = adamw_update(
        step_project, step_project_mom, step_project_sq, shards[1] * scale, 0.06, 0.1
    )
    route_new = adamw_update(router_weight, router_mom, router_sq, shards[2] * scale, 0.06, 0.1)
    chan_new = adamw_update(channel_param, channel_mom, channel_sq, shards[3] * scale, 1.0, 0.0)
    gains_new = adamw_update(norm_gains, gains_mom, gains_sq, shards[4] * scale, 0.4, 0.0)
    return (
        loss_total,
        loss_count,
        grad_norm,
        row_loss,
        *table_new,
        new_in,
        mom_in,
        new_out,
        mom_out,
        new_up,
        mom_up,
        new_down,
        mom_down,
        *x_new,
        *step_new,
        *route_new,
        *chan_new,
        *gains_new,
    )


def solution(mesh):
    in_specs = (
        P(None, "mat", None),
        P(None, "mat", "seq", None),
        P(None, "mat", None),
        P(None, "mat", "seq"),
        P(None, "mat", None),
        P(None, "mat", None),
        P("seq", "mat"),
        P("seq", "mat"),
        P("seq", "mat"),
        P(None, "mat"),
        P(None, "mat"),
        P("mat", None),
        P("mat", None),
        P("seq", None, "mat"),
        P("seq", None, "mat"),
        P("seq", "mat", None),
        P("seq", "mat", None),
        P("mat", None),
        P("mat", None),
        P("mat", None),
        P(None, "mat"),
        P(None, "mat"),
        P(None, "mat"),
        P("mat", None),
        P("mat", None),
        P("mat", None),
        P(None, "mat"),
        P(None, "mat"),
        P(None, "mat"),
        P(None, "mat"),
        P(None, "mat"),
        P(None, "mat"),
    )
    out_specs = (
        P(),
        P(),
        P(),
        P(None, "mat", "seq"),
        P("seq", "mat"),
        P("seq", "mat"),
        P("seq", "mat"),
        P(None, "mat"),
        P(None, "mat"),
        P("mat", None),
        P("mat", None),
        P("seq", None, "mat"),
        P("seq", None, "mat"),
        P("seq", "mat", None),
        P("seq", "mat", None),
        P("mat", None),
        P("mat", None),
        P("mat", None),
        P(None, "mat"),
        P(None, "mat"),
        P(None, "mat"),
        P("mat", None),
        P("mat", None),
        P("mat", None),
        P(None, "mat"),
        P(None, "mat"),
        P(None, "mat"),
        P(None, "mat"),
        P(None, "mat"),
        P(None, "mat"),
    )
    return jax.shard_map(local, mesh=mesh, in_specs=in_specs, out_specs=out_specs, check_vma=False)
```
